32 devices in a mesh: groups: 2 (over y), space: 8 (over z, x), rhs: 2 (over core).
Axes of the slice: x: 2, y: 2, z: 4, core: 2. Of those that a mesh axis runs over, the one named last changes fastest.
Arguments:
- vectors: bfloat16 [65536, 256], P(('groups', 'space'), 'rhs'), parts along dimension 0, may hold values from -6 to 6
- near_blocks: bfloat16 [128, 12, 256, 256], P('space'), may hold values from -0.109375 to 0.109375
- near_list: int32 [128, 12], P('space'), may hold values from 0 to 127, as said below
- basis: bfloat16 [128, 256, 64], P('space'), may hold values from -0.375 to 0.375
- up_one: bfloat16 [128, 64, 64], P('space'), may hold values from -0.5 to 0.5
- up_two: bfloat16 [64, 64, 64], P('space'), may hold values from -0.5 to 0.5
- couple_zero: bfloat16 [128, 16, 64, 64], P('space'), may hold values from -0.1875 to 0.1875
- couple_one: bfloat16 [64, 16, 64, 64], P('space'), may hold values from -0.1875 to 0.1875
- couple_two: bfloat16 [32, 16, 64, 64], P('space'), may hold values from -0.1875 to 0.1875
- far_zero: int32 [128, 16], P('space'), may hold values from 0 to 127, as said below
- far_one: int32 [64, 16], P('space'), may hold values from 0 to 63, as said below
- far_two: int32 [32, 16], P('space'), may hold values from 0 to 31, as said below
Outputs:
- product: bfloat16 [65536, 256], P(('groups', 'space'), 'rhs'), parts along dimension 0
The draws below stay inside these ranges and needn't reach their ends.
There are 2 independent parts, one for each index of `groups`. The reference program is written for one: setup_inputs(seed, part) draws one part's arguments, and reference() takes and returns one part's arrays. A program takes and returns all parts, laid end to end along the dimension named above; an argument that names none is the same for every part. Nothing has to cross between parts.
Inputs may be any that keep to these rules, and one draw needn't show every extreme that they name: `near_list`: entry 0 of each leaf's list is the leaf itself; entries may repeat. Entry 1 is the first leaf of the next index of space and entry 2 the last leaf of the previous index (the leaf itself where that index does not exist); every other entry is a leaf of the leaf's own index of space (leaves i * 16 to (i+1) * 16 - 1). `far_zero`: each entry names a node of the leaf level held by an index of space at most 2 away from the index that holds the listing node (index i holds nodes i * 16 to (i+1) * 16 - 1). `far_one`: each entry names a node of level one held by an index of space at most 2 away from the index that holds the listing node (index i holds nodes i * 8 to (i+1) * 8 - 1). `far_two`: each entry names a node of level two held by an index of space at most 2 away from the index that holds the listing node (index i holds nodes i * 4 to (i+1) * 4 - 1).
All inputs are finite; a program needn't handle non-finite values.
Results may differ from the reference program's by a relative error of at most 0.005.
Values may be sent and summed in bfloat16 or wider, within the bound.
No kernel may reach another device: no remote copies, remote signals or barrier semaphores. Data moves between devices by JAX's collectives and lax.ppermute only.
A program may use at most 128 MiB of HBM per device.

```python
import jax
import jax.numpy as jnp
from jax import lax

LEAF = 256
RANK = 64
NEAR = 12
FAR = 16
REACH = 2
LEAF_DEV = 16
LEAVES = 128
POINTS = 32768
COLS = 256


def draw_near_list(key, part):
    key = jax.random.fold_in(key, 11)
    devices = LEAVES // LEAF_DEV
    leaf_ids = jnp.arange(LEAVES, dtype=jnp.int32)
    home = leaf_ids // LEAF_DEV
    slot_ids = jnp.arange(NEAR, dtype=jnp.int32)[None, :]
    own_leaf = home[:, None] * LEAF_DEV + jax.random.randint(key, (LEAVES, NEAR), 0, LEAF_DEV, dtype=jnp.int32)
    next_first = jnp.where(home + 1 < devices, (home + 1) * LEAF_DEV, leaf_ids)
    prev_last = jnp.where(home > 0, home * LEAF_DEV - 1, leaf_ids)
    chosen = jnp.where(slot_ids == 1, next_first[:, None], own_leaf)
    chosen = jnp.where(slot_ids == 2, prev_last[:, None], chosen)
    chosen = jnp.where(slot_ids == 0, leaf_ids[:, None], chosen)
    return chosen.astype(jnp.int32)


def nearby_list(key, nodes, per_dev):
    devices = nodes // per_dev
    key_dev, key_node, key_turn = jax.random.split(key, 3)
    node_ids = jnp.arange(nodes, dtype=jnp.int32)
    home = (node_ids // per_dev)[:, None]
    slot_ids = jnp.arange(FAR, dtype=jnp.int32)[None, :]
    offsets = jnp.concatenate([jnp.arange(-REACH, 0, dtype=jnp.int32), jnp.arange(1, REACH + 1, dtype=jnp.int32)])
    turn = jax.random.randint(key_turn, (nodes, 1), 0, 2 * REACH, dtype=jnp.int32)
    forced = offsets[(slot_ids + turn) % (2 * REACH)]
    random_step = jax.random.randint(key_dev, (nodes, FAR), -REACH, REACH + 1, dtype=jnp.int32)
    step = jnp.where(slot_ids < 2 * REACH, forced, random_step)
    target = home + step
    target = jnp.where((target < 0) | (target >= devices), home - step, target)
    chosen = target * per_dev + jax.random.randint(key_node, (nodes, FAR), 0, per_dev, dtype=jnp.int32)
    return chosen.astype(jnp.int32)


def draw_far_zero(key, part):
    key = jax.random.fold_in(key, 21)
    return nearby_list(key, LEAVES, LEAF_DEV)


def draw_far_one(key, part):
    key = jax.random.fold_in(key, 22)
    return nearby_list(key, LEAVES // 2, LEAF_DEV // 2)


def draw_far_two(key, part):
    key = jax.random.fold_in(key, 23)
    return nearby_list(key, LEAVES // 4, LEAF_DEV // 4)


def shard_levels(rng, shape, pieces, least, top_value):
    gain = 1.0
    for position, blocks in pieces:
        steps = jax.random.uniform(jax.random.fold_in(jax.random.fold_in(rng, 6), position), (blocks,), jnp.float32, least / len(pieces), top_value / len(pieces))
        gain = gain * jnp.repeat(jnp.exp(steps), shape[position] // blocks).reshape((-1,) + (1,) * (len(shape) - 1 - position))
    return gain


def centred(own_key, shape, scale, reach, cuts=(), held_as=jnp.bfloat16):
    result = jax.random.normal(own_key, shape, jnp.float32) * scale
    if len(cuts) > 0:
        result = shard_levels(own_key, shape, cuts, -0.22, 0.18) * result
    return jnp.clip(result, min=-reach, max=reach).astype(held_as)


def setup_inputs(seed: int = 0, part: int = 0) -> dict:
    key_of = jax.random.split(jax.random.key(seed), 13)
    part_keys = jax.random.split(jax.random.fold_in(key_of[12], part), 13)
    vectors = centred(part_keys[0], (POINTS, COLS), 1.0, 6.0, ((0, 8), (1, 2)))
    near_blocks = centred(key_of[1], (LEAVES, NEAR, LEAF, LEAF), (LEAF * NEAR) ** -0.5, 0.109375, ((0, 8),))
    near_list = draw_near_list(jax.random.fold_in(key_of[12], 71), part)
    basis = centred(key_of[3], (LEAVES, LEAF, RANK), LEAF ** -0.5, 0.375, ((0, 8),))
    up_one = centred(key_of[4], (LEAVES, RANK, RANK), (2 * RANK) ** -0.5, 0.5, ((0, 8),))
    up_two = centred(key_of[5], (LEAVES // 2, RANK, RANK), (2 * RANK) ** -0.5, 0.5, ((0, 8),))
    couple_zero = centred(key_of[6], (LEAVES, FAR, RANK, RANK), (FAR * RANK) ** -0.5, 0.1875, ((0, 8),))
    couple_one = centred(key_of[7], (LEAVES // 2, FAR, RANK, RANK), (FAR * RANK) ** -0.5, 0.1875, ((0, 8),))
    couple_two = centred(key_of[8], (LEAVES // 4, FAR, RANK, RANK), (FAR * RANK) ** -0.5, 0.1875, ((0, 8),))
    far_zero = draw_far_zero(jax.random.fold_in(key_of[12], 71), part)
    far_one = draw_far_one(jax.random.fold_in(key_of[12], 71), part)
    far_two = draw_far_two(jax.random.fold_in(key_of[12], 71), part)
    return {"vectors": vectors, "near_blocks": near_blocks, "near_list": near_list, "basis": basis, "up_one": up_one, "up_two": up_two, "couple_zero": couple_zero, "couple_one": couple_one, "couple_two": couple_two, "far_zero": far_zero, "far_one": far_one, "far_two": far_two}


def couple_level(matrices, partner_list, coefficients):
    def one_node(args):
        node_mats, node_list = args
        picked = coefficients[node_list].astype(jnp.float32)
        return jnp.einsum('kab,kbc->ac', node_mats.astype(jnp.float32), picked)
    return lax.map(one_node, (matrices, partner_list))


def reference(vectors, near_blocks, near_list, basis, up_one, up_two, couple_zero, couple_one, couple_two, far_zero, far_one, far_two):
    points = vectors.reshape(LEAVES, LEAF, COLS)

    def near_leaf(args):
        blocks, partners = args
        partner_rows = points[partners].astype(jnp.float32)
        return jnp.einsum('kpq,kqc->pc', blocks.astype(jnp.float32), partner_rows)

    near_term = lax.map(near_leaf, (near_blocks, near_list))
    basis_f = basis.astype(jnp.float32)
    up_one_f = up_one.astype(jnp.float32)
    up_two_f = up_two.astype(jnp.float32)
    coef_zero = jnp.einsum('lpr,lpc->lrc', basis_f, points.astype(jnp.float32)).astype(jnp.bfloat16)
    lifted = jnp.einsum('lab,lac->lbc', up_one_f, coef_zero.astype(jnp.float32))
    coef_one = lifted.reshape(LEAVES // 2, 2, RANK, COLS).sum(axis=1).astype(jnp.bfloat16)
    lifted = jnp.einsum('lab,lac->lbc', up_two_f, coef_one.astype(jnp.float32))
    coef_two = lifted.reshape(LEAVES // 4, 2, RANK, COLS).sum(axis=1).astype(jnp.bfloat16)
    field_zero = couple_level(couple_zero, far_zero, coef_zero)
    field_one = couple_level(couple_one, far_one, coef_one)
    field_two = couple_level(couple_two, far_two, coef_two)
    down_two = field_two.astype(jnp.bfloat16)
    parent_two = jnp.repeat(down_two, 2, axis=0).astype(jnp.float32)
    down_one = (field_one + jnp.einsum('pab,pbc->pac', up_two_f, parent_two)).astype(jnp.bfloat16)
    parent_one = jnp.repeat(down_one, 2, axis=0).astype(jnp.float32)
    down_zero = (field_zero + jnp.einsum('lab,lbc->lac', up_one_f, parent_one)).astype(jnp.bfloat16)
    far_term = jnp.einsum('lpr,lrc->lpc', basis_f, down_zero.astype(jnp.float32))
    return (near_term + far_term).astype(jnp.bfloat16).reshape(POINTS, COLS)
```

```python
import functools

import jax
import jax.numpy as jnp
from jax import lax
from jax.experimental import pallas as pl
from jax.experimental.pallas import tpu as pltpu
from jax.sharding import PartitionSpec as P

LEAF = 256
REACH = 2
MIB = 1024 * 1024


def dot(a, b):
    return jnp.dot(a, b, preferred_element_type=jnp.float32)


def dot_t(a, b):
    return lax.dot_general(a, b, (((0,), (0,)), ((), ())), preferred_element_type=jnp.float32)


def up_kernel(x_ref, basis_ref, up_one_ref, up_two_ref, plain_ref, ahead_ref, behind_ref):
    leaves, rank = basis_ref.shape[:2]
    total = leaves + leaves // 2 + leaves // 4

    def put(node, value):
        rows = pl.ds(node * rank, rank)
        plain_ref[rows, :] = value
        ahead_ref[rows, :] = value
        behind_ref[rows, :] = value

    first_one, first_two = leaves, leaves + leaves // 2
    ones = []
    for p in range(leaves // 2):
        pair = []
        for leaf in (2 * p, 2 * p + 1):
            coef = dot(basis_ref[leaf], x_ref[pl.ds(leaf * LEAF, LEAF), :])
            coef = coef.astype(jnp.bfloat16)
            put(leaf, coef)
            pair.append(coef)
        up = up_one_ref[2 * p : 2 * p + 2].reshape(2 * rank, rank)
        coef = dot_t(up, jnp.concatenate(pair, axis=0)).astype(jnp.bfloat16)
        put(first_one + p, coef)
        ones.append(coef)
    for q in range(leaves // 4):
        up = up_two_ref[2 * q : 2 * q + 2].reshape(2 * rank, rank)
        coef = dot_t(up, jnp.concatenate(ones[2 * q : 2 * q + 2], axis=0)).astype(jnp.bfloat16)
        put(first_two + q, coef)
    edge = pl.ds(total * rank, LEAF)
    ahead_ref[edge, :] = x_ref[pl.ds((leaves - 1) * LEAF, LEAF), :]
    behind_ref[edge, :] = x_ref[pl.ds(0, LEAF), :]


def near_kernel(list_ref, x_ref, self_ref, a_ref, b_ref, c_ref, out_ref):
    leaf = pl.program_id(0)

    def rows(slot):
        start = pl.multiple_of(list_ref[leaf, slot] * LEAF, LEAF)
        return x_ref[pl.ds(start, LEAF), :]

    total = dot(self_ref[0, 0], rows(0))
    slot = 3
    for ref in (a_ref, b_ref, c_ref):
        for k in range(ref.shape[1]):
            total += dot(ref[0, k], rows(slot))
            slot += 1
    out_ref[...] = total


def far_kernel(
    zero_list,
    one_list,
    two_list,
    own_edge,
    own_ref,
    before_two,
    before_one,
    after_one,
    after_two,
    x_ref,
    near_ref,
    next_ref,
    prev_ref,
    basis_ref,
    up_one_ref,
    up_two_ref,
    couple_zero_ref,
    couple_one_ref,
    couple_two_ref,
    out_ref,
    zero_buf,
    one_buf,
    two_buf,
    edge_buf,
    sems,
):
    step = pl.program_id(0)
    steps = pl.num_programs(0)
    leaves = zero_list.shape[0]
    rank = basis_ref.shape[1]
    fars = zero_list.shape[1]
    pieces = (before_two, before_one, own_ref, after_one, after_two)
    sizes = (leaves * rank, leaves // 2 * rank, leaves // 4 * rank)

    @pl.when(step == 0)
    def _():
        copies = []
        for i, piece in enumerate(pieces):
            start = 0
            for j, (buf, size) in enumerate(zip((zero_buf, one_buf, two_buf), sizes)):
                copies.append(
                    pltpu.make_async_copy(
                        piece.at[pl.ds(start, size), :],
                        buf.at[pl.ds(i * size, size), :],
                        sems.at[i * 3 + j],
                    )
                )
                start += size
        total = sum(sizes)
        for i, piece in enumerate((before_one, after_one)):
            copies.append(
                pltpu.make_async_copy(
                    piece.at[pl.ds(total, LEAF), :], edge_buf.at[i], sems.at[15 + i]
                )
            )
        for copy in copies:
            copy.start()
        for copy in copies:
            copy.wait()

    def field(matrices, where, node, buf):
        total = None
        for k in range(fars):
            start = pl.multiple_of(where[node, k] * rank, rank)
            term = dot(matrices[k], buf[pl.ds(start, rank), :])
            total = term if total is None else total + term
        return total

    down_two = field(couple_two_ref.at[0], two_list, step, two_buf).astype(jnp.bfloat16)
    for i in range(2):
        down_one = field(couple_one_ref.at[i], one_list, 2 * step + i, one_buf)
        down_one = (down_one + dot(up_two_ref[i], down_two)).astype(jnp.bfloat16)
        for j in range(2):
            n = 2 * i + j
            leaf = 4 * step + n
            down_zero = field(couple_zero_ref.at[n], zero_list, leaf, zero_buf)
            down_zero = (down_zero + dot(up_one_ref[n], down_one)).astype(jnp.bfloat16)
            total = near_ref[pl.ds(n * LEAF, LEAF), :] + dot_t(basis_ref[n], down_zero)
            own_rows = x_ref[pl.ds(n * LEAF, LEAF), :]
            rows = jnp.where(own_edge[0] == 1, own_rows, edge_buf[1])
            total += dot(next_ref[n, 0], rows)
            rows = jnp.where(own_edge[1] == 1, own_rows, edge_buf[0])
            total += dot(prev_ref[n, 0], rows)
            out_ref[pl.ds(n * LEAF, LEAF), :] = total.astype(jnp.bfloat16)


def whole(shape):
    return pl.BlockSpec(shape, lambda *_: (0,) * len(shape))


def body(
    vectors,
    near_blocks,
    near_list,
    basis,
    up_one,
    up_two,
    couple_zero,
    couple_one,
    couple_two,
    far_zero,
    far_one,
    far_two,
):
    leaves = near_list.shape[0]
    nears = near_list.shape[1]
    columns = vectors.shape[1]
    rank = basis.shape[2]
    fars = far_zero.shape[1]
    size = lax.axis_size("space")
    myself = lax.axis_index("space")
    nodes = leaves + leaves // 2 + leaves // 4
    basis_t = jnp.swapaxes(basis, 1, 2)

    plain, ahead, behind = pl.pallas_call(
        up_kernel,
        out_shape=[
            jax.ShapeDtypeStruct((nodes * rank, columns), jnp.bfloat16),
            jax.ShapeDtypeStruct((nodes * rank + LEAF, columns), jnp.bfloat16),
            jax.ShapeDtypeStruct((nodes * rank + LEAF, columns), jnp.bfloat16),
        ],
        compiler_params=pltpu.CompilerParams(vmem_limit_bytes=24 * MIB),
        name="up_pass",
    )(vectors, basis_t, up_one, up_two)

    def shift(array, by):
        return lax.ppermute(
            array, "space", [(i, i + by) for i in range(size) if 0 <= i + by < size]
        )

    before_one = shift(ahead, 1)
    after_one = shift(behind, -1)
    before_two = shift(plain, 2)
    after_two = shift(plain, -2)

    third = (nears - 3) // 3
    near = pl.pallas_call(
        near_kernel,
        grid_spec=pltpu.PrefetchScalarGridSpec(
            num_scalar_prefetch=1,
            grid=(leaves,),
            in_specs=[
                whole(vectors.shape),
                pl.BlockSpec((1, 1, LEAF, LEAF), lambda l, _: (l, 0, 0, 0)),
                pl.BlockSpec((1, third, LEAF, LEAF), lambda l, _: (l, 1, 0, 0)),
                pl.BlockSpec((1, third, LEAF, LEAF), lambda l, _: (l, 2, 0, 0)),
                pl.BlockSpec((1, third, LEAF, LEAF), lambda l, _: (l, 3, 0, 0)),
            ],
            out_specs=pl.BlockSpec((LEAF, columns), lambda l, _: (l, 0)),
        ),
        out_shape=jax.ShapeDtypeStruct((leaves * LEAF, columns), jnp.float32),
        compiler_params=pltpu.CompilerParams(vmem_limit_bytes=24 * MIB),
        cost_estimate=pl.CostEstimate(
            flops=2 * leaves * (nears - 2) * LEAF * LEAF * columns,
            bytes_accessed=2 * leaves * (nears - 2) * LEAF * LEAF + 6 * leaves * LEAF * columns,
            transcendentals=0,
        ),
        name="near_own",
    )(near_list - myself * leaves, vectors, *([near_blocks] * 4))

    first = myself - REACH
    own_edge = jnp.stack([myself == size - 1, myself == 0]).astype(jnp.int32)
    any_spec = pl.BlockSpec(memory_space=pl.ANY)
    return pl.pallas_call(
        far_kernel,
        grid_spec=pltpu.PrefetchScalarGridSpec(
            num_scalar_prefetch=4,
            grid=(leaves // 4,),
            in_specs=[any_spec] * 5
            + [
                pl.BlockSpec((4 * LEAF, columns), lambda q, *_: (q, 0)),
                pl.BlockSpec((4 * LEAF, columns), lambda q, *_: (q, 0)),
                pl.BlockSpec((4, 1, LEAF, LEAF), lambda q, *_: (q, 1, 0, 0)),
                pl.BlockSpec((4, 1, LEAF, LEAF), lambda q, *_: (q, 2, 0, 0)),
                pl.BlockSpec((4, rank, LEAF), lambda q, *_: (q, 0, 0)),
                pl.BlockSpec((4, rank, rank), lambda q, *_: (q, 0, 0)),
                pl.BlockSpec((2, rank, rank), lambda q, *_: (q, 0, 0)),
                pl.BlockSpec((4, fars, rank, rank), lambda q, *_: (q, 0, 0, 0)),
                pl.BlockSpec((2, fars, rank, rank), lambda q, *_: (q, 0, 0, 0)),
                pl.BlockSpec((1, fars, rank, rank), lambda q, *_: (q, 0, 0, 0)),
            ],
            out_specs=pl.BlockSpec((4 * LEAF, columns), lambda q, *_: (q, 0)),
            scratch_shapes=[
                pltpu.VMEM((5 * leaves * rank, columns), jnp.bfloat16),
                pltpu.VMEM((5 * (leaves // 2) * rank, columns), jnp.bfloat16),
                pltpu.VMEM((5 * (leaves // 4) * rank, columns), jnp.bfloat16),
                pltpu.VMEM((2, LEAF, columns), jnp.bfloat16),
                pltpu.SemaphoreType.DMA((17,)),
            ],
        ),
        out_shape=jax.ShapeDtypeStruct(vectors.shape, jnp.bfloat16),
        compiler_params=pltpu.CompilerParams(vmem_limit_bytes=32 * MIB),
        name="far_down",
    )(
        far_zero - first * leaves,
        far_one - first * (leaves // 2),
        far_two - first * (leaves // 4),
        own_edge,
        plain,
        before_two,
        before_one,
        after_one,
        after_two,
        vectors,
        near,
        near_blocks,
        near_blocks,
        basis_t,
        up_one,
        up_two,
        couple_zero,
        couple_one,
        couple_two,
    )


def solution(mesh):
    placed = (
        P(("groups", "space"), "rhs"),
        P("space", None, None, None),
        P("space", None),
        P("space", None, None),
        P("space", None, None),
        P("space", None, None),
        P("space", None, None, None),
        P("space", None, None, None),
        P("space", None, None, None),
        P("space", None),
        P("space", None),
        P("space", None),
    )
    return jax.shard_map(
        body, mesh=mesh, in_specs=placed, out_specs=P(("groups", "space"), "rhs"), check_vma=False
    )
```

```python
import jax
import jax.numpy as jnp
from jax import lax
from jax.experimental import pallas as pl
from jax.experimental.pallas import tpu as pltpu
from jax.sharding import PartitionSpec as P

LEAF = 256
REACH = 2
SPAN = 2 * REACH + 1
DEPTH = 4
MIB = 1024 * 1024


def dot(a, b):
    return jnp.dot(a, b, preferred_element_type=jnp.float32)


def dot_t(a, b):
    return lax.dot_general(a, b, (((0,), (0,)), ((), ())), preferred_element_type=jnp.float32)


def up_kernel(
    me_ref, x_hbm, basis_hbm, up_one_hbm, up_two_hbm, plain_ref, pair_ref,
    x_ref, basis_ref, up_one_ref, up_two_ref, sems,
):
    leaves, rank = basis_ref.shape[:2]
    steps = leaves // 4
    copies = []
    for q in range(steps):
        rows = pl.ds(q * 4 * LEAF, 4 * LEAF)
        some = pl.ds(q * 4, 4)
        copies.append(
            (
                pltpu.make_async_copy(x_hbm.at[rows, :], x_ref.at[rows, :], sems.at[2 * q]),
                pltpu.make_async_copy(basis_hbm.at[some], basis_ref.at[some], sems.at[2 * q + 1]),
            )
        )
    ups = (
        pltpu.make_async_copy(up_one_hbm, up_one_ref, sems.at[2 * steps]),
        pltpu.make_async_copy(up_two_hbm, up_two_ref, sems.at[2 * steps + 1]),
    )
    for pair in (copies[0], ups, *copies[1:]):
        for copy in pair:
            copy.start()

    def put(node, value):
        plain_ref[pl.ds(node * rank, rank), :] = value
        pair_ref[pl.ds(2 * LEAF + node * rank, rank), :] = value

    first_one, first_two = leaves, leaves + leaves // 2
    for q in range(steps):
        for copy in copies[q]:
            copy.wait()
        if q == 0:
            for copy in ups:
                copy.wait()
        ones = []
        for p in (2 * q, 2 * q + 1):
            pair = []
            for leaf in (2 * p, 2 * p + 1):
                coef = dot(basis_ref[leaf], x_ref[pl.ds(leaf * LEAF, LEAF), :])
                coef = coef.astype(jnp.bfloat16)
                put(leaf, coef)
                pair.append(coef)
            up = up_one_ref[2 * p : 2 * p + 2].reshape(2 * rank, rank)
            coef = dot_t(up, jnp.concatenate(pair, axis=0)).astype(jnp.bfloat16)
            put(first_one + p, coef)
            ones.append(coef)
        up = up_two_ref[2 * q : 2 * q + 2].reshape(2 * rank, rank)
        put(first_two + q, dot_t(up, jnp.concatenate(ones, axis=0)).astype(jnp.bfloat16))
    odd = lax.rem(me_ref[0], 2)
    last = (leaves - 1) * LEAF
    near_edge = pl.multiple_of((1 - odd) * last, LEAF)
    far_edge = pl.multiple_of(odd * last, LEAF)
    pair_ref[pl.ds(0, LEAF), :] = x_ref[pl.ds(near_edge, LEAF), :]
    pair_ref[pl.ds(LEAF, LEAF), :] = x_ref[pl.ds(far_edge, LEAF), :]


def near_kernel(
    me_ref, list_ref, x_hbm, blocks_hbm, zero_hbm, one_hbm, two_hbm,
    out_ref, edge_ref, zero_ref, one_ref, two_ref,
    x_ref, block_buf, zero_buf, one_buf, two_buf, sems, x_sem, edge_sem, *, size,
):
    leaves, nears = list_ref.shape
    half, quarter = one_buf.shape[1], two_buf.shape[1]
    first = me_ref[0] * leaves

    def copies(leaf, slot):
        pairs = (
            (blocks_hbm.at[leaf, pl.ds(0, 1)], block_buf.at[slot, pl.ds(0, 1)]),
            (blocks_hbm.at[leaf, pl.ds(3, nears - 3)], block_buf.at[slot, pl.ds(1, nears - 3)]),
            (zero_hbm.at[leaf], zero_buf.at[slot]),
            (one_hbm.at[leaf // 2, pl.ds(leaf % 2 * half, half)], one_buf.at[slot]),
            (two_hbm.at[leaf // 4, pl.ds(leaf % 4 * quarter, quarter)], two_buf.at[slot]),
        )
        return [
            pltpu.make_async_copy(src, dst, sems.at[slot, i]) for i, (src, dst) in enumerate(pairs)
        ]

    x_copy = pltpu.make_async_copy(x_hbm, x_ref, x_sem)
    edge_copy = pltpu.make_async_copy(blocks_hbm.at[:, pl.ds(1, 2)], edge_ref, edge_sem)
    x_copy.start()
    for leaf in range(DEPTH - 1):
        for copy in copies(leaf, leaf):
            copy.start()
    x_copy.wait()

    def step(leaf, carry):
        slot = lax.rem(leaf, DEPTH)

        @pl.when(leaf + DEPTH - 1 < leaves)
        def _():
            for copy in copies(leaf + DEPTH - 1, lax.rem(leaf + DEPTH - 1, DEPTH)):
                copy.start()

        @pl.when(leaf + DEPTH - 1 == leaves)
        def _():
            edge_copy.start()

        for copy in copies(leaf, slot):
            copy.wait()
        rows = []
        for k in (0, *range(3, nears)):
            start = pl.multiple_of((list_ref[leaf, k] - first) * LEAF, LEAF)
            rows.append(x_ref[pl.ds(start, LEAF), :])
        blocks = [block_buf[slot, k] for k in range(nears - 2)]
        total = dot(jnp.concatenate(blocks, axis=1), jnp.concatenate(rows, axis=0))
        out_ref[pl.ds(pl.multiple_of(leaf * LEAF, LEAF), LEAF), :] = total
        for buf, ref in ((zero_buf, zero_ref), (one_buf, one_ref), (two_buf, two_ref)):
            wide = [buf[slot, k] for k in range(buf.shape[1])]
            ref[leaf] = jnp.concatenate(wide, axis=1)
        return carry

    lax.fori_loop(0, leaves, step, 0)
    edge_copy.wait()

    for side, here in ((0, me_ref[0] == size - 1), (1, me_ref[0] == 0)):

        @pl.when(here)
        def _():
            def own(leaf, carry):
                rows = pl.ds(pl.multiple_of(leaf * LEAF, LEAF), LEAF)
                out_ref[rows, :] += dot(edge_ref[leaf, side], x_ref[rows, :])
                return carry

            lax.fori_loop(0, leaves, own, 0)


def far_kernel(
    me_ref, zero_list, one_list, two_list,
    own_ref, pair_ref, before_ref, after_ref, low_ref, high_ref,
    near_ref, edge_ref, basis_ref, up_one_ref, up_two_ref, zero_ref, one_ref, two_ref,
    out_ref, zero_buf, one_buf, two_buf, sems,
):
    leaves, fars = zero_list.shape
    rank = basis_ref.shape[1]
    me = me_ref[0]
    odd = lax.rem(me, 2)
    sizes = (leaves * rank, leaves // 2 * rank, leaves // 4 * rank)
    bufs = (zero_buf, one_buf, two_buf)
    pair_at = REACH + 1 - 2 * odd
    diag_at = REACH - 1 + 2 * odd
    plans = (
        (own_ref, 0, (0, 1, 2), REACH),
        (before_ref, 0, (0, 1, 2), 0),
        (after_ref, 0, (0, 1, 2), SPAN - 1),
        (pair_ref, 2 * LEAF, (0, 1, 2), pair_at),
        (low_ref, LEAF, (0,), diag_at),
        (high_ref, 0, (1, 2), diag_at),
    )
    copies = []
    for ref, start, levels, place in plans:
        for level in levels:
            at = pl.multiple_of(place * sizes[level], sizes[level])
            copies.append(
                pltpu.make_async_copy(
                    ref.at[pl.ds(start, sizes[level]), :],
                    bufs[level].at[pl.ds(at, sizes[level]), :],
                    sems.at[len(copies)],
                )
            )
            start += sizes[level]
    for copy in copies:
        copy.start()
    for copy in copies:
        copy.wait()

    def field(wide, where, node, first, buf):
        picked = []
        for k in range(fars):
            start = pl.multiple_of((where[node, k] - first) * rank, rank)
            picked.append(buf[pl.ds(start, rank), :])
        return dot(jnp.concatenate(wide, axis=1), jnp.concatenate(picked, axis=0))

    pair_rows, diag_rows = pair_ref[pl.ds(0, LEAF), :], low_ref[pl.ds(0, LEAF), :]
    edge_rows = jnp.concatenate([pair_rows, diag_rows], axis=0)

    def step(q, carry):
        wide = [two_ref[4 * q + i] for i in range(4)]
        first = (me - REACH) * (leaves // 4)
        down_two = field(wide, two_list, q, first, two_buf).astype(jnp.bfloat16)
        for i in range(2):
            p = 2 * q + i
            wide = [one_ref[2 * p + j] for j in range(2)]
            first = (me - REACH) * (leaves // 2)
            down_one = field(wide, one_list, p, first, one_buf)
            down_one = (down_one + dot(up_two_ref[p], down_two)).astype(jnp.bfloat16)
            for j in range(2):
                leaf = 2 * p + j
                first = (me - REACH) * leaves
                down_zero = field([zero_ref[leaf]], zero_list, leaf, first, zero_buf)
                down_zero = (down_zero + dot(up_one_ref[leaf], down_one)).astype(jnp.bfloat16)
                rows = pl.ds(pl.multiple_of(leaf * LEAF, LEAF), LEAF)
                total = near_ref[rows, :] + dot_t(basis_ref[leaf], down_zero)
                sides = [edge_ref[leaf, odd], edge_ref[leaf, 1 - odd]]
                total += dot(jnp.concatenate(sides, axis=1), edge_rows)
                out_ref[rows, :] = total.astype(jnp.bfloat16)
        return carry

    lax.fori_loop(0, leaves // 4, step, 0)


def body(
    vectors,
    near_blocks,
    near_list,
    basis,
    up_one,
    up_two,
    couple_zero,
    couple_one,
    couple_two,
    far_zero,
    far_one,
    far_two,
):
    leaves, nears = near_list.shape
    columns = vectors.shape[1]
    rank = basis.shape[2]
    fars = far_zero.shape[1]
    size = lax.axis_size("space")
    myself = lax.axis_index("space")
    me = myself.astype(jnp.int32).reshape(1)
    nodes = leaves + leaves // 2 + leaves // 4
    basis_t = jnp.swapaxes(basis, 1, 2)
    bf16 = jnp.bfloat16

    hbm = pl.BlockSpec(memory_space=pltpu.HBM)
    vmem = pl.BlockSpec(memory_space=pltpu.VMEM)
    smem = pl.BlockSpec(memory_space=pltpu.SMEM)

    plain, pair = pl.pallas_call(
        up_kernel,
        in_specs=[smem] + [hbm] * 4,
        out_specs=[vmem] * 2,
        out_shape=[
            jax.ShapeDtypeStruct((nodes * rank, columns), bf16),
            jax.ShapeDtypeStruct((2 * LEAF + nodes * rank, columns), bf16),
        ],
        scratch_shapes=[
            pltpu.VMEM(vectors.shape, bf16),
            pltpu.VMEM(basis_t.shape, bf16),
            pltpu.VMEM(up_one.shape, bf16),
            pltpu.VMEM(up_two.shape, bf16),
            pltpu.SemaphoreType.DMA((leaves // 2 + 2,)),
        ],
        compiler_params=pltpu.CompilerParams(vmem_limit_bytes=16 * MIB),
        name="up_pass",
    )(me, *[pltpu.with_memory_space_constraint(a, pltpu.HBM) for a in (vectors, basis_t, up_one, up_two)])

    def send(array, to):
        return lax.ppermute(
            array, "space", [(i, to(i)) for i in range(size) if 0 <= to(i) < size]
        )

    from_pair = send(pair, lambda i: i + 1 - 2 * (i % 2))
    before = send(plain, lambda i: i + 2)
    after = send(plain, lambda i: i - 2)

    near, edge, wide_zero, wide_one, wide_two = pl.pallas_call(
        lambda *refs: near_kernel(*refs, size=size),
        in_specs=[smem] * 2 + [hbm] * 5,
        out_specs=[vmem] * 5,
        out_shape=[
            jax.ShapeDtypeStruct(vectors.shape, jnp.float32),
            jax.ShapeDtypeStruct((leaves, 2, LEAF, LEAF), bf16),
            jax.ShapeDtypeStruct((leaves, rank, fars * rank), bf16),
            jax.ShapeDtypeStruct((leaves, rank, fars // 2 * rank), bf16),
            jax.ShapeDtypeStruct((leaves, rank, fars // 4 * rank), bf16),
        ],
        scratch_shapes=[
            pltpu.VMEM(vectors.shape, bf16),
            pltpu.VMEM((DEPTH, nears - 2, LEAF, LEAF), bf16),
            pltpu.VMEM((DEPTH, fars, rank, rank), bf16),
            pltpu.VMEM((DEPTH, fars // 2, rank, rank), bf16),
            pltpu.VMEM((DEPTH, fars // 4, rank, rank), bf16),
            pltpu.SemaphoreType.DMA((DEPTH, 5)),
            pltpu.SemaphoreType.DMA,
            pltpu.SemaphoreType.DMA,
        ],
        compiler_params=pltpu.CompilerParams(vmem_limit_bytes=32 * MIB),
        cost_estimate=pl.CostEstimate(
            flops=2 * leaves * (nears - 2) * LEAF * LEAF * columns,
            bytes_accessed=2 * leaves * nears * LEAF * LEAF + 6 * leaves * LEAF * columns,
            transcendentals=0,
        ),
        name="near_own",
    )(
        me,
        near_list,
        *[
            pltpu.with_memory_space_constraint(a, pltpu.HBM)
            for a in (vectors, near_blocks, couple_zero, couple_one, couple_two)
        ],
    )

    from_pair, before, after, near = lax.optimization_barrier((from_pair, before, after, near))
    split = LEAF + leaves * rank
    low = send(from_pair[LEAF : LEAF + split], lambda i: i + 2 - 4 * (i % 2))
    upper = jnp.where(me[0] % 2 == 1, before[leaves * rank :], after[leaves * rank :])
    high = send(upper, lambda i: i + 1 - 2 * (i % 2))

    return pl.pallas_call(
        far_kernel,
        in_specs=[smem] * 4 + [vmem] * 14,
        out_specs=vmem,
        out_shape=jax.ShapeDtypeStruct(vectors.shape, bf16),
        scratch_shapes=[
            pltpu.VMEM((SPAN * leaves * rank, columns), bf16),
            pltpu.VMEM((SPAN * (leaves // 2) * rank, columns), bf16),
            pltpu.VMEM((SPAN * (leaves // 4) * rank, columns), bf16),
            pltpu.SemaphoreType.DMA((15,)),
        ],
        compiler_params=pltpu.CompilerParams(vmem_limit_bytes=32 * MIB),
        name="far_down",
    )(
        me, far_zero, far_one, far_two,
        plain, from_pair, before, after, low, high,
        near, edge, basis_t, up_one, up_two, wide_zero, wide_one, wide_two,
    )


def solution(mesh):
    placed = (
        P(("groups", "space"), "rhs"),
        P("space", None, None, None),
        P("space", None),
        P("space", None, None),
        P("space", None, None),
        P("space", None, None),
        P("space", None, None, None),
        P("space", None, None, None),
        P("space", None, None, None),
        P("space", None),
        P("space", None),
        P("space", None),
    )
    return jax.shard_map(
        body, mesh=mesh, in_specs=placed, out_specs=P(("groups", "space"), "rhs"), check_vma=False
    )
```

```python
import jax
import jax.numpy as jnp
from jax import lax
from jax.experimental import pallas as pl
from jax.experimental.pallas import tpu as pltpu
from jax.sharding import PartitionSpec as P

LEAF = 256
REACH = 2
SPAN = 2 * REACH + 1
DEPTH = 4
MIB = 1024 * 1024


def dot(a, b):
    return jnp.dot(a, b, preferred_element_type=jnp.float32)


def dot_t(a, b):
    return lax.dot_general(a, b, (((0,), (0,)), ((), ())), preferred_element_type=jnp.float32)


def up_kernel(
    me_ref, x_hbm, basis_hbm, up_one_hbm, up_two_hbm, plain_ref, pair_ref,
    x_ref, basis_ref, up_one_ref, up_two_ref, sems,
):
    leaves, rank = basis_ref.shape[:2]
    steps = leaves // 4
    copies = []
    for q in range(steps):
        rows = pl.ds(q * 4 * LEAF, 4 * LEAF)
        some = pl.ds(q * 4, 4)
        copies.append(
            (
                pltpu.make_async_copy(x_hbm.at[rows, :], x_ref.at[rows, :], sems.at[2 * q]),
                pltpu.make_async_copy(basis_hbm.at[some], basis_ref.at[some], sems.at[2 * q + 1]),
            )
        )
    ups = (
        pltpu.make_async_copy(up_one_hbm, up_one_ref, sems.at[2 * steps]),
        pltpu.make_async_copy(up_two_hbm, up_two_ref, sems.at[2 * steps + 1]),
    )
    for pair in (*copies, ups):
        for copy in pair:
            copy.start()

    def put(node, value):
        value = value.astype(jnp.bfloat16)
        plain_ref[pl.ds(node * rank, rank), :] = value
        pair_ref[pl.ds(node * rank, rank), :] = value
        return value

    def join(ups, pair):
        return dot_t(ups.reshape(2 * rank, rank), jnp.concatenate(pair, axis=0))

    zeros = []
    for q in range(steps):
        for copy in copies[q]:
            copy.wait()
        for leaf in range(4 * q, 4 * q + 4):
            coef = dot(basis_ref[leaf], x_ref[pl.ds(leaf * LEAF, LEAF), :])
            zeros.append(put(leaf, coef))
    for copy in ups:
        copy.wait()
    ones = []
    for p in range(leaves // 2):
        pair = slice(2 * p, 2 * p + 2)
        ones.append(put(leaves + p, join(up_one_ref[pair], zeros[pair])))
    for q in range(leaves // 4):
        pair = slice(2 * q, 2 * q + 2)
        put(leaves + leaves // 2 + q, join(up_two_ref[pair], ones[pair]))
    odd = lax.rem(me_ref[0], 2)
    last = (leaves - 1) * LEAF
    end = pl.ds(plain_ref.shape[0] - LEAF, LEAF)
    pair_ref[end, :] = x_ref[pl.ds(pl.multiple_of((1 - odd) * last, LEAF), LEAF), :]
    plain_ref[end, :] = x_ref[pl.ds(pl.multiple_of(odd * last, LEAF), LEAF), :]


def near_kernel(
    me_ref, list_hbm, x_hbm, blocks_hbm, out_ref, edge_ref,
    list_ref, x_ref, block_buf, sems, x_sem, list_sem, *, size,
):
    leaves, nears = list_ref.shape
    me = me_ref[0]
    first = me * leaves

    def copies(leaf, slot):
        pairs = (
            (blocks_hbm.at[leaf, pl.ds(0, 1)], block_buf.at[slot, pl.ds(0, 1)]),
            (blocks_hbm.at[leaf, pl.ds(3, nears - 3)], block_buf.at[slot, pl.ds(1, nears - 3)]),
            (blocks_hbm.at[leaf, pl.ds(1, 2)], edge_ref.at[leaf]),
        )
        return [
            pltpu.make_async_copy(src, dst, sems.at[slot, i]) for i, (src, dst) in enumerate(pairs)
        ]

    x_copy = pltpu.make_async_copy(x_hbm, x_ref, x_sem)
    list_copy = pltpu.make_async_copy(list_hbm, list_ref, list_sem)
    list_copy.start()
    x_copy.start()
    for leaf in range(DEPTH - 1):
        for copy in copies(leaf, leaf):
            copy.start()
    list_copy.wait()
    x_copy.wait()

    def step(leaf, carry):
        slot = lax.rem(leaf, DEPTH)

        @pl.when(leaf + DEPTH - 1 < leaves)
        def _():
            for copy in copies(leaf + DEPTH - 1, lax.rem(leaf + DEPTH - 1, DEPTH)):
                copy.start()

        for copy in copies(leaf, slot):
            copy.wait()
        rows = []
        for k in (0, *range(3, nears)):
            start = pl.multiple_of((list_ref[leaf, k] - first) * LEAF, LEAF)
            rows.append(x_ref[pl.ds(start, LEAF), :])
        blocks = [block_buf[slot, k] for k in range(nears - 2)]
        here = pl.ds(pl.multiple_of(leaf * LEAF, LEAF), LEAF)
        out_ref[here, :] = dot(jnp.concatenate(blocks, axis=1), jnp.concatenate(rows, axis=0))

        for side, alone in ((0, me == size - 1), (1, me == 0)):

            @pl.when(alone)
            def _():
                out_ref[here, :] += dot(edge_ref[leaf, side], x_ref[here, :])

        return carry

    lax.fori_loop(0, leaves, step, 0)


def add_edge(near_ref, edge_ref, side, rows):
    leaves = edge_ref.shape[0]

    def step(leaf, carry):
        here = pl.ds(pl.multiple_of(leaf * LEAF, LEAF), LEAF)
        near_ref[here, :] += dot(edge_ref[leaf, side], rows)
        return carry

    lax.fori_loop(0, leaves, step, 0, unroll=4)


def window_copies(plans, wins, sizes, sems):
    copies = []
    for ref, levels, place in plans:
        start = 0
        for level in levels:
            at = pl.multiple_of(place * sizes[level], sizes[level])
            copies.append(
                pltpu.make_async_copy(
                    ref.at[pl.ds(start, sizes[level]), :],
                    wins[level].at[pl.ds(at, sizes[level]), :],
                    sems.at[len(copies)],
                )
            )
            start += sizes[level]
    return copies


def prep_kernel(
    me_ref, own_ref, pair_ref, before_ref, after_ref, near_in, edge_ref, zero_hbm, one_hbm, two_hbm,
    near_ref, zero_win, one_win, two_win, zero_wide, one_wide, two_wide,
    zero_buf, one_buf, two_buf, sems, win_sems,
):
    del near_in
    rank = zero_buf.shape[-1]
    levels = (
        (two_hbm, two_buf, two_wide),
        (one_hbm, one_buf, one_wide),
        (zero_hbm, zero_buf, zero_wide),
    )
    chunks = []
    for hbm, buf, wide in levels:
        for first in range(0, buf.shape[0], 4):
            some = pl.ds(first, 4)
            copy = pltpu.make_async_copy(hbm.at[some], buf.at[some], sems.at[len(chunks)])
            copy.start()
            chunks.append((copy, buf, wide, first))
    odd = lax.rem(me_ref[0], 2)
    plans = (
        (own_ref, (0, 1, 2), REACH),
        (before_ref, (0, 1, 2), 0),
        (after_ref, (0, 1, 2), SPAN - 1),
        (pair_ref, (0, 1, 2), REACH + 1 - 2 * odd),
    )
    wins = (zero_win, one_win, two_win)
    sizes = [win.shape[0] // SPAN for win in wins]
    moves = window_copies(plans, wins, sizes, win_sems)
    for move in moves:
        move.start()
    add_edge(near_ref, edge_ref, odd, pair_ref[pl.ds(pair_ref.shape[0] - LEAF, LEAF), :])
    for copy, buf, wide, first in chunks:
        copy.wait()
        for node in range(first, first + 4):
            fars = buf.shape[1]
            wide[node] = jnp.concatenate([buf[node, k] for k in range(fars)], axis=1)
    for move in moves:
        move.wait()


def far_kernel(
    me_ref, zero_list, one_list, two_list, low_ref, high_ref, near_in, edge_ref,
    basis_ref, up_one_ref, up_two_ref, zero_wide, one_wide, two_wide, zero_in, one_in, two_in,
    out_hbm, near_ref, zero_win, one_win, two_win, out_buf, win_sems, out_sems,
):
    del near_in, zero_in, one_in, two_in
    leaves, fars = zero_list.shape
    rank = basis_ref.shape[1]
    me = me_ref[0]
    odd = lax.rem(me, 2)
    wins = (zero_win, one_win, two_win)
    sizes = [win.shape[0] // SPAN for win in wins]
    place = REACH - 1 + 2 * odd
    moves = window_copies(((low_ref, (0,), place), (high_ref, (1, 2), place)), wins, sizes, win_sems)
    for move in moves:
        move.start()
    add_edge(near_ref, edge_ref, 1 - odd, high_ref[pl.ds(high_ref.shape[0] - LEAF, LEAF), :])
    for move in moves:
        move.wait()

    def field(wide, where, node, win):
        first = (me - REACH) * wide.shape[0]
        picked = []
        for k in range(fars):
            start = pl.multiple_of((where[node, k] - first) * rank, rank)
            picked.append(win[pl.ds(start, rank), :])
        return dot(wide[node], jnp.concatenate(picked, axis=0))

    down_two = [
        field(two_wide, two_list, q, two_win).astype(jnp.bfloat16) for q in range(leaves // 4)
    ]
    down_one = []
    for p in range(leaves // 2):
        total = field(one_wide, one_list, p, one_win) + dot(up_two_ref[p], down_two[p // 2])
        down_one.append(total.astype(jnp.bfloat16))
    outs = []
    for leaf in range(leaves):
        total = field(zero_wide, zero_list, leaf, zero_win)
        total = total + dot(up_one_ref[leaf], down_one[leaf // 2])
        here = pl.ds(leaf * LEAF, LEAF)
        total = near_ref[here, :] + dot_t(basis_ref[leaf], total.astype(jnp.bfloat16))
        out_buf[here, :] = total.astype(jnp.bfloat16)
        if leaf % 4 == 3:
            some = pl.ds((leaf - 3) * LEAF, 4 * LEAF)
            outs.append(
                pltpu.make_async_copy(
                    out_buf.at[some, :], out_hbm.at[some, :], out_sems.at[leaf // 4]
                )
            )
            outs[-1].start()
    for copy in outs:
        copy.wait()


def body(
    vectors,
    near_blocks,
    near_list,
    basis,
    up_one,
    up_two,
    couple_zero,
    couple_one,
    couple_two,
    far_zero,
    far_one,
    far_two,
):
    leaves, nears = near_list.shape
    columns = vectors.shape[1]
    rank = basis.shape[2]
    fars = far_zero.shape[1]
    size = lax.axis_size("space")
    me = lax.axis_index("space").astype(jnp.int32).reshape(1)
    counts = (leaves, leaves // 2, leaves // 4)
    rows = sum(counts) * rank + LEAF
    basis_t = jnp.swapaxes(basis, 1, 2)
    bf16 = jnp.bfloat16

    hbm = pl.BlockSpec(memory_space=pltpu.HBM)
    vmem = pl.BlockSpec(memory_space=pltpu.VMEM)
    smem = pl.BlockSpec(memory_space=pltpu.SMEM)

    def in_hbm(*arrays):
        return [pltpu.with_memory_space_constraint(a, pltpu.HBM) for a in arrays]

    plain, pair = pl.pallas_call(
        up_kernel,
        in_specs=[smem] + [hbm] * 4,
        out_specs=[vmem] * 2,
        out_shape=[jax.ShapeDtypeStruct((rows, columns), bf16)] * 2,
        scratch_shapes=[
            pltpu.VMEM(vectors.shape, bf16),
            pltpu.VMEM(basis_t.shape, bf16),
            pltpu.VMEM(up_one.shape, bf16),
            pltpu.VMEM(up_two.shape, bf16),
            pltpu.SemaphoreType.DMA((leaves // 2 + 2,)),
        ],
        compiler_params=pltpu.CompilerParams(vmem_limit_bytes=16 * MIB),
        name="up_pass",
    )(me, *in_hbm(vectors, basis_t, up_one, up_two))

    def send(array, to):
        return lax.ppermute(
            array, "space", [(i, to(i)) for i in range(size) if 0 <= to(i) < size]
        )

    from_pair = send(pair, lambda i: i + 1 - 2 * (i % 2))
    before = send(plain, lambda i: i + 2)
    after = send(plain, lambda i: i - 2)

    near, edge = pl.pallas_call(
        lambda *refs: near_kernel(*refs, size=size),
        in_specs=[smem] + [hbm] * 3,
        out_specs=[vmem] * 2,
        out_shape=[
            jax.ShapeDtypeStruct(vectors.shape, jnp.float32),
            jax.ShapeDtypeStruct((leaves, 2, LEAF, LEAF), bf16),
        ],
        scratch_shapes=[
            pltpu.SMEM(near_list.shape, jnp.int32),
            pltpu.VMEM(vectors.shape, bf16),
            pltpu.VMEM((DEPTH, nears - 2, LEAF, LEAF), bf16),
            pltpu.SemaphoreType.DMA((DEPTH, 3)),
            pltpu.SemaphoreType.DMA,
            pltpu.SemaphoreType.DMA,
        ],
        compiler_params=pltpu.CompilerParams(vmem_limit_bytes=24 * MIB),
        cost_estimate=pl.CostEstimate(
            flops=2 * leaves * (nears - 2) * LEAF * LEAF * columns,
            bytes_accessed=2 * leaves * nears * LEAF * LEAF + 6 * leaves * LEAF * columns,
            transcendentals=0,
        ),
        name="near_own",
    )(me, *in_hbm(near_list, vectors, near_blocks))

    from_pair, before, after, near = lax.optimization_barrier((from_pair, before, after, near))
    split = leaves * rank
    low = send(from_pair[:split], lambda i: i + 2 - 4 * (i % 2))
    upper = jnp.where(me[0] % 2 == 1, before[split:], after[split:])
    high = send(upper, lambda i: i + 1 - 2 * (i % 2))

    wins = [jax.ShapeDtypeStruct((SPAN * n * rank, columns), bf16) for n in counts]
    near, *rest = pl.pallas_call(
        prep_kernel,
        in_specs=[smem] + [vmem] * 6 + [hbm] * 3,
        out_specs=[vmem] * 7,
        out_shape=[
            jax.ShapeDtypeStruct(vectors.shape, jnp.float32),
            *wins,
            *[jax.ShapeDtypeStruct((n, rank, fars * rank), bf16) for n in counts],
        ],
        input_output_aliases={5: 0},
        scratch_shapes=[
            *[pltpu.VMEM((n, fars, rank, rank), bf16) for n in counts],
            pltpu.SemaphoreType.DMA((sum(n // 4 for n in counts),)),
            pltpu.SemaphoreType.DMA((12,)),
        ],
        compiler_params=pltpu.CompilerParams(vmem_limit_bytes=24 * MIB),
        cost_estimate=pl.CostEstimate(
            flops=2 * leaves * LEAF * LEAF * columns,
            bytes_accessed=4 * sum(counts) * fars * rank * rank,
            transcendentals=0,
        ),
        name="prep",
    )(me, plain, from_pair, before, after, near, edge, *in_hbm(couple_zero, couple_one, couple_two))
    windows, wides = rest[:3], rest[3:]

    out, *_ = pl.pallas_call(
        far_kernel,
        in_specs=[smem] * 4 + [vmem] * 13,
        out_specs=[hbm] + [vmem] * 4,
        out_shape=[
            jax.ShapeDtypeStruct(vectors.shape, bf16),
            jax.ShapeDtypeStruct(vectors.shape, jnp.float32),
            *wins,
        ],
        input_output_aliases={6: 1, 14: 2, 15: 3, 16: 4},
        scratch_shapes=[
            pltpu.VMEM(vectors.shape, bf16),
            pltpu.SemaphoreType.DMA((3,)),
            pltpu.SemaphoreType.DMA((leaves // 4,)),
        ],
        compiler_params=pltpu.CompilerParams(vmem_limit_bytes=24 * MIB),
        name="far_down",
    )(
        me, far_zero, far_one, far_two, low, high, near, edge,
        basis_t, up_one, up_two, *wides, *windows,
    )
    return out


def solution(mesh):
    placed = (
        P(("groups", "space"), "rhs"),
        P("space", None, None, None),
        P("space", None),
        P("space", None, None),
        P("space", None, None),
        P("space", None, None),
        P("space", None, None, None),
        P("space", None, None, None),
        P("space", None, None, None),
        P("space", None),
        P("space", None),
        P("space", None),
    )
    return jax.shard_map(
        body, mesh=mesh, in_specs=placed, out_specs=P(("groups", "space"), "rhs"), check_vma=False
    )
```

```python
import functools

import jax
import jax.numpy as jnp
from jax import lax
from jax.experimental import pallas as pl
from jax.experimental.pallas import tpu as pltpu
from jax.sharding import PartitionSpec as P

LEAF = 256
REACH = 2
SPAN = 2 * REACH + 1
DEPTH = 4
MIB = 1024 * 1024


def dot(a, b):
    return jnp.dot(a, b, preferred_element_type=jnp.float32)


def dot_t(a, b):
    return lax.dot_general(a, b, (((0,), (0,)), ((), ())), preferred_element_type=jnp.float32)


def up_kernel(
    me_ref, x_hbm, basis_hbm, up_one_hbm, up_two_hbm, plain_ref, pair_ref,
    x_ref, basis_ref, up_one_ref, up_two_ref, sems,
):
    leaves, rank = basis_ref.shape[:2]
    steps = leaves // 4
    copies = []
    for q in range(steps):
        rows = pl.ds(q * 4 * LEAF, 4 * LEAF)
        some = pl.ds(q * 4, 4)
        copies.append(
            (
                pltpu.make_async_copy(x_hbm.at[rows, :], x_ref.at[rows, :], sems.at[2 * q]),
                pltpu.make_async_copy(basis_hbm.at[some], basis_ref.at[some], sems.at[2 * q + 1]),
            )
        )
    ups = (
        pltpu.make_async_copy(up_one_hbm, up_one_ref, sems.at[2 * steps]),
        pltpu.make_async_copy(up_two_hbm, up_two_ref, sems.at[2 * steps + 1]),
    )
    for pair in (*copies, ups):
        for copy in pair:
            copy.start()

    def put(node, value):
        value = value.astype(jnp.bfloat16)
        plain_ref[pl.ds(node * rank, rank), :] = value
        pair_ref[pl.ds(node * rank, rank), :] = value
        return value

    def join(ups, pair):
        return dot_t(ups.reshape(2 * rank, rank), jnp.concatenate(pair, axis=0))

    zeros = []
    for q in range(steps):
        for copy in copies[q]:
            copy.wait()
        for leaf in range(4 * q, 4 * q + 4):
            coef = dot(basis_ref[leaf], x_ref[pl.ds(leaf * LEAF, LEAF), :])
            zeros.append(put(leaf, coef))
    for copy in ups:
        copy.wait()
    ones = []
    for p in range(leaves // 2):
        pair = slice(2 * p, 2 * p + 2)
        ones.append(put(leaves + p, join(up_one_ref[pair], zeros[pair])))
    for q in range(leaves // 4):
        pair = slice(2 * q, 2 * q + 2)
        put(leaves + leaves // 2 + q, join(up_two_ref[pair], ones[pair]))
    odd = lax.rem(me_ref[0], 2)
    last = (leaves - 1) * LEAF
    end = pl.ds(plain_ref.shape[0] - LEAF, LEAF)
    pair_ref[end, :] = x_ref[pl.ds(pl.multiple_of((1 - odd) * last, LEAF), LEAF), :]
    plain_ref[end, :] = x_ref[pl.ds(pl.multiple_of(odd * last, LEAF), LEAF), :]


def near_kernel(
    me_ref, list_hbm, x_hbm, blocks_hbm, out_ref, edge_ref,
    list_ref, x_ref, block_buf, sems, x_sem, list_sem,
):
    leaves, nears = list_ref.shape
    first = me_ref[0] * leaves

    def copies(leaf, slot):
        pairs = (
            (blocks_hbm.at[leaf, pl.ds(0, 1)], block_buf.at[slot, pl.ds(0, 1)]),
            (blocks_hbm.at[leaf, pl.ds(3, nears - 3)], block_buf.at[slot, pl.ds(1, nears - 3)]),
            (blocks_hbm.at[leaf, pl.ds(1, 2)], edge_ref.at[leaf]),
        )
        return [
            pltpu.make_async_copy(src, dst, sems.at[slot, i]) for i, (src, dst) in enumerate(pairs)
        ]

    x_copy = pltpu.make_async_copy(x_hbm, x_ref, x_sem)
    list_copy = pltpu.make_async_copy(list_hbm, list_ref, list_sem)
    list_copy.start()
    x_copy.start()
    for leaf in range(DEPTH - 1):
        for copy in copies(leaf, leaf):
            copy.start()
    list_copy.wait()
    x_copy.wait()

    def step(leaf, carry):
        slot = lax.rem(leaf, DEPTH)

        @pl.when(leaf + DEPTH - 1 < leaves)
        def _():
            for copy in copies(leaf + DEPTH - 1, lax.rem(leaf + DEPTH - 1, DEPTH)):
                copy.start()

        for copy in copies(leaf, slot):
            copy.wait()
        rows = []
        for k in (0, *range(3, nears)):
            start = pl.multiple_of((list_ref[leaf, k] - first) * LEAF, LEAF)
            rows.append(x_ref[pl.ds(start, LEAF), :])
        blocks = [block_buf[slot, k] for k in range(nears - 2)]
        here = pl.ds(pl.multiple_of(leaf * LEAF, LEAF), LEAF)
        out_ref[here, :] = dot(jnp.concatenate(blocks, axis=1), jnp.concatenate(rows, axis=0))
        return carry

    lax.fori_loop(0, leaves, step, 0)


def add_edge(near_ref, edge_ref, side, rows):
    leaves = edge_ref.shape[0]

    def step(leaf, carry):
        here = pl.ds(pl.multiple_of(leaf * LEAF, LEAF), LEAF)
        near_ref[here, :] += dot(edge_ref[leaf, side], rows)
        return carry

    lax.fori_loop(0, leaves, step, 0, unroll=4)


def window_copies(plans, wins, sizes, sems):
    copies = []
    for ref, levels, place in plans:
        start = 0
        for level in levels:
            at = pl.multiple_of(place * sizes[level], sizes[level])
            copies.append(
                pltpu.make_async_copy(
                    ref.at[pl.ds(start, sizes[level]), :],
                    wins[level].at[pl.ds(at, sizes[level]), :],
                    sems.at[len(copies)],
                )
            )
            start += sizes[level]
    return copies


def prep_kernel(
    me_ref, own_ref, pair_ref, first_ref, second_ref, near_in, edge_ref,
    x_hbm, zero_hbm, one_hbm, two_hbm,
    near_ref, zero_win, one_win, two_win, zero_wide, one_wide, two_wide,
    x_ref, zero_buf, one_buf, two_buf, sems, win_sems, x_sem, *, size,
):
    del near_in
    rank = zero_buf.shape[-1]
    levels = (
        (two_hbm, two_buf, two_wide),
        (one_hbm, one_buf, one_wide),
        (zero_hbm, zero_buf, zero_wide),
    )
    chunks = []
    for hbm, buf, wide in levels:
        for first in range(0, buf.shape[0], 4):
            some = pl.ds(first, 4)
            copy = pltpu.make_async_copy(hbm.at[some], buf.at[some], sems.at[len(chunks)])
            copy.start()
            chunks.append((copy, buf, wide, first))
    me = me_ref[0]
    odd = lax.rem(me, 2)
    block = lax.rem(me // 2, 2)
    plans = (
        (own_ref, (0, 1, 2), REACH),
        (first_ref, (0, 1, 2), (1 - block) * (SPAN - 1)),
        (second_ref, (0, 1, 2), block * (SPAN - 1)),
        (pair_ref, (0, 1, 2), REACH + 1 - 2 * odd),
    )
    wins = (zero_win, one_win, two_win)
    sizes = [win.shape[0] // SPAN for win in wins]
    moves = window_copies(plans, wins, sizes, win_sems)
    for move in moves:
        move.start()
    add_edge(near_ref, edge_ref, odd, pair_ref[pl.ds(pair_ref.shape[0] - LEAF, LEAF), :])

    @pl.when((me == 0) | (me == size - 1))
    def _():
        x_copy = pltpu.make_async_copy(x_hbm, x_ref, x_sem)
        x_copy.start()
        x_copy.wait()
        for leaf in range(edge_ref.shape[0]):
            here = pl.ds(leaf * LEAF, LEAF)
            near_ref[here, :] += dot(edge_ref[leaf, 1 - odd], x_ref[here, :])

    for copy, buf, wide, first in chunks:
        copy.wait()
        for node in range(first, first + 4):
            fars = buf.shape[1]
            wide[node] = jnp.concatenate([buf[node, k] for k in range(fars)], axis=1)
    for move in moves:
        move.wait()


def far_kernel(
    me_ref, zero_list, one_list, two_list, low_ref, high_ref, near_in, edge_ref,
    basis_ref, up_one_ref, up_two_ref, zero_wide, one_wide, two_wide, zero_in, one_in, two_in,
    out_hbm, near_ref, zero_win, one_win, two_win, out_buf, win_sems, out_sems,
):
    del near_in, zero_in, one_in, two_in
    leaves, fars = zero_list.shape
    rank = basis_ref.shape[1]
    me = me_ref[0]
    odd = lax.rem(me, 2)
    wins = (zero_win, one_win, two_win)
    sizes = [win.shape[0] // SPAN for win in wins]
    place = REACH - 1 + 2 * odd
    moves = window_copies(((low_ref, (0,), place), (high_ref, (1, 2), place)), wins, sizes, win_sems)
    for move in moves:
        move.start()
    add_edge(near_ref, edge_ref, 1 - odd, high_ref[pl.ds(high_ref.shape[0] - LEAF, LEAF), :])
    for move in moves:
        move.wait()

    def field(wide, where, node, win):
        first = (me - REACH) * wide.shape[0]
        picked = []
        for k in range(fars):
            start = pl.multiple_of((where[node, k] - first) * rank, rank)
            picked.append(win[pl.ds(start, rank), :])
        return dot(wide[node], jnp.concatenate(picked, axis=0))

    down_two = [
        field(two_wide, two_list, q, two_win).astype(jnp.bfloat16) for q in range(leaves // 4)
    ]
    down_one = []
    for p in range(leaves // 2):
        total = field(one_wide, one_list, p, one_win) + dot(up_two_ref[p], down_two[p // 2])
        down_one.append(total.astype(jnp.bfloat16))
    outs = []
    for leaf in range(leaves):
        total = field(zero_wide, zero_list, leaf, zero_win)
        total = total + dot(up_one_ref[leaf], down_one[leaf // 2])
        here = pl.ds(leaf * LEAF, LEAF)
        total = near_ref[here, :] + dot_t(basis_ref[leaf], total.astype(jnp.bfloat16))
        out_buf[here, :] = total.astype(jnp.bfloat16)
        if leaf % 4 == 3:
            some = pl.ds((leaf - 3) * LEAF, 4 * LEAF)
            outs.append(
                pltpu.make_async_copy(
                    out_buf.at[some, :], out_hbm.at[some, :], out_sems.at[leaf // 4]
                )
            )
            outs[-1].start()
    for copy in outs:
        copy.wait()


def body(
    vectors,
    near_blocks,
    near_list,
    basis,
    up_one,
    up_two,
    couple_zero,
    couple_one,
    couple_two,
    far_zero,
    far_one,
    far_two,
):
    leaves, nears = near_list.shape
    columns = vectors.shape[1]
    rank = basis.shape[2]
    fars = far_zero.shape[1]
    size = lax.axis_size("space")
    me = lax.axis_index("space").astype(jnp.int32).reshape(1)
    counts = (leaves, leaves // 2, leaves // 4)
    rows = sum(counts) * rank + LEAF
    basis_t = jnp.swapaxes(basis, 1, 2)
    bf16 = jnp.bfloat16

    hbm = pl.BlockSpec(memory_space=pltpu.HBM)
    vmem = pl.BlockSpec(memory_space=pltpu.VMEM)
    smem = pl.BlockSpec(memory_space=pltpu.SMEM)

    def in_hbm(*arrays):
        return [pltpu.with_memory_space_constraint(a, pltpu.HBM) for a in arrays]

    plain, pair = pl.pallas_call(
        up_kernel,
        in_specs=[smem] + [hbm] * 4,
        out_specs=[vmem] * 2,
        out_shape=[jax.ShapeDtypeStruct((rows, columns), bf16)] * 2,
        scratch_shapes=[
            pltpu.VMEM(vectors.shape, bf16),
            pltpu.VMEM(basis_t.shape, bf16),
            pltpu.VMEM(up_one.shape, bf16),
            pltpu.VMEM(up_two.shape, bf16),
            pltpu.SemaphoreType.DMA((leaves // 2 + 2,)),
        ],
        compiler_params=pltpu.CompilerParams(vmem_limit_bytes=16 * MIB),
        name="up_pass",
    )(me, *in_hbm(vectors, basis_t, up_one, up_two))

    def send(array, to):
        return lax.ppermute(
            array, "space", [(i, to(i)) for i in range(size) if 0 <= to(i) < size]
        )

    from_pair = send(pair, lambda i: i + 1 - 2 * (i % 2))
    first = send(plain, lambda i: i + 2 - i // 2 % 2 * 4)
    second = send(plain, lambda i: i - 2 + i // 2 % 2 * 4)

    near, edge = pl.pallas_call(
        near_kernel,
        in_specs=[smem] + [hbm] * 3,
        out_specs=[vmem] * 2,
        out_shape=[
            jax.ShapeDtypeStruct(vectors.shape, jnp.float32),
            jax.ShapeDtypeStruct((leaves, 2, LEAF, LEAF), bf16),
        ],
        scratch_shapes=[
            pltpu.SMEM(near_list.shape, jnp.int32),
            pltpu.VMEM(vectors.shape, bf16),
            pltpu.VMEM((DEPTH, nears - 2, LEAF, LEAF), bf16),
            pltpu.SemaphoreType.DMA((DEPTH, 3)),
            pltpu.SemaphoreType.DMA,
            pltpu.SemaphoreType.DMA,
        ],
        compiler_params=pltpu.CompilerParams(vmem_limit_bytes=24 * MIB),
        cost_estimate=pl.CostEstimate(
            flops=2 * leaves * (nears - 2) * LEAF * LEAF * columns,
            bytes_accessed=2 * leaves * nears * LEAF * LEAF + 6 * leaves * LEAF * columns,
            transcendentals=0,
        ),
        name="near_own",
    )(me, *in_hbm(near_list, vectors, near_blocks))

    from_pair, first, second, near = lax.optimization_barrier((from_pair, first, second, near))
    split = leaves * rank
    low = send(from_pair[:split], lambda i: i + 2 - 4 * (i % 2))
    upper = jnp.where((me[0] // 2 + me[0]) % 2 == 0, first[split:], second[split:])
    high = send(upper, lambda i: i + 1 - 2 * (i % 2))

    wins = [jax.ShapeDtypeStruct((SPAN * n * rank, columns), bf16) for n in counts]
    near, *rest = pl.pallas_call(
        functools.partial(prep_kernel, size=size),
        in_specs=[smem] + [vmem] * 6 + [hbm] * 4,
        out_specs=[vmem] * 7,
        out_shape=[
            jax.ShapeDtypeStruct(vectors.shape, jnp.float32),
            *wins,
            *[jax.ShapeDtypeStruct((n, rank, fars * rank), bf16) for n in counts],
        ],
        input_output_aliases={5: 0},
        scratch_shapes=[
            pltpu.VMEM(vectors.shape, bf16),
            *[pltpu.VMEM((n, fars, rank, rank), bf16) for n in counts],
            pltpu.SemaphoreType.DMA((sum(n // 4 for n in counts),)),
            pltpu.SemaphoreType.DMA((12,)),
            pltpu.SemaphoreType.DMA,
        ],
        compiler_params=pltpu.CompilerParams(vmem_limit_bytes=24 * MIB),
        cost_estimate=pl.CostEstimate(
            flops=2 * leaves * LEAF * LEAF * columns,
            bytes_accessed=4 * sum(counts) * fars * rank * rank,
            transcendentals=0,
        ),
        name="prep",
    )(
        me, plain, from_pair, first, second, near, edge,
        *in_hbm(vectors, couple_zero, couple_one, couple_two),
    )
    windows, wides = rest[:3], rest[3:]

    out, *_ = pl.pallas_call(
        far_kernel,
        in_specs=[smem] * 4 + [vmem] * 13,
        out_specs=[hbm] + [vmem] * 4,
        out_shape=[
            jax.ShapeDtypeStruct(vectors.shape, bf16),
            jax.ShapeDtypeStruct(vectors.shape, jnp.float32),
            *wins,
        ],
        input_output_aliases={6: 1, 14: 2, 15: 3, 16: 4},
        scratch_shapes=[
            pltpu.VMEM(vectors.shape, bf16),
            pltpu.SemaphoreType.DMA((3,)),
            pltpu.SemaphoreType.DMA((leaves // 4,)),
        ],
        compiler_params=pltpu.CompilerParams(vmem_limit_bytes=24 * MIB),
        name="far_down",
    )(
        me, far_zero, far_one, far_two, low, high, near, edge,
        basis_t, up_one, up_two, *wides, *windows,
    )
    return out


def solution(mesh):
    placed = (
        P(("groups", "space"), "rhs"),
        P("space", None, None, None),
        P("space", None),
        P("space", None, None),
        P("space", None, None),
        P("space", None, None),
        P("space", None, None, None),
        P("space", None, None, None),
        P("space", None, None, None),
        P("space", None),
        P("space", None),
        P("space", None),
    )
    return jax.shard_map(
        body, mesh=mesh, in_specs=placed, out_specs=P(("groups", "space"), "rhs"), check_vma=False
    )
```

```python
import functools

import jax
import jax.numpy as jnp
from jax import lax
from jax.experimental import pallas as pl
from jax.experimental.pallas import tpu as pltpu
from jax.sharding import PartitionSpec as P

LEAF = 256
REACH = 2
SPAN = 2 * REACH + 1
DEPTH = 4
MIB = 1024 * 1024


def dot(a, b):
    return jnp.dot(a, b, preferred_element_type=jnp.float32)


def dot_t(a, b):
    return lax.dot_general(a, b, (((0,), (0,)), ((), ())), preferred_element_type=jnp.float32)


def up_kernel(
    me_ref, x_hbm, basis_hbm, up_one_hbm, up_two_hbm, plain_ref, pair_ref, x_ref,
    basis_ref, up_one_ref, up_two_ref, sems,
):
    leaves, rank = basis_ref.shape[:2]
    steps = leaves // 4
    copies = []
    for q in range(steps):
        rows = pl.ds(q * 4 * LEAF, 4 * LEAF)
        some = pl.ds(q * 4, 4)
        copies.append(
            (
                pltpu.make_async_copy(x_hbm.at[rows, :], x_ref.at[rows, :], sems.at[2 * q]),
                pltpu.make_async_copy(basis_hbm.at[some], basis_ref.at[some], sems.at[2 * q + 1]),
            )
        )
    ups = (
        pltpu.make_async_copy(up_one_hbm, up_one_ref, sems.at[2 * steps]),
        pltpu.make_async_copy(up_two_hbm, up_two_ref, sems.at[2 * steps + 1]),
    )
    for pair in (*copies, ups):
        for copy in pair:
            copy.start()

    def put(node, value):
        value = value.astype(jnp.bfloat16)
        plain_ref[pl.ds(node * rank, rank), :] = value
        pair_ref[pl.ds(node * rank, rank), :] = value
        return value

    def join(ups, pair):
        return dot_t(ups.reshape(2 * rank, rank), jnp.concatenate(pair, axis=0))

    zeros = []
    for q in range(steps):
        for copy in copies[q]:
            copy.wait()
        for leaf in range(4 * q, 4 * q + 4):
            coef = dot(basis_ref[leaf], x_ref[pl.ds(leaf * LEAF, LEAF), :])
            zeros.append(put(leaf, coef))
    for copy in ups:
        copy.wait()
    ones = []
    for p in range(leaves // 2):
        pair = slice(2 * p, 2 * p + 2)
        ones.append(put(leaves + p, join(up_one_ref[pair], zeros[pair])))
    for q in range(leaves // 4):
        pair = slice(2 * q, 2 * q + 2)
        put(leaves + leaves // 2 + q, join(up_two_ref[pair], ones[pair]))
    odd = lax.rem(me_ref[0], 2)
    last = (leaves - 1) * LEAF
    end = pl.ds(plain_ref.shape[0] - LEAF, LEAF)
    pair_ref[end, :] = x_ref[pl.ds(pl.multiple_of((1 - odd) * last, LEAF), LEAF), :]
    plain_ref[end, :] = x_ref[pl.ds(pl.multiple_of(odd * last, LEAF), LEAF), :]


def near_kernel(
    me_ref, x_ref, list_hbm, blocks_hbm, out_ref, edge_ref, list_ref, block_buf, sems, list_sem,
):
    leaves, nears = list_ref.shape
    first = me_ref[0] * leaves

    def copies(leaf, slot):
        pairs = (
            (blocks_hbm.at[leaf, pl.ds(0, 1)], block_buf.at[slot, pl.ds(0, 1)]),
            (blocks_hbm.at[leaf, pl.ds(3, nears - 3)], block_buf.at[slot, pl.ds(1, nears - 3)]),
            (blocks_hbm.at[leaf, pl.ds(1, 2)], edge_ref.at[leaf]),
        )
        return [
            pltpu.make_async_copy(src, dst, sems.at[slot, i]) for i, (src, dst) in enumerate(pairs)
        ]

    list_copy = pltpu.make_async_copy(list_hbm, list_ref, list_sem)
    list_copy.start()
    for leaf in range(DEPTH - 1):
        for copy in copies(leaf, leaf):
            copy.start()
    list_copy.wait()

    def step(leaf, carry):
        slot = lax.rem(leaf, DEPTH)

        @pl.when(leaf + DEPTH - 1 < leaves)
        def _():
            for copy in copies(leaf + DEPTH - 1, lax.rem(leaf + DEPTH - 1, DEPTH)):
                copy.start()

        for copy in copies(leaf, slot):
            copy.wait()
        rows = []
        for k in (0, *range(3, nears)):
            start = pl.multiple_of((list_ref[leaf, k] - first) * LEAF, LEAF)
            rows.append(x_ref[pl.ds(start, LEAF), :])
        blocks = [block_buf[slot, k] for k in range(nears - 2)]
        here = pl.ds(pl.multiple_of(leaf * LEAF, LEAF), LEAF)
        out_ref[here, :] = dot(jnp.concatenate(blocks, axis=1), jnp.concatenate(rows, axis=0))
        return carry

    lax.fori_loop(0, leaves, step, 0)


def add_edge(near_ref, edge_ref, side, ref, start, stride):
    leaves = edge_ref.shape[0]

    def step(leaf, carry):
        here = pl.ds(pl.multiple_of(leaf * LEAF, LEAF), LEAF)
        rows = ref[pl.ds(pl.multiple_of(start + leaf * stride, LEAF), LEAF), :]
        near_ref[here, :] += dot(edge_ref[leaf, side], rows)
        return carry

    lax.fori_loop(0, leaves, step, 0, unroll=4)


def window_copies(plans, wins, sizes, sems):
    copies = []
    for ref, levels, place in plans:
        start = 0
        for level in levels:
            at = pl.multiple_of(place * sizes[level], sizes[level])
            copies.append(
                pltpu.make_async_copy(
                    ref.at[pl.ds(start, sizes[level]), :],
                    wins[level].at[pl.ds(at, sizes[level]), :],
                    sems.at[len(copies)],
                )
            )
            start += sizes[level]
    return copies


def prep_kernel(
    me_ref, own_ref, pair_ref, first_ref, second_ref, near_in, edge_ref,
    zero_hbm, one_hbm, two_hbm,
    near_ref, zero_win, one_win, two_win, zero_wide, one_wide, two_wide,
    zero_buf, one_buf, two_buf, sems, win_sems,
):
    del near_in
    rank = zero_buf.shape[-1]
    levels = (
        (two_hbm, two_buf, two_wide),
        (one_hbm, one_buf, one_wide),
        (zero_hbm, zero_buf, zero_wide),
    )
    chunks = []
    for hbm, buf, wide in levels:
        for first in range(0, buf.shape[0], 4):
            some = pl.ds(first, 4)
            copy = pltpu.make_async_copy(hbm.at[some], buf.at[some], sems.at[len(chunks)])
            copy.start()
            chunks.append((copy, buf, wide, first))
    me = me_ref[0]
    odd = lax.rem(me, 2)
    block = lax.rem(me // 2, 2)
    plans = (
        (own_ref, (0, 1, 2), REACH),
        (first_ref, (0, 1, 2), (1 - block) * (SPAN - 1)),
        (second_ref, (0, 1, 2), block * (SPAN - 1)),
        (pair_ref, (0, 1, 2), REACH + 1 - 2 * odd),
    )
    wins = (zero_win, one_win, two_win)
    sizes = [win.shape[0] // SPAN for win in wins]
    moves = window_copies(plans, wins, sizes, win_sems)
    for move in moves:
        move.start()
    add_edge(near_ref, edge_ref, odd, pair_ref, pair_ref.shape[0] - LEAF, 0)
    for copy, buf, wide, first in chunks:
        copy.wait()
        for node in range(first, first + 4):
            fars = buf.shape[1]
            wide[node] = jnp.concatenate([buf[node, k] for k in range(fars)], axis=1)
    for move in moves:
        move.wait()


def far_kernel(
    me_ref, zero_list, one_list, two_list, x_ref, low_ref, high_ref, near_in, edge_ref,
    basis_ref, up_one_ref, up_two_ref, zero_wide, one_wide, two_wide, zero_in, one_in, two_in,
    out_hbm, near_ref, zero_win, one_win, two_win, out_buf, win_sems, out_sems, *, size,
):
    del near_in, zero_in, one_in, two_in
    leaves, fars = zero_list.shape
    rank = basis_ref.shape[1]
    me = me_ref[0]
    odd = lax.rem(me, 2)
    wins = (zero_win, one_win, two_win)
    sizes = [win.shape[0] // SPAN for win in wins]
    place = REACH - 1 + 2 * odd
    moves = window_copies(((low_ref, (0,), place), (high_ref, (1, 2), place)), wins, sizes, win_sems)
    for move in moves:
        move.start()

    alone = (me == 0) | (me == size - 1)

    @pl.when(alone)
    def _():
        add_edge(near_ref, edge_ref, 1 - odd, x_ref, 0, LEAF)

    @pl.when(jnp.logical_not(alone))
    def _():
        add_edge(near_ref, edge_ref, 1 - odd, high_ref, high_ref.shape[0] - LEAF, 0)

    for move in moves:
        move.wait()

    def field(wide, where, node, win):
        first = (me - REACH) * wide.shape[0]
        picked = []
        for k in range(fars):
            start = pl.multiple_of((where[node, k] - first) * rank, rank)
            picked.append(win[pl.ds(start, rank), :])
        return dot(wide[node], jnp.concatenate(picked, axis=0))

    down_two = [
        field(two_wide, two_list, q, two_win).astype(jnp.bfloat16) for q in range(leaves // 4)
    ]
    down_one = []
    for p in range(leaves // 2):
        total = field(one_wide, one_list, p, one_win) + dot(up_two_ref[p], down_two[p // 2])
        down_one.append(total.astype(jnp.bfloat16))
    outs = []
    for leaf in range(leaves):
        total = field(zero_wide, zero_list, leaf, zero_win)
        total = total + dot(up_one_ref[leaf], down_one[leaf // 2])
        here = pl.ds(leaf * LEAF, LEAF)
        total = near_ref[here, :] + dot_t(basis_ref[leaf], total.astype(jnp.bfloat16))
        out_buf[here, :] = total.astype(jnp.bfloat16)
        if leaf % 4 == 3:
            some = pl.ds((leaf - 3) * LEAF, 4 * LEAF)
            outs.append(
                pltpu.make_async_copy(
                    out_buf.at[some, :], out_hbm.at[some, :], out_sems.at[leaf // 4]
                )
            )
            outs[-1].start()
    for copy in outs:
        copy.wait()


def body(
    vectors,
    near_blocks,
    near_list,
    basis,
    up_one,
    up_two,
    couple_zero,
    couple_one,
    couple_two,
    far_zero,
    far_one,
    far_two,
):
    leaves, nears = near_list.shape
    columns = vectors.shape[1]
    rank = basis.shape[2]
    fars = far_zero.shape[1]
    size = lax.axis_size("space")
    me = lax.axis_index("space").astype(jnp.int32).reshape(1)
    counts = (leaves, leaves // 2, leaves // 4)
    rows = sum(counts) * rank + LEAF
    basis_t = jnp.swapaxes(basis, 1, 2)
    bf16 = jnp.bfloat16

    hbm = pl.BlockSpec(memory_space=pltpu.HBM)
    vmem = pl.BlockSpec(memory_space=pltpu.VMEM)
    smem = pl.BlockSpec(memory_space=pltpu.SMEM)

    def in_hbm(*arrays):
        return [pltpu.with_memory_space_constraint(a, pltpu.HBM) for a in arrays]

    plain, pair, points = pl.pallas_call(
        up_kernel,
        in_specs=[smem] + [hbm] * 4,
        out_specs=[vmem] * 3,
        out_shape=[
            jax.ShapeDtypeStruct((rows, columns), bf16),
            jax.ShapeDtypeStruct((rows, columns), bf16),
            jax.ShapeDtypeStruct(vectors.shape, bf16),
        ],
        scratch_shapes=[
            pltpu.VMEM(basis_t.shape, bf16),
            pltpu.VMEM(up_one.shape, bf16),
            pltpu.VMEM(up_two.shape, bf16),
            pltpu.SemaphoreType.DMA((leaves // 2 + 2,)),
        ],
        compiler_params=pltpu.CompilerParams(vmem_limit_bytes=16 * MIB),
        name="up_pass",
    )(me, *in_hbm(vectors, basis_t, up_one, up_two))

    def send(array, to):
        return lax.ppermute(
            array, "space", [(i, to(i) if 0 <= to(i) < size else i) for i in range(size)]
        )

    from_pair = send(pair, lambda i: i + 1 - 2 * (i % 2))
    first = send(plain, lambda i: i + 2 - i // 2 % 2 * 4)
    second = send(plain, lambda i: i - 2 + i // 2 % 2 * 4)

    near, edge = pl.pallas_call(
        near_kernel,
        in_specs=[smem, vmem] + [hbm] * 2,
        out_specs=[vmem] * 2,
        out_shape=[
            jax.ShapeDtypeStruct(vectors.shape, jnp.float32),
            jax.ShapeDtypeStruct((leaves, 2, LEAF, LEAF), bf16),
        ],
        scratch_shapes=[
            pltpu.SMEM(near_list.shape, jnp.int32),
            pltpu.VMEM((DEPTH, nears - 2, LEAF, LEAF), bf16),
            pltpu.SemaphoreType.DMA((DEPTH, 3)),
            pltpu.SemaphoreType.DMA,
        ],
        compiler_params=pltpu.CompilerParams(vmem_limit_bytes=24 * MIB),
        cost_estimate=pl.CostEstimate(
            flops=2 * leaves * (nears - 2) * LEAF * LEAF * columns,
            bytes_accessed=2 * leaves * nears * LEAF * LEAF + 6 * leaves * LEAF * columns,
            transcendentals=0,
        ),
        name="near_own",
    )(me, points, *in_hbm(near_list, near_blocks))

    from_pair, first, second, near = lax.optimization_barrier((from_pair, first, second, near))
    split = leaves * rank
    low = send(from_pair[:split], lambda i: (i + 2 - 4 * (i % 2)) % size)
    upper = jnp.where((me[0] // 2 + me[0]) % 2 == 0, first[split:], second[split:])
    high = send(upper, lambda i: i + 1 - 2 * (i % 2))

    wins = [jax.ShapeDtypeStruct((SPAN * n * rank, columns), bf16) for n in counts]
    near, *rest = pl.pallas_call(
        prep_kernel,
        in_specs=[smem] + [vmem] * 6 + [hbm] * 3,
        out_specs=[vmem] * 7,
        out_shape=[
            jax.ShapeDtypeStruct(vectors.shape, jnp.float32),
            *wins,
            *[jax.ShapeDtypeStruct((n, rank, fars * rank), bf16) for n in counts],
        ],
        input_output_aliases={5: 0},
        scratch_shapes=[
            *[pltpu.VMEM((n, fars, rank, rank), bf16) for n in counts],
            pltpu.SemaphoreType.DMA((sum(n // 4 for n in counts),)),
            pltpu.SemaphoreType.DMA((12,)),
        ],
        compiler_params=pltpu.CompilerParams(vmem_limit_bytes=24 * MIB),
        cost_estimate=pl.CostEstimate(
            flops=2 * leaves * LEAF * LEAF * columns,
            bytes_accessed=4 * sum(counts) * fars * rank * rank,
            transcendentals=0,
        ),
        name="prep",
    )(
        me, plain, from_pair, first, second, near, edge,
        *in_hbm(couple_zero, couple_one, couple_two),
    )
    windows, wides = rest[:3], rest[3:]

    out, *_ = pl.pallas_call(
        functools.partial(far_kernel, size=size),
        in_specs=[smem] * 4 + [vmem] * 14,
        out_specs=[hbm] + [vmem] * 4,
        out_shape=[
            jax.ShapeDtypeStruct(vectors.shape, bf16),
            jax.ShapeDtypeStruct(vectors.shape, jnp.float32),
            *wins,
        ],
        input_output_aliases={7: 1, 15: 2, 16: 3, 17: 4},
        scratch_shapes=[
            pltpu.VMEM(vectors.shape, bf16),
            pltpu.SemaphoreType.DMA((3,)),
            pltpu.SemaphoreType.DMA((leaves // 4,)),
        ],
        compiler_params=pltpu.CompilerParams(vmem_limit_bytes=24 * MIB),
        name="far_down",
    )(
        me, far_zero, far_one, far_two, points, low, high, near, edge,
        basis_t, up_one, up_two, *wides, *windows,
    )
    return out


def solution(mesh):
    placed = (
        P(("groups", "space"), "rhs"),
        P("space", None, None, None),
        P("space", None),
        P("space", None, None),
        P("space", None, None),
        P("space", None, None),
        P("space", None, None, None),
        P("space", None, None, None),
        P("space", None, None, None),
        P("space", None),
        P("space", None),
        P("space", None),
    )
    return jax.shard_map(
        body, mesh=mesh, in_specs=placed, out_specs=P(("groups", "space"), "rhs"), check_vma=False
    )
```

```python
import functools

import jax
import jax.numpy as jnp
from jax import lax
from jax.experimental import pallas as pl
from jax.experimental.pallas import tpu as pltpu
from jax.sharding import PartitionSpec as P

LEAF = 256
REACH = 2
SPAN = 2 * REACH + 1
DEPTH = 4
MIB = 1024 * 1024


def dot(a, b):
    return jnp.dot(a, b, preferred_element_type=jnp.float32)


def dot_t(a, b):
    return lax.dot_general(a, b, (((0,), (0,)), ((), ())), preferred_element_type=jnp.float32)


def up_kernel(
    me_ref, x_hbm, basis_hbm, up_one_hbm, up_two_hbm, plain_ref, pair_ref, x_ref,
    basis_ref, up_one_ref, up_two_ref, sems,
):
    leaves, rank = basis_ref.shape[:2]
    steps = leaves // 4
    copies = []
    for q in range(steps):
        rows = pl.ds(q * 4 * LEAF, 4 * LEAF)
        some = pl.ds(q * 4, 4)
        copies.append(
            (
                pltpu.make_async_copy(x_hbm.at[rows, :], x_ref.at[rows, :], sems.at[2 * q]),
                pltpu.make_async_copy(basis_hbm.at[some], basis_ref.at[some], sems.at[2 * q + 1]),
            )
        )
    ups = (
        pltpu.make_async_copy(up_one_hbm, up_one_ref, sems.at[2 * steps]),
        pltpu.make_async_copy(up_two_hbm, up_two_ref, sems.at[2 * steps + 1]),
    )
    for pair in (*copies, ups):
        for copy in pair:
            copy.start()

    def put(node, value):
        value = value.astype(jnp.bfloat16)
        plain_ref[pl.ds(node * rank, rank), :] = value
        pair_ref[pl.ds(node * rank, rank), :] = value
        return value

    def join(ups, pair):
        return dot_t(ups.reshape(2 * rank, rank), jnp.concatenate(pair, axis=0))

    zeros = []
    for q in range(steps):
        for copy in copies[q]:
            copy.wait()
        for leaf in range(4 * q, 4 * q + 4):
            coef = dot(basis_ref[leaf], x_ref[pl.ds(leaf * LEAF, LEAF), :])
            zeros.append(put(leaf, coef))
    for copy in ups:
        copy.wait()
    ones = []
    for p in range(leaves // 2):
        pair = slice(2 * p, 2 * p + 2)
        ones.append(put(leaves + p, join(up_one_ref[pair], zeros[pair])))
    for q in range(leaves // 4):
        pair = slice(2 * q, 2 * q + 2)
        put(leaves + leaves // 2 + q, join(up_two_ref[pair], ones[pair]))
    odd = lax.rem(me_ref[0], 2)
    last = (leaves - 1) * LEAF
    end = pl.ds(plain_ref.shape[0] - LEAF, LEAF)
    pair_ref[end, :] = x_ref[pl.ds(pl.multiple_of((1 - odd) * last, LEAF), LEAF), :]
    plain_ref[end, :] = x_ref[pl.ds(pl.multiple_of(odd * last, LEAF), LEAF), :]


def near_kernel(
    me_ref, x_ref, list_hbm, blocks_hbm, out_ref, edge_ref, list_ref, block_buf, sems, list_sem,
):
    leaves, nears = list_ref.shape
    first = me_ref[0] * leaves

    def copies(leaf, slot):
        pairs = (
            (blocks_hbm.at[leaf, pl.ds(0, 1)], block_buf.at[slot, pl.ds(0, 1)]),
            (blocks_hbm.at[leaf, pl.ds(3, nears - 3)], block_buf.at[slot, pl.ds(1, nears - 3)]),
            (blocks_hbm.at[leaf, pl.ds(1, 2)], edge_ref.at[leaf]),
        )
        return [
            pltpu.make_async_copy(src, dst, sems.at[slot, i]) for i, (src, dst) in enumerate(pairs)
        ]

    list_copy = pltpu.make_async_copy(list_hbm, list_ref, list_sem)
    list_copy.start()
    for leaf in range(DEPTH - 1):
        for copy in copies(leaf, leaf):
            copy.start()
    list_copy.wait()

    def step(leaf, carry):
        slot = lax.rem(leaf, DEPTH)

        @pl.when(leaf + DEPTH - 1 < leaves)
        def _():
            for copy in copies(leaf + DEPTH - 1, lax.rem(leaf + DEPTH - 1, DEPTH)):
                copy.start()

        for copy in copies(leaf, slot):
            copy.wait()
        rows = []
        for k in (0, *range(3, nears)):
            start = pl.multiple_of((list_ref[leaf, k] - first) * LEAF, LEAF)
            rows.append(x_ref[pl.ds(start, LEAF), :])
        blocks = [block_buf[slot, k] for k in range(nears - 2)]
        here = pl.ds(pl.multiple_of(leaf * LEAF, LEAF), LEAF)
        out_ref[here, :] = dot(jnp.concatenate(blocks, axis=1), jnp.concatenate(rows, axis=0))
        return carry

    lax.fori_loop(0, leaves, step, 0)


def add_edge(near_ref, edge_ref, side, ref, start, stride):
    leaves = edge_ref.shape[0]

    def step(leaf, carry):
        here = pl.ds(pl.multiple_of(leaf * LEAF, LEAF), LEAF)
        rows = ref[pl.ds(pl.multiple_of(start + leaf * stride, LEAF), LEAF), :]
        near_ref[here, :] += dot(edge_ref[leaf, side], rows)
        return carry

    lax.fori_loop(0, leaves, step, 0, unroll=4)


def window_copies(plans, wins, sizes, sems):
    copies = []
    for ref, levels, place in plans:
        start = 0
        for level in levels:
            at = pl.multiple_of(place * sizes[level], sizes[level])
            copies.append(
                pltpu.make_async_copy(
                    ref.at[pl.ds(start, sizes[level]), :],
                    wins[level].at[pl.ds(at, sizes[level]), :],
                    sems.at[len(copies)],
                )
            )
            start += sizes[level]
    return copies


def prep_kernel(
    me_ref, own_ref, pair_ref, first_ref, second_ref, near_in, edge_ref,
    basis_hbm, zero_hbm, one_hbm, two_hbm,
    near_ref, zero_win, one_win, two_win, zero_wide, one_wide, two_wide, basis_ref,
    basis_buf, zero_buf, one_buf, two_buf, sems, win_sems, basis_sem,
):
    del near_in
    rank = zero_buf.shape[-1]
    levels = (
        (two_hbm, two_buf, two_wide),
        (one_hbm, one_buf, one_wide),
        (zero_hbm, zero_buf, zero_wide),
    )
    basis_copy = pltpu.make_async_copy(basis_hbm, basis_buf, basis_sem)
    basis_copy.start()
    chunks = []
    for hbm, buf, wide in levels:
        for first in range(0, buf.shape[0], 4):
            some = pl.ds(first, 4)
            copy = pltpu.make_async_copy(hbm.at[some], buf.at[some], sems.at[len(chunks)])
            copy.start()
            chunks.append((copy, buf, wide, first))
    me = me_ref[0]
    odd = lax.rem(me, 2)
    block = lax.rem(me // 2, 2)
    plans = (
        (own_ref, (0, 1, 2), REACH),
        (first_ref, (0, 1, 2), (1 - block) * (SPAN - 1)),
        (second_ref, (0, 1, 2), block * (SPAN - 1)),
        (pair_ref, (0, 1, 2), REACH + 1 - 2 * odd),
    )
    wins = (zero_win, one_win, two_win)
    sizes = [win.shape[0] // SPAN for win in wins]
    moves = window_copies(plans, wins, sizes, win_sems)
    for move in moves:
        move.start()
    add_edge(near_ref, edge_ref, odd, pair_ref, pair_ref.shape[0] - LEAF, 0)
    basis_copy.wait()
    for leaf in range(basis_ref.shape[0]):
        basis_ref[leaf] = basis_buf[leaf].T
    for copy, buf, wide, first in chunks:
        copy.wait()
        for node in range(first, first + 4):
            fars = buf.shape[1]
            wide[node] = jnp.concatenate([buf[node, k] for k in range(fars)], axis=1)
    for move in moves:
        move.wait()


def far_kernel(
    me_ref, zero_list, one_list, two_list, x_ref, low_ref, high_ref, near_in, edge_ref,
    basis_ref, up_one_ref, up_two_ref, zero_wide, one_wide, two_wide, zero_in, one_in, two_in,
    out_hbm, near_ref, zero_win, one_win, two_win, out_buf, win_sems, out_sems, *, size,
):
    del near_in, zero_in, one_in, two_in
    leaves, fars = zero_list.shape
    rank = basis_ref.shape[2]
    me = me_ref[0]
    odd = lax.rem(me, 2)
    wins = (zero_win, one_win, two_win)
    sizes = [win.shape[0] // SPAN for win in wins]
    place = REACH - 1 + 2 * odd
    moves = window_copies(((low_ref, (0,), place), (high_ref, (1, 2), place)), wins, sizes, win_sems)
    for move in moves:
        move.start()

    alone = (me == 0) | (me == size - 1)

    @pl.when(alone)
    def _():
        add_edge(near_ref, edge_ref, 1 - odd, x_ref, 0, LEAF)

    @pl.when(jnp.logical_not(alone))
    def _():
        add_edge(near_ref, edge_ref, 1 - odd, high_ref, high_ref.shape[0] - LEAF, 0)

    for move in moves:
        move.wait()

    def field(wide, where, node, win):
        first = (me - REACH) * wide.shape[0]
        picked = []
        for k in range(fars):
            start = pl.multiple_of((where[node, k] - first) * rank, rank)
            picked.append(win[pl.ds(start, rank), :])
        return dot(wide[node], jnp.concatenate(picked, axis=0))

    down_two = [
        field(two_wide, two_list, q, two_win).astype(jnp.bfloat16) for q in range(leaves // 4)
    ]
    down_one = []
    for p in range(leaves // 2):
        total = field(one_wide, one_list, p, one_win) + dot(up_two_ref[p], down_two[p // 2])
        down_one.append(total.astype(jnp.bfloat16))
    outs = []
    for leaf in range(leaves):
        total = field(zero_wide, zero_list, leaf, zero_win)
        total = total + dot(up_one_ref[leaf], down_one[leaf // 2])
        here = pl.ds(leaf * LEAF, LEAF)
        total = near_ref[here, :] + dot(basis_ref[leaf], total.astype(jnp.bfloat16))
        out_buf[here, :] = total.astype(jnp.bfloat16)
        if leaf % 4 == 3:
            some = pl.ds((leaf - 3) * LEAF, 4 * LEAF)
            outs.append(
                pltpu.make_async_copy(
                    out_buf.at[some, :], out_hbm.at[some, :], out_sems.at[leaf // 4]
                )
            )
            outs[-1].start()
    for copy in outs:
        copy.wait()


def body(
    vectors,
    near_blocks,
    near_list,
    basis,
    up_one,
    up_two,
    couple_zero,
    couple_one,
    couple_two,
    far_zero,
    far_one,
    far_two,
):
    leaves, nears = near_list.shape
    columns = vectors.shape[1]
    rank = basis.shape[2]
    fars = far_zero.shape[1]
    size = lax.axis_size("space")
    me = lax.axis_index("space").astype(jnp.int32).reshape(1)
    counts = (leaves, leaves // 2, leaves // 4)
    rows = sum(counts) * rank + LEAF
    basis_t = jnp.swapaxes(basis, 1, 2)
    bf16 = jnp.bfloat16

    hbm = pl.BlockSpec(memory_space=pltpu.HBM)
    vmem = pl.BlockSpec(memory_space=pltpu.VMEM)
    smem = pl.BlockSpec(memory_space=pltpu.SMEM)

    def in_hbm(*arrays):
        return [pltpu.with_memory_space_constraint(a, pltpu.HBM) for a in arrays]

    plain, pair, points = pl.pallas_call(
        up_kernel,
        in_specs=[smem] + [hbm] * 4,
        out_specs=[vmem] * 3,
        out_shape=[
            pltpu.VMEM((rows, columns), bf16),
            pltpu.VMEM((rows, columns), bf16),
            pltpu.VMEM(vectors.shape, bf16),
        ],
        scratch_shapes=[
            pltpu.VMEM(basis_t.shape, bf16),
            pltpu.VMEM(up_one.shape, bf16),
            pltpu.VMEM(up_two.shape, bf16),
            pltpu.SemaphoreType.DMA((leaves // 2 + 2,)),
        ],
        compiler_params=pltpu.CompilerParams(vmem_limit_bytes=16 * MIB),
        name="up_pass",
    )(me, *in_hbm(vectors, basis_t, up_one, up_two))

    cores = lax.axis_size("rhs")

    def send(array, to):
        pairs = []
        for i in range(size):
            for c in range(cores):
                j, d = (to(i), c) if 0 <= to(i) < size else (i, cores - 1 - c)
                pairs.append((i * cores + c, j * cores + d))
        return lax.ppermute(array, ("space", "rhs"), pairs)

    from_pair = send(pair, lambda i: i + 1 - 2 * (i % 2))
    first = send(plain, lambda i: i + 2 - i // 2 % 2 * 4)
    second = send(plain, lambda i: i - 2 + i // 2 % 2 * 4)

    near, edge = pl.pallas_call(
        near_kernel,
        in_specs=[smem, vmem] + [hbm] * 2,
        out_specs=[vmem] * 2,
        out_shape=[
            jax.ShapeDtypeStruct(vectors.shape, jnp.float32),
            jax.ShapeDtypeStruct((leaves, 2, LEAF, LEAF), bf16),
        ],
        scratch_shapes=[
            pltpu.SMEM(near_list.shape, jnp.int32),
            pltpu.VMEM((DEPTH, nears - 2, LEAF, LEAF), bf16),
            pltpu.SemaphoreType.DMA((DEPTH, 3)),
            pltpu.SemaphoreType.DMA,
        ],
        compiler_params=pltpu.CompilerParams(vmem_limit_bytes=24 * MIB),
        cost_estimate=pl.CostEstimate(
            flops=2 * leaves * (nears - 2) * LEAF * LEAF * columns,
            bytes_accessed=2 * leaves * nears * LEAF * LEAF + 6 * leaves * LEAF * columns,
            transcendentals=0,
        ),
        name="near_own",
    )(me, points, *in_hbm(near_list, near_blocks))

    from_pair, first, second, near = lax.optimization_barrier((from_pair, first, second, near))
    split = leaves * rank
    low = send(from_pair[:split], lambda i: (i + 2 - 4 * (i % 2)) % size)
    upper = jnp.where((me[0] // 2 + me[0]) % 2 == 0, first[split:], second[split:])
    high = send(upper, lambda i: i + 1 - 2 * (i % 2))

    wins = [jax.ShapeDtypeStruct((SPAN * n * rank, columns), bf16) for n in counts]
    near, *rest = pl.pallas_call(
        prep_kernel,
        in_specs=[smem] + [vmem] * 6 + [hbm] * 4,
        out_specs=[vmem] * 8,
        out_shape=[
            jax.ShapeDtypeStruct(vectors.shape, jnp.float32),
            *wins,
            *[jax.ShapeDtypeStruct((n, rank, fars * rank), bf16) for n in counts],
            jax.ShapeDtypeStruct(basis.shape, bf16),
        ],
        input_output_aliases={5: 0},
        scratch_shapes=[
            pltpu.VMEM(basis_t.shape, bf16),
            *[pltpu.VMEM((n, fars, rank, rank), bf16) for n in counts],
            pltpu.SemaphoreType.DMA((sum(n // 4 for n in counts),)),
            pltpu.SemaphoreType.DMA((12,)),
            pltpu.SemaphoreType.DMA,
        ],
        compiler_params=pltpu.CompilerParams(vmem_limit_bytes=24 * MIB),
        cost_estimate=pl.CostEstimate(
            flops=2 * leaves * LEAF * LEAF * columns,
            bytes_accessed=4 * sum(counts) * fars * rank * rank,
            transcendentals=0,
        ),
        name="prep",
    )(
        me, plain, from_pair, first, second, near, edge,
        *in_hbm(basis_t, couple_zero, couple_one, couple_two),
    )
    windows, wides, basis_n = rest[:3], rest[3:6], rest[6]

    out, *_ = pl.pallas_call(
        functools.partial(far_kernel, size=size),
        in_specs=[smem] * 4 + [vmem] * 14,
        out_specs=[hbm] + [vmem] * 4,
        out_shape=[
            jax.ShapeDtypeStruct(vectors.shape, bf16),
            jax.ShapeDtypeStruct(vectors.shape, jnp.float32),
            *wins,
        ],
        input_output_aliases={7: 1, 15: 2, 16: 3, 17: 4},
        scratch_shapes=[
            pltpu.VMEM(vectors.shape, bf16),
            pltpu.SemaphoreType.DMA((3,)),
            pltpu.SemaphoreType.DMA((leaves // 4,)),
        ],
        compiler_params=pltpu.CompilerParams(vmem_limit_bytes=24 * MIB),
        name="far_down",
    )(
        me, far_zero, far_one, far_two, points, low, high, near, edge,
        basis_n, up_one, up_two, *wides, *windows,
    )
    return out


def solution(mesh):
    placed = (
        P(("groups", "space"), "rhs"),
        P("space", None, None, None),
        P("space", None),
        P("space", None, None),
        P("space", None, None),
        P("space", None, None),
        P("space", None, None, None),
        P("space", None, None, None),
        P("space", None, None, None),
        P("space", None),
        P("space", None),
        P("space", None),
    )
    return jax.shard_map(
        body, mesh=mesh, in_specs=placed, out_specs=P(("groups", "space"), "rhs"), check_vma=False
    )
```

```python
import functools

import jax
import jax.numpy as jnp
from jax import lax
from jax.experimental import pallas as pl
from jax.experimental.pallas import tpu as pltpu
from jax.sharding import PartitionSpec as P

LEAF = 256
REACH = 2
SPAN = 2 * REACH + 1
DEPTH = 4
MIB = 1024 * 1024


def dot(a, b):
    return jnp.dot(a, b, preferred_element_type=jnp.float32)


def dot_t(a, b):
    return lax.dot_general(a, b, (((0,), (0,)), ((), ())), preferred_element_type=jnp.float32)


def up_kernel(
    me_ref, x_hbm, basis_hbm, up_one_hbm, up_two_hbm, plain_ref, pair_ref, points_ref,
    x_ref, basis_ref, up_one_ref, up_two_ref, sems,
):
    leaves, rank = basis_ref.shape[:2]
    steps = leaves // 4
    copies = []
    for q in range(steps):
        rows = pl.ds(q * 4 * LEAF, 4 * LEAF)
        some = pl.ds(q * 4, 4)
        copies.append(
            (
                pltpu.make_async_copy(x_hbm.at[rows, :], x_ref.at[rows, :], sems.at[2 * q]),
                pltpu.make_async_copy(basis_hbm.at[some], basis_ref.at[some], sems.at[2 * q + 1]),
            )
        )
    ups = (
        pltpu.make_async_copy(up_one_hbm, up_one_ref, sems.at[2 * steps]),
        pltpu.make_async_copy(up_two_hbm, up_two_ref, sems.at[2 * steps + 1]),
    )
    keep = pltpu.make_async_copy(x_hbm, points_ref, sems.at[2 * steps + 2])
    for pair in (*copies, ups, (keep,)):
        for copy in pair:
            copy.start()

    def put(node, value):
        value = value.astype(jnp.bfloat16)
        plain_ref[pl.ds(node * rank, rank), :] = value
        pair_ref[pl.ds(node * rank, rank), :] = value
        return value

    def join(ups, pair):
        return dot_t(ups.reshape(2 * rank, rank), jnp.concatenate(pair, axis=0))

    zeros = []
    for q in range(steps):
        for copy in copies[q]:
            copy.wait()
        for leaf in range(4 * q, 4 * q + 4):
            coef = dot(basis_ref[leaf], x_ref[pl.ds(leaf * LEAF, LEAF), :])
            zeros.append(put(leaf, coef))
    for copy in ups:
        copy.wait()
    ones = []
    for p in range(leaves // 2):
        pair = slice(2 * p, 2 * p + 2)
        ones.append(put(leaves + p, join(up_one_ref[pair], zeros[pair])))
    for q in range(leaves // 4):
        pair = slice(2 * q, 2 * q + 2)
        put(leaves + leaves // 2 + q, join(up_two_ref[pair], ones[pair]))
    odd = lax.rem(me_ref[0], 2)
    last = (leaves - 1) * LEAF
    end = pl.ds(plain_ref.shape[0] - LEAF, LEAF)
    pair_ref[end, :] = x_ref[pl.ds(pl.multiple_of((1 - odd) * last, LEAF), LEAF), :]
    plain_ref[end, :] = x_ref[pl.ds(pl.multiple_of(odd * last, LEAF), LEAF), :]
    keep.wait()


def near_kernel(
    me_ref, x_ref, list_hbm, blocks_hbm, out_ref, edge_ref, list_ref, block_buf, sems, list_sem,
):
    leaves, nears = list_ref.shape
    first = me_ref[0] * leaves

    def copies(leaf, slot):
        pairs = (
            (blocks_hbm.at[leaf, pl.ds(0, 1)], block_buf.at[slot, pl.ds(0, 1)]),
            (blocks_hbm.at[leaf, pl.ds(3, nears - 3)], block_buf.at[slot, pl.ds(1, nears - 3)]),
            (blocks_hbm.at[leaf, pl.ds(1, 2)], edge_ref.at[leaf]),
        )
        return [
            pltpu.make_async_copy(src, dst, sems.at[slot, i]) for i, (src, dst) in enumerate(pairs)
        ]

    list_copy = pltpu.make_async_copy(list_hbm, list_ref, list_sem)
    list_copy.start()
    for leaf in range(DEPTH - 1):
        for copy in copies(leaf, leaf):
            copy.start()
    list_copy.wait()

    def step(leaf, carry):
        slot = lax.rem(leaf, DEPTH)

        @pl.when(leaf + DEPTH - 1 < leaves)
        def _():
            for copy in copies(leaf + DEPTH - 1, lax.rem(leaf + DEPTH - 1, DEPTH)):
                copy.start()

        for copy in copies(leaf, slot):
            copy.wait()
        rows = []
        for k in (0, *range(3, nears)):
            start = pl.multiple_of((list_ref[leaf, k] - first) * LEAF, LEAF)
            rows.append(x_ref[pl.ds(start, LEAF), :])
        blocks = [block_buf[slot, k] for k in range(nears - 2)]
        here = pl.ds(pl.multiple_of(leaf * LEAF, LEAF), LEAF)
        out_ref[here, :] = dot(jnp.concatenate(blocks, axis=1), jnp.concatenate(rows, axis=0))
        return carry

    lax.fori_loop(0, leaves, step, 0)


def add_edge(sum_ref, near_ref, edge_ref, side, ref, start, stride):
    leaves = edge_ref.shape[0]

    def step(leaf, carry):
        here = pl.ds(pl.multiple_of(leaf * LEAF, LEAF), LEAF)
        rows = ref[pl.ds(pl.multiple_of(start + leaf * stride, LEAF), LEAF), :]
        sum_ref[here, :] = near_ref[here, :] + dot(edge_ref[leaf, side], rows)
        return carry

    lax.fori_loop(0, leaves, step, 0, unroll=4)


def window_copies(plans, wins, sizes, sems):
    copies = []
    for ref, levels, place in plans:
        start = 0
        for level in levels:
            at = pl.multiple_of(place * sizes[level], sizes[level])
            copies.append(
                pltpu.make_async_copy(
                    ref.at[pl.ds(start, sizes[level]), :],
                    wins[level].at[pl.ds(at, sizes[level]), :],
                    sems.at[len(copies)],
                )
            )
            start += sizes[level]
    return copies


def prep_kernel(
    me_ref, own_ref, pair_ref, first_ref, second_ref, near_ref, edge_ref,
    zero_hbm, one_hbm, two_hbm,
    sum_ref, zero_win, one_win, two_win, zero_wide, one_wide, two_wide,
    sum_buf, zero_buf, one_buf, two_buf, sems, win_sems, sum_sem,
):
    rank = zero_buf.shape[-1]
    levels = (
        (two_hbm, two_buf, two_wide),
        (one_hbm, one_buf, one_wide),
        (zero_hbm, zero_buf, zero_wide),
    )
    chunks = []
    for hbm, buf, wide in levels:
        for first in range(0, buf.shape[0], 4):
            some = pl.ds(first, 4)
            copy = pltpu.make_async_copy(hbm.at[some], buf.at[some], sems.at[len(chunks)])
            copy.start()
            chunks.append((copy, buf, wide, first))
    me = me_ref[0]
    odd = lax.rem(me, 2)
    block = lax.rem(me // 2, 2)
    plans = (
        (own_ref, (0, 1, 2), REACH),
        (first_ref, (0, 1, 2), (1 - block) * (SPAN - 1)),
        (second_ref, (0, 1, 2), block * (SPAN - 1)),
        (pair_ref, (0, 1, 2), REACH + 1 - 2 * odd),
    )
    wins = (zero_win, one_win, two_win)
    sizes = [win.shape[0] // SPAN for win in wins]
    moves = window_copies(plans, wins, sizes, win_sems)
    for move in moves:
        move.start()
    add_edge(sum_buf, near_ref, edge_ref, odd, pair_ref, pair_ref.shape[0] - LEAF, 0)
    moves.append(pltpu.make_async_copy(sum_buf, sum_ref, sum_sem))
    moves[-1].start()
    for copy, buf, wide, first in chunks:
        copy.wait()
        for node in range(first, first + 4):
            fars = buf.shape[1]
            wide[node] = jnp.concatenate([buf[node, k] for k in range(fars)], axis=1)
    for move in moves:
        move.wait()


def far_kernel(
    me_ref, zero_list, one_list, two_list, x_ref, low_first, low_second, high_ref, near_ref, edge_ref,
    basis_ref, up_one_ref, up_two_ref, zero_wide, one_wide, two_wide, zero_in, one_in, two_in,
    out_hbm, zero_win, one_win, two_win, sum_buf, out_buf, win_sems, out_sems, *, size,
):
    del zero_in, one_in, two_in
    leaves, fars = zero_list.shape
    rank = basis_ref.shape[1]
    me = me_ref[0]
    odd = lax.rem(me, 2)
    wins = (zero_win, one_win, two_win)
    sizes = [win.shape[0] // SPAN for win in wins]
    place = REACH - 1 + 2 * odd
    plans = ((low_first, (0,), place), (high_ref, (1, 2), place))
    moves = window_copies(plans, wins, sizes, win_sems)
    other = window_copies(((low_second, (0,), place),), wins, sizes, win_sems)[0]
    from_first = lax.rem(me + me // 2, 2) == 1
    for move in moves[1:]:
        move.start()
    pl.when(from_first)(moves[0].start)
    pl.when(jnp.logical_not(from_first))(other.start)

    alone = (me == 0) | (me == size - 1)

    @pl.when(alone)
    def _():
        add_edge(sum_buf, near_ref, edge_ref, 1 - odd, x_ref, 0, LEAF)

    @pl.when(jnp.logical_not(alone))
    def _():
        add_edge(sum_buf, near_ref, edge_ref, 1 - odd, high_ref, high_ref.shape[0] - LEAF, 0)

    for move in moves:
        move.wait()

    def field(wide, where, node, win):
        first = (me - REACH) * wide.shape[0]
        picked = []
        for k in range(fars):
            start = pl.multiple_of((where[node, k] - first) * rank, rank)
            picked.append(win[pl.ds(start, rank), :])
        return dot(wide[node], jnp.concatenate(picked, axis=0))

    down_two = [
        field(two_wide, two_list, q, two_win).astype(jnp.bfloat16) for q in range(leaves // 4)
    ]
    down_one = []
    for p in range(leaves // 2):
        total = field(one_wide, one_list, p, one_win) + dot(up_two_ref[p], down_two[p // 2])
        down_one.append(total.astype(jnp.bfloat16))
    outs = []
    for leaf in range(leaves):
        total = field(zero_wide, zero_list, leaf, zero_win)
        total = total + dot(up_one_ref[leaf], down_one[leaf // 2])
        here = pl.ds(leaf * LEAF, LEAF)
        total = sum_buf[here, :] + dot_t(basis_ref[leaf], total.astype(jnp.bfloat16))
        out_buf[here, :] = total.astype(jnp.bfloat16)
        if leaf % 4 == 3:
            some = pl.ds((leaf - 3) * LEAF, 4 * LEAF)
            outs.append(
                pltpu.make_async_copy(
                    out_buf.at[some, :], out_hbm.at[some, :], out_sems.at[leaf // 4]
                )
            )
            outs[-1].start()
    for copy in outs:
        copy.wait()


def body(
    vectors,
    near_blocks,
    near_list,
    basis,
    up_one,
    up_two,
    couple_zero,
    couple_one,
    couple_two,
    far_zero,
    far_one,
    far_two,
):
    leaves, nears = near_list.shape
    columns = vectors.shape[1]
    rank = basis.shape[2]
    fars = far_zero.shape[1]
    size = lax.axis_size("space")
    me = lax.axis_index("space").astype(jnp.int32).reshape(1)
    counts = (leaves, leaves // 2, leaves // 4)
    rows = sum(counts) * rank + LEAF
    basis_t = jnp.swapaxes(basis, 1, 2)
    bf16 = jnp.bfloat16

    hbm = pl.BlockSpec(memory_space=pltpu.HBM)
    vmem = pl.BlockSpec(memory_space=pltpu.VMEM)
    smem = pl.BlockSpec(memory_space=pltpu.SMEM)

    def in_hbm(*arrays):
        return [pltpu.with_memory_space_constraint(a, pltpu.HBM) for a in arrays]

    plain, pair, points = pl.pallas_call(
        up_kernel,
        in_specs=[smem] + [hbm] * 4,
        out_specs=[vmem] * 3,
        out_shape=[
            pltpu.VMEM((rows, columns), bf16),
            pltpu.VMEM((rows, columns), bf16),
            pltpu.VMEM(vectors.shape, bf16),
        ],
        scratch_shapes=[
            pltpu.VMEM(vectors.shape, bf16),
            pltpu.VMEM(basis_t.shape, bf16),
            pltpu.VMEM(up_one.shape, bf16),
            pltpu.VMEM(up_two.shape, bf16),
            pltpu.SemaphoreType.DMA((leaves // 2 + 3,)),
        ],
        compiler_params=pltpu.CompilerParams(vmem_limit_bytes=16 * MIB),
        name="up_pass",
    )(me, *in_hbm(vectors, basis_t, up_one, up_two))

    cores = lax.axis_size("rhs")

    def send(array, to):
        pairs = []
        for i in range(size):
            for c in range(cores):
                j, d = (to(i), c) if 0 <= to(i) < size else (i, cores - 1 - c)
                pairs.append((i * cores + c, j * cores + d))
        return lax.ppermute(array, ("space", "rhs"), pairs)

    from_pair = send(pair, lambda i: i + 1 - 2 * (i % 2))
    turns = (lambda i: i + 2 - i // 2 % 2 * 4, lambda i: i - 2 + i // 2 % 2 * 4)
    first, second = [send(plain, turn) for turn in turns]

    near, edge = pl.pallas_call(
        near_kernel,
        in_specs=[smem, vmem] + [hbm] * 2,
        out_specs=[vmem] * 2,
        out_shape=[
            jax.ShapeDtypeStruct(vectors.shape, jnp.float32),
            jax.ShapeDtypeStruct((leaves, 2, LEAF, LEAF), bf16),
        ],
        scratch_shapes=[
            pltpu.SMEM(near_list.shape, jnp.int32),
            pltpu.VMEM((DEPTH, nears - 2, LEAF, LEAF), bf16),
            pltpu.SemaphoreType.DMA((DEPTH, 3)),
            pltpu.SemaphoreType.DMA,
        ],
        compiler_params=pltpu.CompilerParams(vmem_limit_bytes=24 * MIB),
        cost_estimate=pl.CostEstimate(
            flops=2 * leaves * (nears - 2) * LEAF * LEAF * columns,
            bytes_accessed=2 * leaves * nears * LEAF * LEAF + 6 * leaves * LEAF * columns,
            transcendentals=0,
        ),
        name="near_own",
    )(me, points, *in_hbm(near_list, near_blocks))

    split = leaves * rank
    from_pair, near = lax.optimization_barrier((from_pair, near))
    lows = [send(from_pair[:split], turn) for turn in turns]
    first, second, near = lax.optimization_barrier((first, second, near))
    upper = jnp.where((me[0] // 2 + me[0]) % 2 == 0, first[split:], second[split:])
    high = send(upper, lambda i: i + 1 - 2 * (i % 2))

    wins = [jax.ShapeDtypeStruct((SPAN * n * rank, columns), bf16) for n in counts]
    near, *rest = pl.pallas_call(
        prep_kernel,
        in_specs=[smem] + [vmem] * 6 + [hbm] * 3,
        out_specs=[vmem] * 7,
        out_shape=[
            jax.ShapeDtypeStruct(vectors.shape, jnp.float32),
            *wins,
            *[jax.ShapeDtypeStruct((n, rank, fars * rank), bf16) for n in counts],
        ],
        scratch_shapes=[
            pltpu.VMEM(vectors.shape, jnp.float32),
            *[pltpu.VMEM((n, fars, rank, rank), bf16) for n in counts],
            pltpu.SemaphoreType.DMA((sum(n // 4 for n in counts),)),
            pltpu.SemaphoreType.DMA((12,)),
            pltpu.SemaphoreType.DMA,
        ],
        compiler_params=pltpu.CompilerParams(vmem_limit_bytes=24 * MIB),
        cost_estimate=pl.CostEstimate(
            flops=2 * leaves * LEAF * LEAF * columns,
            bytes_accessed=4 * sum(counts) * fars * rank * rank,
            transcendentals=0,
        ),
        name="prep",
    )(
        me, plain, from_pair, first, second, near, edge,
        *in_hbm(couple_zero, couple_one, couple_two),
    )
    windows, wides = rest[:3], rest[3:]

    out, *_ = pl.pallas_call(
        functools.partial(far_kernel, size=size),
        in_specs=[smem] * 4 + [vmem] * 15,
        out_specs=[hbm] + [vmem] * 3,
        out_shape=[jax.ShapeDtypeStruct(vectors.shape, bf16), *wins],
        input_output_aliases={16: 1, 17: 2, 18: 3},
        scratch_shapes=[
            pltpu.VMEM(vectors.shape, jnp.float32),
            pltpu.VMEM(vectors.shape, bf16),
            pltpu.SemaphoreType.DMA((3,)),
            pltpu.SemaphoreType.DMA((leaves // 4,)),
        ],
        compiler_params=pltpu.CompilerParams(vmem_limit_bytes=24 * MIB),
        name="far_down",
    )(
        me, far_zero, far_one, far_two, points, *lows, high, near, edge,
        basis_t, up_one, up_two, *wides, *windows,
    )
    return out


def solution(mesh):
    placed = (
        P(("groups", "space"), "rhs"),
        P("space", None, None, None),
        P("space", None),
        P("space", None, None),
        P("space", None, None),
        P("space", None, None),
        P("space", None, None, None),
        P("space", None, None, None),
        P("space", None, None, None),
        P("space", None),
        P("space", None),
        P("space", None),
    )
    return jax.shard_map(
        body, mesh=mesh, in_specs=placed, out_specs=P(("groups", "space"), "rhs"), check_vma=False
    )
```

```python
import functools

import jax
import jax.numpy as jnp
from jax import lax
from jax.experimental import pallas as pl
from jax.experimental.pallas import tpu as pltpu
from jax.sharding import PartitionSpec as P

LEAF = 256
REACH = 2
SPAN = 2 * REACH + 1
DEPTH = 4
MIB = 1024 * 1024


def dot(a, b):
    return jnp.dot(a, b, preferred_element_type=jnp.float32)


def dot_t(a, b):
    return lax.dot_general(a, b, (((0,), (0,)), ((), ())), preferred_element_type=jnp.float32)


def up_kernel(
    me_ref, x_hbm, basis_hbm, up_one_hbm, up_two_hbm, plain_ref, pair_ref,
    x_ref, basis_ref, up_one_ref, up_two_ref, sems,
):
    leaves, rank = basis_ref.shape[:2]
    steps = leaves // 4
    copies = []
    for q in range(steps):
        rows = pl.ds(q * 4 * LEAF, 4 * LEAF)
        some = pl.ds(q * 4, 4)
        copies.append(
            (
                pltpu.make_async_copy(x_hbm.at[rows, :], x_ref.at[rows, :], sems.at[2 * q]),
                pltpu.make_async_copy(basis_hbm.at[some], basis_ref.at[some], sems.at[2 * q + 1]),
            )
        )
    ups = (
        pltpu.make_async_copy(up_one_hbm, up_one_ref, sems.at[2 * steps]),
        pltpu.make_async_copy(up_two_hbm, up_two_ref, sems.at[2 * steps + 1]),
    )
    for pair in (*copies, ups):
        for copy in pair:
            copy.start()

    def put(node, value):
        value = value.astype(jnp.bfloat16)
        plain_ref[pl.ds(node * rank, rank), :] = value
        pair_ref[pl.ds(2 * LEAF + node * rank, rank), :] = value
        return value

    def join(ups, pair):
        return dot_t(ups.reshape(2 * rank, rank), jnp.concatenate(pair, axis=0))

    zeros = []
    for q in range(steps):
        for copy in copies[q]:
            copy.wait()
        for leaf in range(4 * q, 4 * q + 4):
            coef = dot(basis_ref[leaf], x_ref[pl.ds(leaf * LEAF, LEAF), :])
            zeros.append(put(leaf, coef))
    for copy in ups:
        copy.wait()
    ones = []
    for p in range(leaves // 2):
        pair = slice(2 * p, 2 * p + 2)
        ones.append(put(leaves + p, join(up_one_ref[pair], zeros[pair])))
    for q in range(leaves // 4):
        pair = slice(2 * q, 2 * q + 2)
        put(leaves + leaves // 2 + q, join(up_two_ref[pair], ones[pair]))
    odd = lax.rem(me_ref[0], 2)
    last = (leaves - 1) * LEAF
    near_edge = pl.multiple_of((1 - odd) * last, LEAF)
    far_edge = pl.multiple_of(odd * last, LEAF)
    pair_ref[pl.ds(0, LEAF), :] = x_ref[pl.ds(near_edge, LEAF), :]
    pair_ref[pl.ds(LEAF, LEAF), :] = x_ref[pl.ds(far_edge, LEAF), :]


def last_place(me):
    return REACH - 1 + 2 * lax.rem(me, 2)


def near_kernel(
    me_ref, x_ref, near_hbm, zero_list_hbm, one_list_hbm, two_list_hbm,
    blocks_hbm, zero_hbm, one_hbm, two_hbm,
    out_ref, edge_ref, zero_wide, one_wide, two_wide, starts_ref,
    near_list, zero_list, one_list, two_list, turn_ref,
    block_buf, zero_buf, upper_buf, sems, list_sems,
):
    leaves, nears = near_list.shape
    ones, twos = one_wide.shape[0], two_wide.shape[0]
    fars, rank = zero_buf.shape[1:3]
    total = leaves + ones + twos
    me = me_ref[0]

    def copies(leaf, slot):
        pairs = (
            (blocks_hbm.at[leaf, pl.ds(0, 1)], block_buf.at[slot, pl.ds(0, 1)]),
            (blocks_hbm.at[leaf, pl.ds(3, nears - 3)], block_buf.at[slot, pl.ds(1, nears - 3)]),
            (blocks_hbm.at[leaf, pl.ds(1, 2)], edge_ref.at[leaf]),
            (zero_hbm.at[leaf], zero_buf.at[slot]),
        )
        return [
            pltpu.make_async_copy(src, dst, sems.at[slot, i]) for i, (src, dst) in enumerate(pairs)
        ]

    def upper(leaf, slot, act):
        sem = sems.at[slot, 4]

        @pl.when(leaf < ones)
        def _():
            act(pltpu.make_async_copy(one_hbm.at[leaf], upper_buf.at[slot], sem))

        @pl.when((leaf >= ones) & (leaf < ones + twos))
        def _():
            act(pltpu.make_async_copy(two_hbm.at[leaf - ones], upper_buf.at[slot], sem))

    def fetch(leaf, slot):
        for copy in copies(leaf, slot):
            copy.start()
        upper(leaf, slot, lambda copy: copy.start())

    hbms = (near_hbm, zero_list_hbm, one_list_hbm, two_list_hbm)
    lists = (near_list, zero_list, one_list, two_list)
    moves = [
        pltpu.make_async_copy(src, dst, list_sems.at[i])
        for i, (src, dst) in enumerate(zip(hbms, lists))
    ]
    for move in moves:
        move.start()
    for leaf in range(DEPTH - 1):
        fetch(leaf, leaf)
    starts_ref[total, 0] = 0
    for move in moves:
        move.wait()

    def pack(where, node, row, buf, wide):
        per = where.shape[0]
        first = (me - REACH) * per
        low = last_place(me) * per
        count = jnp.int32(0)
        for k in range(fars):
            index = where[node, k] - first
            late = (index >= low) & (index < low + per)
            at = jnp.where(late, count, fars - 1 - k + count)
            starts_ref[row, at] = index * rank
            turn_ref[at] = k
            count = count + late.astype(jnp.int32)
        starts_ref[total, 0] = jnp.maximum(starts_ref[total, 0], count)
        wide[node] = jnp.concatenate([buf[turn_ref[k]] for k in range(fars)], axis=1)

    def step(leaf, carry):
        slot = lax.rem(leaf, DEPTH)

        @pl.when(leaf + DEPTH - 1 < leaves)
        def _():
            fetch(leaf + DEPTH - 1, lax.rem(leaf + DEPTH - 1, DEPTH))

        for copy in copies(leaf, slot):
            copy.wait()
        upper(leaf, slot, lambda copy: copy.wait())
        rows = []
        for k in (0, *range(3, nears)):
            start = pl.multiple_of((near_list[leaf, k] - me * leaves) * LEAF, LEAF)
            rows.append(x_ref[pl.ds(start, LEAF), :])
        blocks = [block_buf[slot, k] for k in range(nears - 2)]
        here = pl.ds(pl.multiple_of(leaf * LEAF, LEAF), LEAF)
        out_ref[here, :] = dot(jnp.concatenate(blocks, axis=1), jnp.concatenate(rows, axis=0))
        pack(zero_list, leaf, leaf, zero_buf.at[slot], zero_wide)

        @pl.when(leaf < ones)
        def _():
            pack(one_list, leaf, leaves + leaf, upper_buf.at[slot], one_wide)

        @pl.when((leaf >= ones) & (leaf < ones + twos))
        def _():
            pack(two_list, leaf - ones, leaves + leaf, upper_buf.at[slot], two_wide)

        return carry

    lax.fori_loop(0, leaves, step, 0)


def add_edge(sum_ref, near_ref, edge_ref, side, ref, start, stride):
    leaves = edge_ref.shape[0]

    def step(leaf, carry):
        here = pl.ds(pl.multiple_of(leaf * LEAF, LEAF), LEAF)
        rows = ref[pl.ds(pl.multiple_of(start + leaf * stride, LEAF), LEAF), :]
        sum_ref[here, :] = near_ref[here, :] + dot(edge_ref[leaf, side], rows)
        return carry

    lax.fori_loop(0, leaves, step, 0, unroll=4)


def window_copies(plans, sems):
    copies = []
    for ref, start, win, at, size in plans:
        copies.append(
            pltpu.make_async_copy(
                ref.at[pl.ds(start, size), :], win.at[pl.ds(at, size), :], sems.at[len(copies)]
            )
        )
    return copies


def field(wide, starts_ref, row, win, slots):
    rank = wide.shape[0]
    rows = []
    for k in slots:
        rows.append(win[pl.ds(pl.multiple_of(starts_ref[row, k], rank), rank), :])
    some = wide[:, slots[0] * rank : (slots[-1] + 1) * rank]
    return dot(some, jnp.concatenate(rows, axis=0))


def mid_kernel(
    me_ref, starts_ref, own_ref, pair_ref, first_ref, second_ref, near_ref, edge_ref,
    zero_wide, one_wide, two_wide, sum_ref, zero_win, one_win, two_win, part_ref, sems,
):
    me = me_ref[0]
    odd = lax.rem(me, 2)
    block = lax.rem(me // 2, 2)
    wins, wides = (zero_win, one_win, two_win), (zero_wide, one_wide, two_wide)
    pieces = (
        (own_ref, 0, REACH),
        (first_ref, 0, (1 - block) * (SPAN - 1)),
        (second_ref, 0, block * (SPAN - 1)),
        (pair_ref, 2 * LEAF, REACH + 1 - 2 * odd),
    )
    plans = []
    for ref, start, place in pieces:
        for win in wins:
            size = win.shape[0] // SPAN
            plans.append((ref, start, win, pl.multiple_of(place * size, size), size))
            start += size
    moves = window_copies(plans, sems)
    for move in moves:
        move.start()
    add_edge(sum_ref, near_ref, edge_ref, odd, pair_ref, 0, 0)
    for move in moves:
        move.wait()
    row = 0
    for wide, win in zip(wides, wins):
        nodes, rank, deep = wide.shape
        fars = deep // rank
        for node in range(nodes):
            part = field(wide.at[node], starts_ref, row, win, range(fars // 2, fars))
            part_ref[pl.ds(row * rank, rank), :] = part
            row += 1


def far_kernel(
    me_ref, starts_ref, x_ref, low_first, low_second, high_ref, near_ref, edge_ref,
    basis_ref, up_one_ref, up_two_ref, zero_wide, one_wide, two_wide,
    zero_in, one_in, two_in, part_in,
    out_hbm, zero_win, one_win, two_win, part_ref, sum_buf, out_buf, win_sems, out_sems, *, size,
):
    del zero_in, one_in, two_in, part_in
    leaves, rank, deep = zero_wide.shape
    ones, twos = leaves // 2, leaves // 4
    fars = deep // rank
    me = me_ref[0]
    odd = lax.rem(me, 2)
    place = last_place(me)
    sizes = [n * rank for n in (leaves, ones, twos)]
    at = [pl.multiple_of(place * n, n) for n in sizes]
    split = sizes[0] - LEAF
    moves = window_copies(
        (
            (low_first, LEAF, zero_win, at[0], split),
            (high_ref, 0, zero_win, pl.multiple_of(at[0] + split, LEAF), LEAF),
            (high_ref, LEAF, one_win, at[1], sizes[1]),
            (high_ref, LEAF + sizes[1], two_win, at[2], sizes[2]),
        ),
        win_sems,
    )
    other = window_copies(((low_second, LEAF, zero_win, at[0], split),), win_sems)[0]
    from_first = lax.rem(me + me // 2, 2) == 1
    for move in moves[1:]:
        move.start()
    pl.when(from_first)(moves[0].start)
    pl.when(jnp.logical_not(from_first))(other.start)

    alone = (me == 0) | (me == size - 1)

    @pl.when(alone)
    def _():
        add_edge(sum_buf, near_ref, edge_ref, 1 - odd, x_ref, 0, LEAF)

    @pl.when(jnp.logical_not(alone) & from_first)
    def _():
        add_edge(sum_buf, near_ref, edge_ref, 1 - odd, low_first, 0, 0)

    @pl.when(jnp.logical_not(alone) & jnp.logical_not(from_first))
    def _():
        add_edge(sum_buf, near_ref, edge_ref, 1 - odd, low_second, 0, 0)

    for move in moves:
        move.wait()

    @pl.when(starts_ref[leaves + ones + twos, 0] > fars // 2)
    def _():
        levels = ((zero_wide, zero_win, 0), (one_wide, one_win, leaves))
        for wide, win, base in (*levels, (two_wide, two_win, leaves + ones)):

            def again(node, carry):
                row = base + node
                part = field(wide.at[node], starts_ref, row, win, range(fars // 2, fars))
                part_ref[pl.ds(pl.multiple_of(row * rank, rank), rank), :] = part
                return carry

            lax.fori_loop(0, wide.shape[0], again, 0)

    def whole_field(wide, win, node, row):
        part = part_ref[pl.ds(row * rank, rank), :]
        return part + field(wide.at[node], starts_ref, row, win, range(fars // 2))

    down_two = [
        whole_field(two_wide, two_win, q, leaves + ones + q).astype(jnp.bfloat16)
        for q in range(twos)
    ]
    down_one = []
    for p in range(ones):
        total = whole_field(one_wide, one_win, p, leaves + p) + dot(up_two_ref[p], down_two[p // 2])
        down_one.append(total.astype(jnp.bfloat16))
    outs = []
    for leaf in range(leaves):
        total = whole_field(zero_wide, zero_win, leaf, leaf)
        total = total + dot(up_one_ref[leaf], down_one[leaf // 2])
        here = pl.ds(leaf * LEAF, LEAF)
        total = sum_buf[here, :] + dot_t(basis_ref[leaf], total.astype(jnp.bfloat16))
        out_buf[here, :] = total.astype(jnp.bfloat16)
        if leaf % 4 == 3:
            some = pl.ds((leaf - 3) * LEAF, 4 * LEAF)
            outs.append(
                pltpu.make_async_copy(
                    out_buf.at[some, :], out_hbm.at[some, :], out_sems.at[leaf // 4]
                )
            )
            outs[-1].start()
    for copy in outs:
        copy.wait()


def body(
    vectors,
    near_blocks,
    near_list,
    basis,
    up_one,
    up_two,
    couple_zero,
    couple_one,
    couple_two,
    far_zero,
    far_one,
    far_two,
):
    leaves, nears = near_list.shape
    columns = vectors.shape[1]
    rank = basis.shape[2]
    fars = far_zero.shape[1]
    size = lax.axis_size("space")
    cores = lax.axis_size("rhs")
    me = lax.axis_index("space").astype(jnp.int32).reshape(1)
    counts = (leaves, leaves // 2, leaves // 4)
    nodes = sum(counts)
    basis_t = jnp.swapaxes(basis, 1, 2)
    bf16, f32 = jnp.bfloat16, jnp.float32

    hbm = pl.BlockSpec(memory_space=pltpu.HBM)
    vmem = pl.BlockSpec(memory_space=pltpu.VMEM)
    smem = pl.BlockSpec(memory_space=pltpu.SMEM)

    def in_hbm(*arrays):
        return [pltpu.with_memory_space_constraint(a, pltpu.HBM) for a in arrays]

    plain, pair = pl.pallas_call(
        up_kernel,
        in_specs=[smem] + [hbm] * 4,
        out_specs=[vmem] * 2,
        out_shape=[
            pltpu.VMEM((nodes * rank, columns), bf16),
            pltpu.VMEM((2 * LEAF + nodes * rank, columns), bf16),
        ],
        scratch_shapes=[
            pltpu.VMEM(vectors.shape, bf16),
            pltpu.VMEM(basis_t.shape, bf16),
            pltpu.VMEM(up_one.shape, bf16),
            pltpu.VMEM(up_two.shape, bf16),
            pltpu.SemaphoreType.DMA((leaves // 2 + 2,)),
        ],
        compiler_params=pltpu.CompilerParams(vmem_limit_bytes=8 * MIB),
        name="up_pass",
    )(me, *in_hbm(vectors, basis_t, up_one, up_two))

    def send(array, to):
        pairs = []
        for i in range(size):
            for c in range(cores):
                j, d = (to(i), c) if 0 <= to(i) < size else (i, cores - 1 - c)
                pairs.append((i * cores + c, j * cores + d))
        return lax.ppermute(array, ("space", "rhs"), pairs)

    def partner(i):
        return i + 1 - 2 * (i % 2)

    from_pair = send(pair, partner)
    turns = (lambda i: i + 2 - i // 2 % 2 * 4, lambda i: i - 2 + i // 2 % 2 * 4)
    first, second = [send(plain, turn) for turn in turns]

    near, edge, *wides, starts = pl.pallas_call(
        near_kernel,
        in_specs=[smem, vmem] + [hbm] * 8,
        out_specs=[vmem] * 5 + [smem],
        out_shape=[
            pltpu.VMEM(vectors.shape, f32),
            pltpu.VMEM((leaves, 2, LEAF, LEAF), bf16),
            *[pltpu.VMEM((n, rank, fars * rank), bf16) for n in counts],
            jax.ShapeDtypeStruct((nodes + 1, fars), jnp.int32),
        ],
        scratch_shapes=[
            *[pltpu.SMEM(a.shape, jnp.int32) for a in (near_list, far_zero, far_one, far_two)],
            pltpu.SMEM((fars,), jnp.int32),
            pltpu.VMEM((DEPTH, nears - 2, LEAF, LEAF), bf16),
            pltpu.VMEM((DEPTH, fars, rank, rank), bf16),
            pltpu.VMEM((DEPTH, fars, rank, rank), bf16),
            pltpu.SemaphoreType.DMA((DEPTH, 5)),
            pltpu.SemaphoreType.DMA((4,)),
        ],
        compiler_params=pltpu.CompilerParams(vmem_limit_bytes=16 * MIB),
        cost_estimate=pl.CostEstimate(
            flops=2 * leaves * (nears - 2) * LEAF * LEAF * columns,
            bytes_accessed=2 * leaves * nears * LEAF * LEAF + 6 * leaves * LEAF * columns,
            transcendentals=0,
        ),
        name="near_own",
    )(
        me,
        pltpu.with_memory_space_constraint(vectors, pltpu.VMEM),
        *in_hbm(near_list, far_zero, far_one, far_two),
        *in_hbm(near_blocks, couple_zero, couple_one, couple_two),
    )

    split = leaves * rank - LEAF
    from_pair, near = lax.optimization_barrier((from_pair, near))
    lows = [send(from_pair[LEAF : 2 * LEAF + split], turn) for turn in turns]
    first, second, near = lax.optimization_barrier((first, second, near))
    upper = jnp.where((me[0] // 2 + me[0]) % 2 == 0, first[split:], second[split:])
    high = send(upper, partner)

    sums, *windows, part = pl.pallas_call(
        mid_kernel,
        in_specs=[smem] * 2 + [vmem] * 9,
        out_specs=[vmem] * 5,
        out_shape=[
            pltpu.VMEM(vectors.shape, f32),
            *[pltpu.VMEM((SPAN * n * rank, columns), bf16) for n in counts],
            pltpu.VMEM((nodes * rank, columns), f32),
        ],
        scratch_shapes=[pltpu.SemaphoreType.DMA((12,))],
        compiler_params=pltpu.CompilerParams(vmem_limit_bytes=8 * MIB),
        cost_estimate=pl.CostEstimate(
            flops=2 * leaves * LEAF * LEAF * columns + nodes * fars * rank * rank * columns,
            bytes_accessed=4 * nodes * fars * rank * rank,
            transcendentals=0,
        ),
        name="mid",
    )(me, starts, plain, from_pair, first, second, near, edge, *wides)

    out, *_ = pl.pallas_call(
        functools.partial(far_kernel, size=size),
        in_specs=[smem] * 2 + [vmem] * 16,
        out_specs=[hbm] + [vmem] * 4,
        out_shape=[
            jax.ShapeDtypeStruct(vectors.shape, bf16),
            *[pltpu.VMEM((SPAN * n * rank, columns), bf16) for n in counts],
            pltpu.VMEM((nodes * rank, columns), f32),
        ],
        input_output_aliases={14: 1, 15: 2, 16: 3, 17: 4},
        scratch_shapes=[
            pltpu.VMEM(vectors.shape, f32),
            pltpu.VMEM(vectors.shape, bf16),
            pltpu.SemaphoreType.DMA((4,)),
            pltpu.SemaphoreType.DMA((leaves // 4,)),
        ],
        compiler_params=pltpu.CompilerParams(vmem_limit_bytes=16 * MIB),
        name="far_down",
    )(
        me, starts, pltpu.with_memory_space_constraint(vectors, pltpu.VMEM), *lows, high, sums, edge,
        basis_t, up_one, up_two, *wides, *windows, part,
    )
    return out


def solution(mesh):
    placed = (
        P(("groups", "space"), "rhs"),
        P("space", None, None, None),
        P("space", None),
        P("space", None, None),
        P("space", None, None),
        P("space", None, None),
        P("space", None, None, None),
        P("space", None, None, None),
        P("space", None, None, None),
        P("space", None),
        P("space", None),
        P("space", None),
    )
    return jax.shard_map(
        body, mesh=mesh, in_specs=placed, out_specs=P(("groups", "space"), "rhs"), check_vma=False
    )
```

```python
import functools

import jax
import jax.numpy as jnp
from jax import lax
from jax.experimental import pallas as pl
from jax.experimental.pallas import tpu as pltpu
from jax.sharding import PartitionSpec as P

LEAF = 256
REACH = 2
SPAN = 2 * REACH + 1
DEPTH = 4
MIB = 1024 * 1024


def dot(a, b):
    return jnp.dot(a, b, preferred_element_type=jnp.float32)


def dot_t(a, b):
    return lax.dot_general(a, b, (((0,), (0,)), ((), ())), preferred_element_type=jnp.float32)


def up_kernel(
    me_ref, x_hbm, basis_hbm, up_one_hbm, up_two_hbm, plain_ref, pair_ref,
    x_ref, basis_ref, up_one_ref, up_two_ref, sems,
):
    leaves, rank = basis_ref.shape[:2]
    steps = leaves // 4
    copies = []
    for q in range(steps):
        rows = pl.ds(q * 4 * LEAF, 4 * LEAF)
        some = pl.ds(q * 4, 4)
        copies.append(
            (
                pltpu.make_async_copy(x_hbm.at[rows, :], x_ref.at[rows, :], sems.at[2 * q]),
                pltpu.make_async_copy(basis_hbm.at[some], basis_ref.at[some], sems.at[2 * q + 1]),
            )
        )
    ups = (
        pltpu.make_async_copy(up_one_hbm, up_one_ref, sems.at[2 * steps]),
        pltpu.make_async_copy(up_two_hbm, up_two_ref, sems.at[2 * steps + 1]),
    )
    for pair in (*copies, ups):
        for copy in pair:
            copy.start()

    def put(node, value):
        value = value.astype(jnp.bfloat16)
        plain_ref[pl.ds(node * rank, rank), :] = value
        pair_ref[pl.ds(2 * LEAF + node * rank, rank), :] = value
        return value

    def join(ups, pair):
        return dot_t(ups.reshape(2 * rank, rank), jnp.concatenate(pair, axis=0))

    zeros = []
    for q in range(steps):
        for copy in copies[q]:
            copy.wait()
        for leaf in range(4 * q, 4 * q + 4):
            coef = dot(basis_ref[leaf], x_ref[pl.ds(leaf * LEAF, LEAF), :])
            zeros.append(put(leaf, coef))
    for copy in ups:
        copy.wait()
    ones = []
    for p in range(leaves // 2):
        pair = slice(2 * p, 2 * p + 2)
        ones.append(put(leaves + p, join(up_one_ref[pair], zeros[pair])))
    for q in range(leaves // 4):
        pair = slice(2 * q, 2 * q + 2)
        put(leaves + leaves // 2 + q, join(up_two_ref[pair], ones[pair]))
    odd = lax.rem(me_ref[0], 2)
    last = (leaves - 1) * LEAF
    near_edge = pl.multiple_of((1 - odd) * last, LEAF)
    far_edge = pl.multiple_of(odd * last, LEAF)
    pair_ref[pl.ds(0, LEAF), :] = x_ref[pl.ds(near_edge, LEAF), :]
    pair_ref[pl.ds(LEAF, LEAF), :] = x_ref[pl.ds(far_edge, LEAF), :]


def last_place(me):
    return REACH - 1 + 2 * lax.rem(me, 2)


def near_kernel(
    me_ref, list_hbm, x_hbm, blocks_hbm, out_ref, edge_ref, x_ref,
    list_ref, block_buf, sems, x_sem, list_sem,
):
    leaves, nears = list_ref.shape
    first = me_ref[0] * leaves

    def copies(leaf, slot):
        pairs = (
            (blocks_hbm.at[leaf, pl.ds(0, 1)], block_buf.at[slot, pl.ds(0, 1)]),
            (blocks_hbm.at[leaf, pl.ds(3, nears - 3)], block_buf.at[slot, pl.ds(1, nears - 3)]),
            (blocks_hbm.at[leaf, pl.ds(1, 2)], edge_ref.at[leaf]),
        )
        return [
            pltpu.make_async_copy(src, dst, sems.at[slot, i]) for i, (src, dst) in enumerate(pairs)
        ]

    list_copy = pltpu.make_async_copy(list_hbm, list_ref, list_sem)
    x_copy = pltpu.make_async_copy(x_hbm, x_ref, x_sem)
    list_copy.start()
    x_copy.start()
    for leaf in range(DEPTH - 1):
        for copy in copies(leaf, leaf):
            copy.start()
    list_copy.wait()
    x_copy.wait()

    def step(leaf, carry):
        slot = lax.rem(leaf, DEPTH)

        @pl.when(leaf + DEPTH - 1 < leaves)
        def _():
            for copy in copies(leaf + DEPTH - 1, lax.rem(leaf + DEPTH - 1, DEPTH)):
                copy.start()

        for copy in copies(leaf, slot):
            copy.wait()
        rows = []
        for k in (0, *range(3, nears)):
            start = pl.multiple_of((list_ref[leaf, k] - first) * LEAF, LEAF)
            rows.append(x_ref[pl.ds(start, LEAF), :])
        blocks = [block_buf[slot, k] for k in range(nears - 2)]
        here = pl.ds(pl.multiple_of(leaf * LEAF, LEAF), LEAF)
        out_ref[here, :] = dot(jnp.concatenate(blocks, axis=1), jnp.concatenate(rows, axis=0))
        return carry

    lax.fori_loop(0, leaves, step, 0)


def add_edge(sum_ref, near_ref, edge_ref, side, rows):
    for leaf in range(edge_ref.shape[0]):
        here = pl.ds(leaf * LEAF, LEAF)
        sum_ref[here, :] = near_ref[here, :] + dot(edge_ref[leaf, side], rows)


def window_copies(plans, sems):
    copies = []
    for ref, start, win, at, size in plans:
        copies.append(
            pltpu.make_async_copy(
                ref.at[pl.ds(start, size), :], win.at[pl.ds(at, size), :], sems.at[len(copies)]
            )
        )
    return copies


def prep_kernel(
    me_ref, own_ref, pair_ref, first_ref, second_ref, near_ref, edge_ref,
    zero_hbm, one_hbm, two_hbm,
    sum_ref, zero_win, one_win, two_win, zero_wide, one_wide, two_wide,
    zero_buf, one_buf, two_buf, sems, win_sems,
):
    levels = (
        (two_hbm, two_buf, two_wide),
        (one_hbm, one_buf, one_wide),
        (zero_hbm, zero_buf, zero_wide),
    )
    chunks = []
    for hbm, buf, wide in levels:
        for first in range(0, buf.shape[0], 4):
            some = pl.ds(first, 4)
            copy = pltpu.make_async_copy(hbm.at[some], buf.at[some], sems.at[len(chunks)])
            copy.start()
            chunks.append((copy, buf, wide, first))
    me = me_ref[0]
    odd = lax.rem(me, 2)
    block = lax.rem(me // 2, 2)
    pieces = (
        (own_ref, 0, REACH),
        (first_ref, 0, (1 - block) * (SPAN - 1)),
        (second_ref, 0, block * (SPAN - 1)),
        (pair_ref, 2 * LEAF, REACH + 1 - 2 * odd),
    )
    plans = []
    for ref, start, place in pieces:
        for win in (zero_win, one_win, two_win):
            size = win.shape[0] // SPAN
            plans.append((ref, start, win, pl.multiple_of(place * size, size), size))
            start += size
    moves = window_copies(plans, win_sems)
    for move in moves:
        move.start()
    add_edge(sum_ref, near_ref, edge_ref, odd, pair_ref[pl.ds(0, LEAF), :])
    for copy, buf, wide, first in chunks:
        copy.wait()
        for node in range(first, first + 4):
            fars = buf.shape[1]
            wide[node] = jnp.concatenate([buf[node, k] for k in range(fars)], axis=1)
    for move in moves:
        move.wait()


def far_kernel(
    me_ref, zero_list, one_list, two_list, x_ref, low_first, low_second, high_ref, near_ref, edge_ref,
    basis_ref, up_one_ref, up_two_ref, zero_wide, one_wide, two_wide, zero_in, one_in, two_in,
    out_hbm, zero_win, one_win, two_win,
    sum_buf, out_buf, rows_buf, field_buf, down_buf, win_sems, out_sems, *, size,
):
    del zero_in, one_in, two_in
    leaves, rank, deep = zero_wide.shape
    ones, twos = leaves // 2, leaves // 4
    fars = deep // rank
    me = me_ref[0]
    odd = lax.rem(me, 2)
    place = REACH - 1 + 2 * odd
    sizes = [n * rank for n in (leaves, ones, twos)]
    at = [pl.multiple_of(place * n, n) for n in sizes]
    split = sizes[0] - LEAF
    moves = window_copies(
        (
            (low_first, LEAF, zero_win, at[0], split),
            (high_ref, 0, zero_win, pl.multiple_of(at[0] + split, LEAF), LEAF),
            (high_ref, LEAF, one_win, at[1], sizes[1]),
            (high_ref, LEAF + sizes[1], two_win, at[2], sizes[2]),
        ),
        win_sems,
    )
    other = window_copies(((low_second, LEAF, zero_win, at[0], split),), win_sems)[0]
    from_first = lax.rem(me + me // 2, 2) == 1
    for move in moves[1:]:
        move.start()

    @pl.when(from_first)
    def _():
        moves[0].start()
        rows_buf[...] = low_first[pl.ds(0, LEAF), :]

    @pl.when(jnp.logical_not(from_first))
    def _():
        other.start()
        rows_buf[...] = low_second[pl.ds(0, LEAF), :]

    alone = (me == 0) | (me == size - 1)

    @pl.when(alone)
    def _():
        for leaf in range(leaves):
            here = pl.ds(leaf * LEAF, LEAF)
            sum_buf[here, :] = near_ref[here, :] + dot(edge_ref[leaf, 1 - odd], x_ref[here, :])

    @pl.when(jnp.logical_not(alone))
    def _():
        add_edge(sum_buf, near_ref, edge_ref, 1 - odd, rows_buf[...])

    for move in moves:
        move.wait()

    def node_rows(row):
        return pl.ds(row * rank, rank)

    base = leaves + ones
    levels = (
        (two_wide, two_list, two_win, base),
        (one_wide, one_list, one_win, leaves),
        (zero_wide, zero_list, zero_win, 0),
    )
    for wide, where, win, row in levels:
        first = (me - REACH) * wide.shape[0]
        for node in range(wide.shape[0]):
            picked = []
            for k in range(fars):
                start = pl.multiple_of((where[node, k] - first) * rank, rank)
                picked.append(win[pl.ds(start, rank), :])
            field_buf[node_rows(row + node), :] = dot(wide[node], jnp.concatenate(picked, axis=0))
    for q in range(twos):
        down_buf[node_rows(base + q), :] = field_buf[node_rows(base + q), :].astype(jnp.bfloat16)
    for p in range(ones):
        total = dot(up_two_ref[p], down_buf[node_rows(base + p // 2), :])
        total = total + field_buf[node_rows(leaves + p), :]
        down_buf[node_rows(leaves + p), :] = total.astype(jnp.bfloat16)
    for leaf in range(leaves):
        total = dot(up_one_ref[leaf], down_buf[node_rows(leaves + leaf // 2), :])
        total = total + field_buf[node_rows(leaf), :]
        down_buf[node_rows(leaf), :] = total.astype(jnp.bfloat16)
    outs = []
    for leaf in range(leaves):
        here = pl.ds(leaf * LEAF, LEAF)
        total = sum_buf[here, :] + dot_t(basis_ref[leaf], down_buf[node_rows(leaf), :])
        out_buf[here, :] = total.astype(jnp.bfloat16)
        if leaf % 4 == 3:
            some = pl.ds((leaf - 3) * LEAF, 4 * LEAF)
            outs.append(
                pltpu.make_async_copy(
                    out_buf.at[some, :], out_hbm.at[some, :], out_sems.at[leaf // 4]
                )
            )
            outs[-1].start()
    for copy in outs:
        copy.wait()


def body(
    vectors,
    near_blocks,
    near_list,
    basis,
    up_one,
    up_two,
    couple_zero,
    couple_one,
    couple_two,
    far_zero,
    far_one,
    far_two,
):
    leaves, nears = near_list.shape
    columns = vectors.shape[1]
    rank = basis.shape[2]
    fars = far_zero.shape[1]
    size = lax.axis_size("space")
    cores = lax.axis_size("rhs")
    me = lax.axis_index("space").astype(jnp.int32).reshape(1)
    counts = (leaves, leaves // 2, leaves // 4)
    nodes = sum(counts)
    basis_t = jnp.swapaxes(basis, 1, 2)
    bf16, f32 = jnp.bfloat16, jnp.float32

    hbm = pl.BlockSpec(memory_space=pltpu.HBM)
    vmem = pl.BlockSpec(memory_space=pltpu.VMEM)
    smem = pl.BlockSpec(memory_space=pltpu.SMEM)

    def in_hbm(*arrays):
        return [pltpu.with_memory_space_constraint(a, pltpu.HBM) for a in arrays]

    plain, pair = pl.pallas_call(
        up_kernel,
        in_specs=[smem] + [hbm] * 4,
        out_specs=[vmem] * 2,
        out_shape=[
            pltpu.VMEM((nodes * rank, columns), bf16),
            pltpu.VMEM((2 * LEAF + nodes * rank, columns), bf16),
        ],
        scratch_shapes=[
            pltpu.VMEM(vectors.shape, bf16),
            pltpu.VMEM(basis_t.shape, bf16),
            pltpu.VMEM(up_one.shape, bf16),
            pltpu.VMEM(up_two.shape, bf16),
            pltpu.SemaphoreType.DMA((leaves // 2 + 2,)),
        ],
        compiler_params=pltpu.CompilerParams(vmem_limit_bytes=8 * MIB),
        name="up_pass",
    )(me, *in_hbm(vectors, basis_t, up_one, up_two))

    def send(array, to):
        pairs = []
        for i in range(size):
            for c in range(cores):
                j, d = (to(i), c) if 0 <= to(i) < size else (i, cores - 1 - c)
                pairs.append((i * cores + c, j * cores + d))
        return lax.ppermute(array, ("space", "rhs"), pairs)

    def partner(i):
        return i + 1 - 2 * (i % 2)

    from_pair = send(pair, partner)
    turns = (lambda i: i + 2 - i // 2 % 2 * 4, lambda i: i - 2 + i // 2 % 2 * 4)
    first, second = [send(plain, turn) for turn in turns]

    near, edge, points = pl.pallas_call(
        near_kernel,
        in_specs=[smem] + [hbm] * 3,
        out_specs=[vmem] * 3,
        out_shape=[
            pltpu.VMEM(vectors.shape, f32),
            pltpu.VMEM((leaves, 2, LEAF, LEAF), bf16),
            pltpu.VMEM(vectors.shape, bf16),
        ],
        scratch_shapes=[
            pltpu.SMEM(near_list.shape, jnp.int32),
            pltpu.VMEM((DEPTH, nears - 2, LEAF, LEAF), bf16),
            pltpu.SemaphoreType.DMA((DEPTH, 3)),
            pltpu.SemaphoreType.DMA,
            pltpu.SemaphoreType.DMA,
        ],
        compiler_params=pltpu.CompilerParams(vmem_limit_bytes=16 * MIB),
        cost_estimate=pl.CostEstimate(
            flops=2 * leaves * (nears - 2) * LEAF * LEAF * columns,
            bytes_accessed=2 * leaves * nears * LEAF * LEAF + 6 * leaves * LEAF * columns,
            transcendentals=0,
        ),
        name="near_own",
    )(me, *in_hbm(near_list, vectors, near_blocks))

    split = leaves * rank - LEAF
    from_pair, near = lax.optimization_barrier((from_pair, near))
    lows = [send(from_pair[LEAF : 2 * LEAF + split], turn) for turn in turns]
    first, second, near = lax.optimization_barrier((first, second, near))
    upper = jnp.where((me[0] // 2 + me[0]) % 2 == 0, first[split:], second[split:])
    high = send(upper, partner)

    sums, *rest = pl.pallas_call(
        prep_kernel,
        in_specs=[smem] + [vmem] * 6 + [hbm] * 3,
        out_specs=[vmem] * 7,
        out_shape=[
            pltpu.VMEM(vectors.shape, f32),
            *[pltpu.VMEM((SPAN * n * rank, columns), bf16) for n in counts],
            *[pltpu.VMEM((n, rank, fars * rank), bf16) for n in counts],
        ],
        scratch_shapes=[
            *[pltpu.VMEM((n, fars, rank, rank), bf16) for n in counts],
            pltpu.SemaphoreType.DMA((sum(n // 4 for n in counts),)),
            pltpu.SemaphoreType.DMA((12,)),
        ],
        compiler_params=pltpu.CompilerParams(vmem_limit_bytes=16 * MIB),
        cost_estimate=pl.CostEstimate(
            flops=2 * leaves * LEAF * LEAF * columns,
            bytes_accessed=4 * nodes * fars * rank * rank,
            transcendentals=0,
        ),
        name="prep",
    )(me, plain, from_pair, first, second, near, edge, *in_hbm(couple_zero, couple_one, couple_two))
    windows, wides = rest[:3], rest[3:]

    out, *_ = pl.pallas_call(
        functools.partial(far_kernel, size=size),
        in_specs=[smem] * 4 + [vmem] * 15,
        out_specs=[hbm] + [vmem] * 3,
        out_shape=[
            jax.ShapeDtypeStruct(vectors.shape, bf16),
            *[pltpu.VMEM((SPAN * n * rank, columns), bf16) for n in counts],
        ],
        input_output_aliases={16: 1, 17: 2, 18: 3},
        scratch_shapes=[
            pltpu.VMEM(vectors.shape, f32),
            pltpu.VMEM(vectors.shape, bf16),
            pltpu.VMEM((LEAF, columns), bf16),
            pltpu.VMEM((nodes * rank, columns), f32),
            pltpu.VMEM((nodes * rank, columns), bf16),
            pltpu.SemaphoreType.DMA((4,)),
            pltpu.SemaphoreType.DMA((leaves // 4,)),
        ],
        compiler_params=pltpu.CompilerParams(vmem_limit_bytes=16 * MIB),
        name="far_down",
    )(
        me, far_zero, far_one, far_two, points, *lows, high, sums, edge,
        basis_t, up_one, up_two, *wides, *windows,
    )
    return out


def solution(mesh):
    placed = (
        P(("groups", "space"), "rhs"),
        P("space", None, None, None),
        P("space", None),
        P("space", None, None),
        P("space", None, None),
        P("space", None, None),
        P("space", None, None, None),
        P("space", None, None, None),
        P("space", None, None, None),
        P("space", None),
        P("space", None),
        P("space", None),
    )
    return jax.shard_map(
        body, mesh=mesh, in_specs=placed, out_specs=P(("groups", "space"), "rhs"), check_vma=False
    )
```

```python
import functools

import jax
import jax.numpy as jnp
from jax import lax
from jax.experimental import pallas as pl
from jax.experimental.pallas import tpu as pltpu
from jax.sharding import PartitionSpec as P

LEAF = 256
REACH = 2
SPAN = 2 * REACH + 1
DEPTH = 4
MIB = 1024 * 1024


def dot(a, b):
    return jnp.dot(a, b, preferred_element_type=jnp.float32)


def dot_t(a, b):
    return lax.dot_general(a, b, (((0,), (0,)), ((), ())), preferred_element_type=jnp.float32)


def up_kernel(
    me_ref, x_hbm, basis_hbm, up_one_hbm, up_two_hbm, plain_ref, pair_ref,
    x_ref, basis_ref, up_one_ref, up_two_ref, sems,
):
    leaves, rank = basis_ref.shape[:2]
    steps = leaves // 4
    copies = []
    for q in range(steps):
        rows = pl.ds(q * 4 * LEAF, 4 * LEAF)
        some = pl.ds(q * 4, 4)
        copies.append(
            (
                pltpu.make_async_copy(x_hbm.at[rows, :], x_ref.at[rows, :], sems.at[2 * q]),
                pltpu.make_async_copy(basis_hbm.at[some], basis_ref.at[some], sems.at[2 * q + 1]),
            )
        )
    ups = (
        pltpu.make_async_copy(up_one_hbm, up_one_ref, sems.at[2 * steps]),
        pltpu.make_async_copy(up_two_hbm, up_two_ref, sems.at[2 * steps + 1]),
    )
    for pair in (*copies, ups):
        for copy in pair:
            copy.start()

    def put(node, value):
        value = value.astype(jnp.bfloat16)
        plain_ref[pl.ds(node * rank, rank), :] = value
        pair_ref[pl.ds(node * rank, rank), :] = value
        return value

    def join(ups, pair):
        return dot_t(ups.reshape(2 * rank, rank), jnp.concatenate(pair, axis=0))

    zeros = []
    for q in range(steps):
        for copy in copies[q]:
            copy.wait()
        for leaf in range(4 * q, 4 * q + 4):
            coef = dot(basis_ref[leaf], x_ref[pl.ds(leaf * LEAF, LEAF), :])
            zeros.append(put(leaf, coef))
    for copy in ups:
        copy.wait()
    ones = []
    for p in range(leaves // 2):
        pair = slice(2 * p, 2 * p + 2)
        ones.append(put(leaves + p, join(up_one_ref[pair], zeros[pair])))
    for q in range(leaves // 4):
        pair = slice(2 * q, 2 * q + 2)
        put(leaves + leaves // 2 + q, join(up_two_ref[pair], ones[pair]))
    odd = lax.rem(me_ref[0], 2)
    last = (leaves - 1) * LEAF
    end = pl.ds(plain_ref.shape[0] - LEAF, LEAF)
    pair_ref[end, :] = x_ref[pl.ds(pl.multiple_of((1 - odd) * last, LEAF), LEAF), :]
    plain_ref[end, :] = x_ref[pl.ds(pl.multiple_of(odd * last, LEAF), LEAF), :]


def near_kernel(
    me_ref, list_hbm, x_hbm, blocks_hbm, out_ref, edge_ref, x_ref,
    list_ref, block_buf, sems, x_sem, list_sem,
):
    leaves, nears = list_ref.shape
    first = me_ref[0] * leaves

    def copies(leaf, slot):
        pairs = (
            (blocks_hbm.at[leaf, pl.ds(0, 1)], block_buf.at[slot, pl.ds(0, 1)]),
            (blocks_hbm.at[leaf, pl.ds(3, nears - 3)], block_buf.at[slot, pl.ds(1, nears - 3)]),
            (blocks_hbm.at[leaf, pl.ds(1, 2)], edge_ref.at[leaf]),
        )
        return [
            pltpu.make_async_copy(src, dst, sems.at[slot, i]) for i, (src, dst) in enumerate(pairs)
        ]

    list_copy = pltpu.make_async_copy(list_hbm, list_ref, list_sem)
    x_copy = pltpu.make_async_copy(x_hbm, x_ref, x_sem)
    list_copy.start()
    x_copy.start()
    for leaf in range(DEPTH - 1):
        for copy in copies(leaf, leaf):
            copy.start()
    list_copy.wait()
    x_copy.wait()

    def step(leaf, carry):
        slot = lax.rem(leaf, DEPTH)

        @pl.when(leaf + DEPTH - 1 < leaves)
        def _():
            for copy in copies(leaf + DEPTH - 1, lax.rem(leaf + DEPTH - 1, DEPTH)):
                copy.start()

        for copy in copies(leaf, slot):
            copy.wait()
        rows = []
        for k in (0, *range(3, nears)):
            start = pl.multiple_of((list_ref[leaf, k] - first) * LEAF, LEAF)
            rows.append(x_ref[pl.ds(start, LEAF), :])
        blocks = [block_buf[slot, k] for k in range(nears - 2)]
        here = pl.ds(pl.multiple_of(leaf * LEAF, LEAF), LEAF)
        out_ref[here, :] = dot(jnp.concatenate(blocks, axis=1), jnp.concatenate(rows, axis=0))
        return carry

    lax.fori_loop(0, leaves, step, 0)


def add_edge(sum_ref, near_ref, edge_ref, side, rows):
    for leaf in range(edge_ref.shape[0]):
        here = pl.ds(leaf * LEAF, LEAF)
        sum_ref[here, :] = near_ref[here, :] + dot(edge_ref[leaf, side], rows)


def window_copies(plans, sems):
    copies = []
    for ref, start, win, at, size in plans:
        copies.append(
            pltpu.make_async_copy(
                ref.at[pl.ds(start, size), :], win.at[pl.ds(at, size), :], sems.at[len(copies)]
            )
        )
    return copies


def prep_kernel(
    me_ref, own_ref, pair_ref, first_ref, second_ref, near_ref, edge_ref,
    zero_hbm, one_hbm, two_hbm,
    sum_ref, zero_win, one_win, two_win, zero_wide, one_wide, two_wide,
    zero_buf, one_buf, two_buf, sems, win_sems,
):
    levels = (
        (two_hbm, two_buf, two_wide),
        (one_hbm, one_buf, one_wide),
        (zero_hbm, zero_buf, zero_wide),
    )
    chunks = []
    for hbm, buf, wide in levels:
        for first in range(0, buf.shape[0], 4):
            some = pl.ds(first, 4)
            copy = pltpu.make_async_copy(hbm.at[some], buf.at[some], sems.at[len(chunks)])
            copy.start()
            chunks.append((copy, buf, wide, first))
    me = me_ref[0]
    odd = lax.rem(me, 2)
    block = lax.rem(me // 2, 2)
    pieces = (
        (own_ref, 0, REACH),
        (first_ref, 0, (1 - block) * (SPAN - 1)),
        (second_ref, 0, block * (SPAN - 1)),
        (pair_ref, 0, REACH + 1 - 2 * odd),
    )
    plans = []
    for ref, start, place in pieces:
        for win in (zero_win, one_win, two_win):
            size = win.shape[0] // SPAN
            plans.append((ref, start, win, pl.multiple_of(place * size, size), size))
            start += size
    moves = window_copies(plans, win_sems)
    for move in moves:
        move.start()
    add_edge(sum_ref, near_ref, edge_ref, odd, pair_ref[pl.ds(pair_ref.shape[0] - LEAF, LEAF), :])
    for copy, buf, wide, first in chunks:
        copy.wait()
        for node in range(first, first + 4):
            fars = buf.shape[1]
            wide[node] = jnp.concatenate([buf[node, k] for k in range(fars)], axis=1)
    for move in moves:
        move.wait()


def far_kernel(
    me_ref, zero_list, one_list, two_list, x_ref, low_first, low_second, high_ref, near_ref, edge_ref,
    basis_ref, up_one_ref, up_two_ref, zero_wide, one_wide, two_wide, zero_in, one_in, two_in,
    out_hbm, zero_win, one_win, two_win,
    sum_buf, out_buf, field_buf, down_buf, win_sems, out_sems, *, size,
):
    del zero_in, one_in, two_in
    leaves, rank, deep = zero_wide.shape
    ones, twos = leaves // 2, leaves // 4
    fars = deep // rank
    me = me_ref[0]
    odd = lax.rem(me, 2)
    place = REACH - 1 + 2 * odd
    sizes = [n * rank for n in (leaves, ones, twos)]
    at = [pl.multiple_of(place * n, n) for n in sizes]
    moves = window_copies(
        (
            (low_first, 0, zero_win, at[0], sizes[0]),
            (high_ref, 0, one_win, at[1], sizes[1]),
            (high_ref, sizes[1], two_win, at[2], sizes[2]),
        ),
        win_sems,
    )
    other = window_copies(((low_second, 0, zero_win, at[0], sizes[0]),), win_sems)[0]
    from_first = lax.rem(me + me // 2, 2) == 1
    for move in moves[1:]:
        move.start()

    pl.when(from_first)(moves[0].start)
    pl.when(jnp.logical_not(from_first))(other.start)

    alone = (me == 0) | (me == size - 1)

    @pl.when(alone)
    def _():
        for leaf in range(leaves):
            here = pl.ds(leaf * LEAF, LEAF)
            sum_buf[here, :] = near_ref[here, :] + dot(edge_ref[leaf, 1 - odd], x_ref[here, :])

    @pl.when(jnp.logical_not(alone))
    def _():
        rows = high_ref[pl.ds(high_ref.shape[0] - LEAF, LEAF), :]
        add_edge(sum_buf, near_ref, edge_ref, 1 - odd, rows)

    for move in moves:
        move.wait()

    def node_rows(row):
        return pl.ds(row * rank, rank)

    base = leaves + ones
    levels = (
        (two_wide, two_list, two_win, base),
        (one_wide, one_list, one_win, leaves),
        (zero_wide, zero_list, zero_win, 0),
    )
    for wide, where, win, row in levels:
        first = (me - REACH) * wide.shape[0]
        for node in range(wide.shape[0]):
            picked = []
            for k in range(fars):
                start = pl.multiple_of((where[node, k] - first) * rank, rank)
                picked.append(win[pl.ds(start, rank), :])
            field_buf[node_rows(row + node), :] = dot(wide[node], jnp.concatenate(picked, axis=0))
    for q in range(twos):
        down_buf[node_rows(base + q), :] = field_buf[node_rows(base + q), :].astype(jnp.bfloat16)
    for p in range(ones):
        total = dot(up_two_ref[p], down_buf[node_rows(base + p // 2), :])
        total = total + field_buf[node_rows(leaves + p), :]
        down_buf[node_rows(leaves + p), :] = total.astype(jnp.bfloat16)
    for leaf in range(leaves):
        total = dot(up_one_ref[leaf], down_buf[node_rows(leaves + leaf // 2), :])
        total = total + field_buf[node_rows(leaf), :]
        down_buf[node_rows(leaf), :] = total.astype(jnp.bfloat16)
    outs = []
    for leaf in range(leaves):
        here = pl.ds(leaf * LEAF, LEAF)
        total = sum_buf[here, :] + dot_t(basis_ref[leaf], down_buf[node_rows(leaf), :])
        out_buf[here, :] = total.astype(jnp.bfloat16)
        if leaf % 4 == 3:
            some = pl.ds((leaf - 3) * LEAF, 4 * LEAF)
            outs.append(
                pltpu.make_async_copy(
                    out_buf.at[some, :], out_hbm.at[some, :], out_sems.at[leaf // 4]
                )
            )
            outs[-1].start()
    for copy in outs:
        copy.wait()


def body(
    vectors,
    near_blocks,
    near_list,
    basis,
    up_one,
    up_two,
    couple_zero,
    couple_one,
    couple_two,
    far_zero,
    far_one,
    far_two,
):
    leaves, nears = near_list.shape
    columns = vectors.shape[1]
    rank = basis.shape[2]
    fars = far_zero.shape[1]
    size = lax.axis_size("space")
    cores = lax.axis_size("rhs")
    me = lax.axis_index("space").astype(jnp.int32).reshape(1)
    counts = (leaves, leaves // 2, leaves // 4)
    nodes = sum(counts)
    basis_t = jnp.swapaxes(basis, 1, 2)
    bf16, f32 = jnp.bfloat16, jnp.float32

    hbm = pl.BlockSpec(memory_space=pltpu.HBM)
    vmem = pl.BlockSpec(memory_space=pltpu.VMEM)
    smem = pl.BlockSpec(memory_space=pltpu.SMEM)

    def in_hbm(*arrays):
        return [pltpu.with_memory_space_constraint(a, pltpu.HBM) for a in arrays]

    plain, pair = pl.pallas_call(
        up_kernel,
        in_specs=[smem] + [hbm] * 4,
        out_specs=[vmem] * 2,
        out_shape=[
            pltpu.VMEM((nodes * rank + LEAF, columns), bf16),
            pltpu.VMEM((nodes * rank + LEAF, columns), bf16),
        ],
        scratch_shapes=[
            pltpu.VMEM(vectors.shape, bf16),
            pltpu.VMEM(basis_t.shape, bf16),
            pltpu.VMEM(up_one.shape, bf16),
            pltpu.VMEM(up_two.shape, bf16),
            pltpu.SemaphoreType.DMA((leaves // 2 + 2,)),
        ],
        compiler_params=pltpu.CompilerParams(vmem_limit_bytes=8 * MIB),
        name="up_pass",
    )(me, *in_hbm(vectors, basis_t, up_one, up_two))

    def send(array, to):
        pairs = []
        for i in range(size):
            for c in range(cores):
                j, d = (to(i), c) if 0 <= to(i) < size else (i, cores - 1 - c)
                pairs.append((i * cores + c, j * cores + d))
        return lax.ppermute(array, ("space", "rhs"), pairs)

    def partner(i):
        return i + 1 - 2 * (i % 2)

    from_pair = send(pair, partner)
    turns = (lambda i: i + 2 - i // 2 % 2 * 4, lambda i: i - 2 + i // 2 % 2 * 4)
    first, second = [send(plain, turn) for turn in turns]

    near, edge, points = pl.pallas_call(
        near_kernel,
        in_specs=[smem] + [hbm] * 3,
        out_specs=[vmem] * 3,
        out_shape=[
            pltpu.VMEM(vectors.shape, f32),
            pltpu.VMEM((leaves, 2, LEAF, LEAF), bf16),
            pltpu.VMEM(vectors.shape, bf16),
        ],
        scratch_shapes=[
            pltpu.SMEM(near_list.shape, jnp.int32),
            pltpu.VMEM((DEPTH, nears - 2, LEAF, LEAF), bf16),
            pltpu.SemaphoreType.DMA((DEPTH, 3)),
            pltpu.SemaphoreType.DMA,
            pltpu.SemaphoreType.DMA,
        ],
        compiler_params=pltpu.CompilerParams(vmem_limit_bytes=16 * MIB),
        cost_estimate=pl.CostEstimate(
            flops=2 * leaves * (nears - 2) * LEAF * LEAF * columns,
            bytes_accessed=2 * leaves * nears * LEAF * LEAF + 6 * leaves * LEAF * columns,
            transcendentals=0,
        ),
        name="near_own",
    )(me, *in_hbm(near_list, vectors, near_blocks))

    split = leaves * rank
    from_pair, near = lax.optimization_barrier((from_pair, near))
    lows = [send(from_pair[:split], turn) for turn in turns]
    first, second, near = lax.optimization_barrier((first, second, near))
    upper = jnp.where((me[0] // 2 + me[0]) % 2 == 0, first[split:], second[split:])
    high = send(upper, partner)

    sums, *rest = pl.pallas_call(
        prep_kernel,
        in_specs=[smem] + [vmem] * 6 + [hbm] * 3,
        out_specs=[vmem] * 7,
        out_shape=[
            pltpu.VMEM(vectors.shape, f32),
            *[pltpu.VMEM((SPAN * n * rank, columns), bf16) for n in counts],
            *[pltpu.VMEM((n, rank, fars * rank), bf16) for n in counts],
        ],
        scratch_shapes=[
            *[pltpu.VMEM((n, fars, rank, rank), bf16) for n in counts],
            pltpu.SemaphoreType.DMA((sum(n // 4 for n in counts),)),
            pltpu.SemaphoreType.DMA((12,)),
        ],
        compiler_params=pltpu.CompilerParams(vmem_limit_bytes=16 * MIB),
        cost_estimate=pl.CostEstimate(
            flops=4 * 10**9,
            bytes_accessed=4 * nodes * fars * rank * rank,
            transcendentals=0,
        ),
        name="prep",
    )(me, plain, from_pair, first, second, near, edge, *in_hbm(couple_zero, couple_one, couple_two))
    windows, wides = rest[:3], rest[3:]

    out, *_ = pl.pallas_call(
        functools.partial(far_kernel, size=size),
        in_specs=[smem] * 4 + [vmem] * 15,
        out_specs=[hbm] + [vmem] * 3,
        out_shape=[
            jax.ShapeDtypeStruct(vectors.shape, bf16),
            *[pltpu.VMEM((SPAN * n * rank, columns), bf16) for n in counts],
        ],
        input_output_aliases={16: 1, 17: 2, 18: 3},
        scratch_shapes=[
            pltpu.VMEM(vectors.shape, f32),
            pltpu.VMEM(vectors.shape, bf16),
            pltpu.VMEM((nodes * rank, columns), f32),
            pltpu.VMEM((nodes * rank, columns), bf16),
            pltpu.SemaphoreType.DMA((3,)),
            pltpu.SemaphoreType.DMA((leaves // 4,)),
        ],
        compiler_params=pltpu.CompilerParams(vmem_limit_bytes=16 * MIB),
        name="far_down",
    )(
        me, far_zero, far_one, far_two, points, *lows, high, sums, edge,
        basis_t, up_one, up_two, *wides, *windows,
    )
    return out


def solution(mesh):
    placed = (
        P(("groups", "space"), "rhs"),
        P("space", None, None, None),
        P("space", None),
        P("space", None, None),
        P("space", None, None),
        P("space", None, None),
        P("space", None, None, None),
        P("space", None, None, None),
        P("space", None, None, None),
        P("space", None),
        P("space", None),
        P("space", None),
    )
    return jax.shard_map(
        body, mesh=mesh, in_specs=placed, out_specs=P(("groups", "space"), "rhs"), check_vma=False
    )
```

```python
import functools

import jax
import jax.numpy as jnp
from jax import lax
from jax.experimental import pallas as pl
from jax.experimental.pallas import tpu as pltpu
from jax.sharding import PartitionSpec as P

LEAF = 256
REACH = 2
SPAN = 2 * REACH + 1
DEPTH = 4
MIB = 1024 * 1024


def dot(a, b):
    return jnp.dot(a, b, preferred_element_type=jnp.float32)


def dot_t(a, b):
    return lax.dot_general(a, b, (((0,), (0,)), ((), ())), preferred_element_type=jnp.float32)


def up_kernel(
    me_ref, x_hbm, basis_hbm, up_one_hbm, up_two_hbm, plain_ref, pair_ref,
    x_ref, basis_ref, up_one_ref, up_two_ref, sems,
):
    leaves, rank = basis_ref.shape[:2]
    steps = leaves // 4
    copies = []
    for q in range(steps):
        rows = pl.ds(q * 4 * LEAF, 4 * LEAF)
        some = pl.ds(q * 4, 4)
        copies.append(
            (
                pltpu.make_async_copy(x_hbm.at[rows, :], x_ref.at[rows, :], sems.at[2 * q]),
                pltpu.make_async_copy(basis_hbm.at[some], basis_ref.at[some], sems.at[2 * q + 1]),
            )
        )
    ups = (
        pltpu.make_async_copy(up_one_hbm, up_one_ref, sems.at[2 * steps]),
        pltpu.make_async_copy(up_two_hbm, up_two_ref, sems.at[2 * steps + 1]),
    )
    for pair in (*copies, ups):
        for copy in pair:
            copy.start()

    def put(node, value):
        value = value.astype(jnp.bfloat16)
        plain_ref[pl.ds(node * rank, rank), :] = value
        pair_ref[pl.ds(node * rank, rank), :] = value
        return value

    def join(ups, pair):
        return dot_t(ups.reshape(2 * rank, rank), jnp.concatenate(pair, axis=0))

    zeros = []
    for q in range(steps):
        for copy in copies[q]:
            copy.wait()
        for leaf in range(4 * q, 4 * q + 4):
            coef = dot(basis_ref[leaf], x_ref[pl.ds(leaf * LEAF, LEAF), :])
            zeros.append(put(leaf, coef))
    for copy in ups:
        copy.wait()
    ones = []
    for p in range(leaves // 2):
        pair = slice(2 * p, 2 * p + 2)
        ones.append(put(leaves + p, join(up_one_ref[pair], zeros[pair])))
    for q in range(leaves // 4):
        pair = slice(2 * q, 2 * q + 2)
        put(leaves + leaves // 2 + q, join(up_two_ref[pair], ones[pair]))
    odd = lax.rem(me_ref[0], 2)
    last = (leaves - 1) * LEAF
    end = pl.ds(plain_ref.shape[0] - LEAF, LEAF)
    pair_ref[end, :] = x_ref[pl.ds(pl.multiple_of((1 - odd) * last, LEAF), LEAF), :]
    plain_ref[end, :] = x_ref[pl.ds(pl.multiple_of(odd * last, LEAF), LEAF), :]


def near_kernel(
    me_ref, list_hbm, x_hbm, blocks_hbm, out_ref, x_ref, list_ref, block_buf, sems, x_sems, list_sem,
):
    leaves, nears = list_ref.shape
    first = me_ref[0] * leaves

    def copies(leaf, slot):
        pairs = (
            (blocks_hbm.at[leaf, pl.ds(0, 1)], block_buf.at[slot, pl.ds(0, 1)]),
            (blocks_hbm.at[leaf, pl.ds(3, nears - 3)], block_buf.at[slot, pl.ds(1, nears - 3)]),
        )
        return [
            pltpu.make_async_copy(src, dst, sems.at[slot, i]) for i, (src, dst) in enumerate(pairs)
        ]

    list_copy = pltpu.make_async_copy(list_hbm, list_ref, list_sem)
    list_copy.start()
    x_copies = []
    for q in range(leaves // 4):
        rows = pl.ds(q * 4 * LEAF, 4 * LEAF)
        x_copies.append(
            pltpu.make_async_copy(x_hbm.at[rows, :], x_ref.at[rows, :], x_sems.at[q])
        )
    for copy in x_copies:
        copy.start()
    for leaf in range(DEPTH - 1):
        for copy in copies(leaf, leaf):
            copy.start()
    list_copy.wait()
    for copy in x_copies:
        copy.wait()

    def step(leaf, carry):
        slot = lax.rem(leaf, DEPTH)

        @pl.when(leaf + DEPTH - 1 < leaves)
        def _():
            for copy in copies(leaf + DEPTH - 1, lax.rem(leaf + DEPTH - 1, DEPTH)):
                copy.start()

        for copy in copies(leaf, slot):
            copy.wait()
        rows = []
        for k in (0, *range(3, nears)):
            start = pl.multiple_of((list_ref[leaf, k] - first) * LEAF, LEAF)
            rows.append(x_ref[pl.ds(start, LEAF), :])
        blocks = [block_buf[slot, k] for k in range(nears - 2)]
        here = pl.ds(pl.multiple_of(leaf * LEAF, LEAF), LEAF)
        out_ref[here, :] = dot(jnp.concatenate(blocks, axis=1), jnp.concatenate(rows, axis=0))
        return carry

    lax.fori_loop(0, leaves, step, 0)


def add_edge(sum_ref, near_ref, edge_ref, side, rows):
    for leaf in range(edge_ref.shape[0]):
        here = pl.ds(leaf * LEAF, LEAF)
        sum_ref[here, :] = near_ref[here, :] + dot(edge_ref[leaf, side], rows)


def window_copies(plans, sems):
    copies = []
    for ref, start, win, at, size in plans:
        copies.append(
            pltpu.make_async_copy(
                ref.at[pl.ds(start, size), :], win.at[pl.ds(at, size), :], sems.at[len(copies)]
            )
        )
    return copies


def prep_kernel(
    me_ref, own_ref, pair_ref, first_ref, second_ref, near_ref,
    blocks_hbm, zero_hbm, one_hbm, two_hbm,
    sum_ref, edge_ref, zero_win, one_win, two_win, zero_wide, one_wide, two_wide,
    zero_buf, one_buf, two_buf, sems, win_sems, edge_sems,
):
    levels = (
        (two_hbm, two_buf, two_wide),
        (one_hbm, one_buf, one_wide),
        (zero_hbm, zero_buf, zero_wide),
    )
    chunks = []
    for hbm, buf, wide in levels:
        for first in range(0, buf.shape[0], 4):
            some = pl.ds(first, 4)
            copy = pltpu.make_async_copy(hbm.at[some], buf.at[some], sems.at[len(chunks)])
            copy.start()
            chunks.append((copy, buf, wide, first))
    edges = []
    for q in range(edge_ref.shape[0] // 4):
        some = pl.ds(4 * q, 4)
        src = blocks_hbm.at[some, pl.ds(1, 2)]
        edges.append(pltpu.make_async_copy(src, edge_ref.at[some], edge_sems.at[q]))
        edges[-1].start()
    me = me_ref[0]
    odd = lax.rem(me, 2)
    block = lax.rem(me // 2, 2)
    pieces = (
        (own_ref, 0, REACH),
        (first_ref, 0, (1 - block) * (SPAN - 1)),
        (second_ref, 0, block * (SPAN - 1)),
        (pair_ref, 0, REACH + 1 - 2 * odd),
    )
    plans = []
    for ref, start, place in pieces:
        for win in (zero_win, one_win, two_win):
            size = win.shape[0] // SPAN
            plans.append((ref, start, win, pl.multiple_of(place * size, size), size))
            start += size
    moves = window_copies(plans, win_sems)
    for move in moves:
        move.start()
    for copy, buf, wide, first in chunks:
        copy.wait()
        for node in range(first, first + 4):
            fars = buf.shape[1]
            wide[node] = jnp.concatenate([buf[node, k] for k in range(fars)], axis=1)
    for copy in edges:
        copy.wait()
    add_edge(sum_ref, near_ref, edge_ref, odd, pair_ref[pl.ds(pair_ref.shape[0] - LEAF, LEAF), :])
    for move in moves:
        move.wait()


def far_kernel(
    me_ref, zero_list, one_list, two_list, x_ref, got_first, got_second, near_ref, edge_ref,
    basis_ref, up_one_ref, up_two_ref, zero_wide, one_wide, two_wide, zero_in, one_in, two_in,
    out_hbm, zero_win, one_win, two_win,
    sum_buf, out_buf, rows_buf, field_buf, down_buf, win_sems, out_sems, *, size,
):
    del zero_in, one_in, two_in
    leaves, rank, deep = zero_wide.shape
    ones, twos = leaves // 2, leaves // 4
    fars = deep // rank
    me = me_ref[0]
    odd = lax.rem(me, 2)
    place = REACH - 1 + 2 * odd
    sizes = [n * rank for n in (leaves, ones, twos)]
    at = [pl.multiple_of(place * n, n) for n in sizes]

    def arrivals(low_ref, high_ref):
        plans = (
            (low_ref, 0, zero_win, at[0], sizes[0]),
            (high_ref, 0, one_win, at[1], sizes[1]),
            (high_ref, sizes[1], two_win, at[2], sizes[2]),
        )
        return window_copies(plans, win_sems)

    moves = arrivals(got_first, got_second)
    other = arrivals(got_second, got_first)
    end = pl.ds(got_first.shape[0] - LEAF, LEAF)
    low_first = lax.rem(me + me // 2, 2) == 1

    @pl.when(low_first)
    def _():
        for move in moves:
            move.start()
        rows_buf[...] = got_second[end, :]

    @pl.when(jnp.logical_not(low_first))
    def _():
        for move in other:
            move.start()
        rows_buf[...] = got_first[end, :]

    alone = (me == 0) | (me == size - 1)

    @pl.when(alone)
    def _():
        for leaf in range(leaves):
            here = pl.ds(leaf * LEAF, LEAF)
            sum_buf[here, :] = near_ref[here, :] + dot(edge_ref[leaf, 1 - odd], x_ref[here, :])

    @pl.when(jnp.logical_not(alone))
    def _():
        add_edge(sum_buf, near_ref, edge_ref, 1 - odd, rows_buf[...])

    for move in moves:
        move.wait()

    def node_rows(row):
        return pl.ds(row * rank, rank)

    base = leaves + ones
    levels = (
        (two_wide, two_list, two_win, base),
        (one_wide, one_list, one_win, leaves),
        (zero_wide, zero_list, zero_win, 0),
    )
    for wide, where, win, row in levels:
        first = (me - REACH) * wide.shape[0]
        for node in range(wide.shape[0]):
            picked = []
            for k in range(fars):
                start = pl.multiple_of((where[node, k] - first) * rank, rank)
                picked.append(win[pl.ds(start, rank), :])
            field_buf[node_rows(row + node), :] = dot(wide[node], jnp.concatenate(picked, axis=0))
    for q in range(twos):
        down_buf[node_rows(base + q), :] = field_buf[node_rows(base + q), :].astype(jnp.bfloat16)
    for p in range(ones):
        total = dot(up_two_ref[p], down_buf[node_rows(base + p // 2), :])
        total = total + field_buf[node_rows(leaves + p), :]
        down_buf[node_rows(leaves + p), :] = total.astype(jnp.bfloat16)
    for leaf in range(leaves):
        total = dot(up_one_ref[leaf], down_buf[node_rows(leaves + leaf // 2), :])
        total = total + field_buf[node_rows(leaf), :]
        down_buf[node_rows(leaf), :] = total.astype(jnp.bfloat16)
    outs = []
    for leaf in range(leaves):
        here = pl.ds(leaf * LEAF, LEAF)
        total = sum_buf[here, :] + dot_t(basis_ref[leaf], down_buf[node_rows(leaf), :])
        out_buf[here, :] = total.astype(jnp.bfloat16)
        if leaf % 4 == 3:
            some = pl.ds((leaf - 3) * LEAF, 4 * LEAF)
            outs.append(
                pltpu.make_async_copy(
                    out_buf.at[some, :], out_hbm.at[some, :], out_sems.at[leaf // 4]
                )
            )
            outs[-1].start()
    for copy in outs:
        copy.wait()


def body(
    vectors,
    near_blocks,
    near_list,
    basis,
    up_one,
    up_two,
    couple_zero,
    couple_one,
    couple_two,
    far_zero,
    far_one,
    far_two,
):
    leaves, nears = near_list.shape
    columns = vectors.shape[1]
    rank = basis.shape[2]
    fars = far_zero.shape[1]
    size = lax.axis_size("space")
    cores = lax.axis_size("rhs")
    me = lax.axis_index("space").astype(jnp.int32).reshape(1)
    counts = (leaves, leaves // 2, leaves // 4)
    nodes = sum(counts)
    basis_t = jnp.swapaxes(basis, 1, 2)
    bf16, f32 = jnp.bfloat16, jnp.float32

    hbm = pl.BlockSpec(memory_space=pltpu.HBM)
    vmem = pl.BlockSpec(memory_space=pltpu.VMEM)
    smem = pl.BlockSpec(memory_space=pltpu.SMEM)

    def in_hbm(*arrays):
        return [pltpu.with_memory_space_constraint(a, pltpu.HBM) for a in arrays]

    plain, pair = pl.pallas_call(
        up_kernel,
        in_specs=[smem] + [hbm] * 4,
        out_specs=[vmem] * 2,
        out_shape=[
            pltpu.VMEM((nodes * rank + LEAF, columns), bf16),
            pltpu.VMEM((nodes * rank + LEAF, columns), bf16),
        ],
        scratch_shapes=[
            pltpu.VMEM(vectors.shape, bf16),
            pltpu.VMEM(basis_t.shape, bf16),
            pltpu.VMEM(up_one.shape, bf16),
            pltpu.VMEM(up_two.shape, bf16),
            pltpu.SemaphoreType.DMA((leaves // 2 + 2,)),
        ],
        compiler_params=pltpu.CompilerParams(vmem_limit_bytes=8 * MIB),
        name="up_pass",
    )(me, *in_hbm(vectors, basis_t, up_one, up_two))

    def send(array, to):
        pairs = []
        for i in range(size):
            for c in range(cores):
                j, d = (to(i), c) if 0 <= to(i) < size else (i, cores - 1 - c)
                pairs.append((i * cores + c, j * cores + d))
        return lax.ppermute(array, ("space", "rhs"), pairs)

    def partner(i):
        return i + 1 - 2 * (i % 2)

    from_pair = send(pair, partner)
    turns = (lambda i: i + 2 - i // 2 % 2 * 4, lambda i: i - 2 + i // 2 % 2 * 4)
    first, second = [send(plain, turn) for turn in turns]

    near, points = pl.pallas_call(
        near_kernel,
        in_specs=[smem] + [hbm] * 3,
        out_specs=[vmem] * 2,
        out_shape=[pltpu.VMEM(vectors.shape, f32), pltpu.VMEM(vectors.shape, bf16)],
        scratch_shapes=[
            pltpu.SMEM(near_list.shape, jnp.int32),
            pltpu.VMEM((DEPTH, nears - 2, LEAF, LEAF), bf16),
            pltpu.SemaphoreType.DMA((DEPTH, 2)),
            pltpu.SemaphoreType.DMA((leaves // 4,)),
            pltpu.SemaphoreType.DMA,
        ],
        compiler_params=pltpu.CompilerParams(vmem_limit_bytes=16 * MIB),
        cost_estimate=pl.CostEstimate(
            flops=2 * leaves * (nears - 2) * LEAF * LEAF * columns,
            bytes_accessed=2 * leaves * nears * LEAF * LEAF + 6 * leaves * LEAF * columns,
            transcendentals=0,
        ),
        name="near_own",
    )(me, *in_hbm(near_list, vectors, near_blocks))

    def cycle(lower):
        def to(i):
            along = i + 2 - i % 2 * 4 if (i // 2 + i) % 2 == lower else partner(i)
            return along if 0 <= along < size else partner(i)

        return to

    split = leaves * rank
    from_pair, first, second, near = lax.optimization_barrier((from_pair, first, second, near))
    even = (me[0] // 2 + me[0]) % 2 == 0
    got_first = send(jnp.where(even, from_pair[:split], second[split:]), cycle(0))
    got_second = send(jnp.where(even, first[split:], from_pair[:split]), cycle(1))

    sums, edge, *rest = pl.pallas_call(
        prep_kernel,
        in_specs=[smem] + [vmem] * 5 + [hbm] * 4,
        out_specs=[vmem] * 8,
        out_shape=[
            pltpu.VMEM(vectors.shape, f32),
            pltpu.VMEM((leaves, 2, LEAF, LEAF), bf16),
            *[pltpu.VMEM((SPAN * n * rank, columns), bf16) for n in counts],
            *[pltpu.VMEM((n, rank, fars * rank), bf16) for n in counts],
        ],
        scratch_shapes=[
            *[pltpu.VMEM((n, fars, rank, rank), bf16) for n in counts],
            pltpu.SemaphoreType.DMA((sum(n // 4 for n in counts),)),
            pltpu.SemaphoreType.DMA((12,)),
            pltpu.SemaphoreType.DMA((leaves // 4,)),
        ],
        compiler_params=pltpu.CompilerParams(vmem_limit_bytes=16 * MIB),
        cost_estimate=pl.CostEstimate(
            flops=2 * leaves * LEAF * LEAF * columns,
            bytes_accessed=4 * nodes * fars * rank * rank + 4 * leaves * LEAF * LEAF,
            transcendentals=0,
        ),
        name="prep",
    )(
        me, plain, from_pair, first, second, near,
        *in_hbm(near_blocks, couple_zero, couple_one, couple_two),
    )
    windows, wides = rest[:3], rest[3:]

    out, *_ = pl.pallas_call(
        functools.partial(far_kernel, size=size),
        in_specs=[smem] * 4 + [vmem] * 14,
        out_specs=[hbm] + [vmem] * 3,
        out_shape=[
            jax.ShapeDtypeStruct(vectors.shape, bf16),
            *[pltpu.VMEM((SPAN * n * rank, columns), bf16) for n in counts],
        ],
        input_output_aliases={15: 1, 16: 2, 17: 3},
        scratch_shapes=[
            pltpu.VMEM(vectors.shape, f32),
            pltpu.VMEM(vectors.shape, bf16),
            pltpu.VMEM((LEAF, columns), bf16),
            pltpu.VMEM((nodes * rank, columns), f32),
            pltpu.VMEM((nodes * rank, columns), bf16),
            pltpu.SemaphoreType.DMA((3,)),
            pltpu.SemaphoreType.DMA((leaves // 4,)),
        ],
        compiler_params=pltpu.CompilerParams(vmem_limit_bytes=16 * MIB),
        name="far_down",
    )(
        me, far_zero, far_one, far_two, points, got_first, got_second, sums, edge,
        basis_t, up_one, up_two, *wides, *windows,
    )
    return out


def solution(mesh):
    placed = (
        P(("groups", "space"), "rhs"),
        P("space", None, None, None),
        P("space", None),
        P("space", None, None),
        P("space", None, None),
        P("space", None, None),
        P("space", None, None, None),
        P("space", None, None, None),
        P("space", None, None, None),
        P("space", None),
        P("space", None),
        P("space", None),
    )
    return jax.shard_map(
        body, mesh=mesh, in_specs=placed, out_specs=P(("groups", "space"), "rhs"), check_vma=False
    )
```

```python
import functools

import jax
import jax.numpy as jnp
from jax import lax
from jax.experimental import pallas as pl
from jax.experimental.pallas import tpu as pltpu
from jax.sharding import PartitionSpec as P

LEAF = 256
REACH = 2
SPAN = 2 * REACH + 1
DEPTH = 4
MIB = 1024 * 1024


def dot(a, b):
    return jnp.dot(a, b, preferred_element_type=jnp.float32)


def dot_t(a, b):
    return lax.dot_general(a, b, (((0,), (0,)), ((), ())), preferred_element_type=jnp.float32)


def up_kernel(
    me_ref, x_hbm, basis_hbm, up_one_hbm, up_two_hbm, plain_ref, pair_ref,
    x_ref, basis_ref, up_one_ref, up_two_ref, sems,
):
    leaves, rank = basis_ref.shape[:2]
    steps = leaves // 4
    copies = []
    for q in range(steps):
        rows = pl.ds(q * 4 * LEAF, 4 * LEAF)
        some = pl.ds(q * 4, 4)
        copies.append(
            (
                pltpu.make_async_copy(x_hbm.at[rows, :], x_ref.at[rows, :], sems.at[2 * q]),
                pltpu.make_async_copy(basis_hbm.at[some], basis_ref.at[some], sems.at[2 * q + 1]),
            )
        )
    ups = (
        pltpu.make_async_copy(up_one_hbm, up_one_ref, sems.at[2 * steps]),
        pltpu.make_async_copy(up_two_hbm, up_two_ref, sems.at[2 * steps + 1]),
    )
    for pair in (*copies, ups):
        for copy in pair:
            copy.start()

    def put(node, value):
        value = value.astype(jnp.bfloat16)
        plain_ref[pl.ds(node * rank, rank), :] = value
        pair_ref[pl.ds(node * rank, rank), :] = value
        return value

    def join(ups, pair):
        return dot_t(ups.reshape(2 * rank, rank), jnp.concatenate(pair, axis=0))

    zeros = []
    for q in range(steps):
        for copy in copies[q]:
            copy.wait()
        for leaf in range(4 * q, 4 * q + 4):
            coef = dot(basis_ref[leaf], x_ref[pl.ds(leaf * LEAF, LEAF), :])
            zeros.append(put(leaf, coef))
    for copy in ups:
        copy.wait()
    ones = []
    for p in range(leaves // 2):
        pair = slice(2 * p, 2 * p + 2)
        ones.append(put(leaves + p, join(up_one_ref[pair], zeros[pair])))
    for q in range(leaves // 4):
        pair = slice(2 * q, 2 * q + 2)
        put(leaves + leaves // 2 + q, join(up_two_ref[pair], ones[pair]))
    odd = lax.rem(me_ref[0], 2)
    last = (leaves - 1) * LEAF
    end = pl.ds(plain_ref.shape[0] - LEAF, LEAF)
    pair_ref[end, :] = x_ref[pl.ds(pl.multiple_of((1 - odd) * last, LEAF), LEAF), :]
    plain_ref[end, :] = x_ref[pl.ds(pl.multiple_of(odd * last, LEAF), LEAF), :]


def near_kernel(
    me_ref, list_hbm, x_hbm, blocks_hbm, out_ref, x_ref, list_ref, block_buf, sems, x_sems, list_sem,
):
    leaves, nears = list_ref.shape
    first = me_ref[0] * leaves

    def copies(leaf, slot):
        pairs = (
            (blocks_hbm.at[leaf, pl.ds(0, 1)], block_buf.at[slot, pl.ds(0, 1)]),
            (blocks_hbm.at[leaf, pl.ds(3, nears - 3)], block_buf.at[slot, pl.ds(1, nears - 3)]),
        )
        return [
            pltpu.make_async_copy(src, dst, sems.at[slot, i]) for i, (src, dst) in enumerate(pairs)
        ]

    list_copy = pltpu.make_async_copy(list_hbm, list_ref, list_sem)
    list_copy.start()
    x_copies = []
    for q in range(leaves // 4):
        rows = pl.ds(q * 4 * LEAF, 4 * LEAF)
        x_copies.append(
            pltpu.make_async_copy(x_hbm.at[rows, :], x_ref.at[rows, :], x_sems.at[q])
        )
    for copy in x_copies:
        copy.start()
    for leaf in range(DEPTH - 1):
        for copy in copies(leaf, leaf):
            copy.start()
    list_copy.wait()
    for copy in x_copies:
        copy.wait()

    def step(leaf, carry):
        slot = lax.rem(leaf, DEPTH)

        @pl.when(leaf + DEPTH - 1 < leaves)
        def _():
            for copy in copies(leaf + DEPTH - 1, lax.rem(leaf + DEPTH - 1, DEPTH)):
                copy.start()

        for copy in copies(leaf, slot):
            copy.wait()
        rows = []
        for k in (0, *range(3, nears)):
            start = pl.multiple_of((list_ref[leaf, k] - first) * LEAF, LEAF)
            rows.append(x_ref[pl.ds(start, LEAF), :])
        blocks = [block_buf[slot, k] for k in range(nears - 2)]
        here = pl.ds(pl.multiple_of(leaf * LEAF, LEAF), LEAF)
        out_ref[here, :] = dot(jnp.concatenate(blocks, axis=1), jnp.concatenate(rows, axis=0))
        return carry

    lax.fori_loop(0, leaves, step, 0)


def add_edge(sum_ref, near_ref, edge_ref, side, rows):
    for leaf in range(edge_ref.shape[0]):
        here = pl.ds(leaf * LEAF, LEAF)
        sum_ref[here, :] = near_ref[here, :] + dot(edge_ref[leaf, side], rows)


def window_copies(plans, sems):
    copies = []
    for ref, start, win, at, size in plans:
        copies.append(
            pltpu.make_async_copy(
                ref.at[pl.ds(start, size), :], win.at[pl.ds(at, size), :], sems.at[len(copies)]
            )
        )
    return copies


def prep_kernel(
    me_ref, own_ref, pair_ref, first_ref, second_ref, near_ref,
    blocks_hbm, zero_hbm, one_hbm, two_hbm,
    sum_ref, edge_ref, zero_win, one_win, two_win, zero_wide, one_wide, two_wide,
    zero_buf, one_buf, two_buf, sems, win_sems, edge_sems,
):
    levels = (
        (two_hbm, two_buf, two_wide),
        (one_hbm, one_buf, one_wide),
        (zero_hbm, zero_buf, zero_wide),
    )
    chunks = []
    for hbm, buf, wide in levels:
        for first in range(0, buf.shape[0], 4):
            some = pl.ds(first, 4)
            copy = pltpu.make_async_copy(hbm.at[some], buf.at[some], sems.at[len(chunks)])
            copy.start()
            chunks.append((copy, buf, wide, first))
    edges = []
    for q in range(edge_ref.shape[0] // 4):
        some = pl.ds(4 * q, 4)
        src = blocks_hbm.at[some, pl.ds(1, 2)]
        edges.append(pltpu.make_async_copy(src, edge_ref.at[some], edge_sems.at[q]))
        edges[-1].start()
    me = me_ref[0]
    odd = lax.rem(me, 2)
    block = lax.rem(me // 2, 2)
    pieces = (
        (own_ref, 0, REACH),
        (first_ref, 0, (1 - block) * (SPAN - 1)),
        (second_ref, 0, block * (SPAN - 1)),
        (pair_ref, 0, REACH + 1 - 2 * odd),
    )
    plans = []
    for ref, start, place in pieces:
        for win in (zero_win, one_win, two_win):
            size = win.shape[0] // SPAN
            plans.append((ref, start, win, pl.multiple_of(place * size, size), size))
            start += size
    moves = window_copies(plans, win_sems)
    for move in moves:
        move.start()
    for copy, buf, wide, first in chunks:
        copy.wait()
        for node in range(first, first + 4):
            fars = buf.shape[1]
            wide[node] = jnp.concatenate([buf[node, k] for k in range(fars)], axis=1)
    for copy in edges:
        copy.wait()
    add_edge(sum_ref, near_ref, edge_ref, odd, pair_ref[pl.ds(pair_ref.shape[0] - LEAF, LEAF), :])
    for move in moves:
        move.wait()


def far_kernel(
    me_ref, zero_list, one_list, two_list, x_ref, got_first, got_second, got_third, near_ref,
    edge_ref, basis_ref, up_one_ref, up_two_ref, zero_wide, one_wide, two_wide, zero_in, one_in, two_in,
    out_hbm, zero_win, one_win, two_win,
    sum_buf, out_buf, rows_buf, field_buf, down_buf, win_sems, out_sems, *, size,
):
    del zero_in, one_in, two_in
    leaves, rank, deep = zero_wide.shape
    ones, twos = leaves // 2, leaves // 4
    fars = deep // rank
    me = me_ref[0]
    odd = lax.rem(me, 2)
    place = REACH - 1 + 2 * odd
    sizes = [n * rank for n in (leaves, ones, twos)]
    at = [pl.multiple_of(place * n, n) for n in sizes]

    def arrivals(low_ref, high_ref):
        plans = (
            (low_ref, 0, zero_win, at[0], sizes[0]),
            (high_ref, 0, one_win, at[1], sizes[1]),
            (high_ref, sizes[1], two_win, at[2], sizes[2]),
        )
        return window_copies(plans, win_sems)

    end = pl.ds(got_first.shape[0] - LEAF, LEAF)
    low_first = lax.rem(me + me // 2, 2) == 1
    at_end = (me < 2) | (me >= size - 2)

    def take(low_ref, high_ref):
        def _():
            for move in arrivals(low_ref, high_ref):
                move.start()
            rows_buf[...] = high_ref[end, :]

        return _

    pl.when(low_first & at_end)(take(got_first, got_second))
    pl.when(low_first & jnp.logical_not(at_end))(take(got_first, got_third))
    pl.when(jnp.logical_not(low_first))(take(got_second, got_third))
    moves = arrivals(got_first, got_second)

    alone = (me == 0) | (me == size - 1)

    @pl.when(alone)
    def _():
        for leaf in range(leaves):
            here = pl.ds(leaf * LEAF, LEAF)
            sum_buf[here, :] = near_ref[here, :] + dot(edge_ref[leaf, 1 - odd], x_ref[here, :])

    @pl.when(jnp.logical_not(alone))
    def _():
        add_edge(sum_buf, near_ref, edge_ref, 1 - odd, rows_buf[...])

    for move in moves:
        move.wait()

    def node_rows(row):
        return pl.ds(row * rank, rank)

    base = leaves + ones
    levels = (
        (two_wide, two_list, two_win, base),
        (one_wide, one_list, one_win, leaves),
        (zero_wide, zero_list, zero_win, 0),
    )
    for wide, where, win, row in levels:
        first = (me - REACH) * wide.shape[0]
        for node in range(wide.shape[0]):
            picked = []
            for k in range(fars):
                start = pl.multiple_of((where[node, k] - first) * rank, rank)
                picked.append(win[pl.ds(start, rank), :])
            field_buf[node_rows(row + node), :] = dot(wide[node], jnp.concatenate(picked, axis=0))
    for q in range(twos):
        down_buf[node_rows(base + q), :] = field_buf[node_rows(base + q), :].astype(jnp.bfloat16)
    for p in range(ones):
        total = dot(up_two_ref[p], down_buf[node_rows(base + p // 2), :])
        total = total + field_buf[node_rows(leaves + p), :]
        down_buf[node_rows(leaves + p), :] = total.astype(jnp.bfloat16)
    for leaf in range(leaves):
        total = dot(up_one_ref[leaf], down_buf[node_rows(leaves + leaf // 2), :])
        total = total + field_buf[node_rows(leaf), :]
        down_buf[node_rows(leaf), :] = total.astype(jnp.bfloat16)
    outs = []
    for leaf in range(leaves):
        here = pl.ds(leaf * LEAF, LEAF)
        total = sum_buf[here, :] + dot_t(basis_ref[leaf], down_buf[node_rows(leaf), :])
        out_buf[here, :] = total.astype(jnp.bfloat16)
        if leaf % 4 == 3:
            some = pl.ds((leaf - 3) * LEAF, 4 * LEAF)
            outs.append(
                pltpu.make_async_copy(
                    out_buf.at[some, :], out_hbm.at[some, :], out_sems.at[leaf // 4]
                )
            )
            outs[-1].start()
    for copy in outs:
        copy.wait()


def body(
    vectors,
    near_blocks,
    near_list,
    basis,
    up_one,
    up_two,
    couple_zero,
    couple_one,
    couple_two,
    far_zero,
    far_one,
    far_two,
):
    leaves, nears = near_list.shape
    columns = vectors.shape[1]
    rank = basis.shape[2]
    fars = far_zero.shape[1]
    size = lax.axis_size("space")
    cores = lax.axis_size("rhs")
    me = lax.axis_index("space").astype(jnp.int32).reshape(1)
    counts = (leaves, leaves // 2, leaves // 4)
    nodes = sum(counts)
    basis_t = jnp.swapaxes(basis, 1, 2)
    bf16, f32 = jnp.bfloat16, jnp.float32

    hbm = pl.BlockSpec(memory_space=pltpu.HBM)
    vmem = pl.BlockSpec(memory_space=pltpu.VMEM)
    smem = pl.BlockSpec(memory_space=pltpu.SMEM)

    def in_hbm(*arrays):
        return [pltpu.with_memory_space_constraint(a, pltpu.HBM) for a in arrays]

    plain, pair = pl.pallas_call(
        up_kernel,
        in_specs=[smem] + [hbm] * 4,
        out_specs=[vmem] * 2,
        out_shape=[
            pltpu.VMEM((nodes * rank + LEAF, columns), bf16),
            pltpu.VMEM((nodes * rank + LEAF, columns), bf16),
        ],
        scratch_shapes=[
            pltpu.VMEM(vectors.shape, bf16),
            pltpu.VMEM(basis_t.shape, bf16),
            pltpu.VMEM(up_one.shape, bf16),
            pltpu.VMEM(up_two.shape, bf16),
            pltpu.SemaphoreType.DMA((leaves // 2 + 2,)),
        ],
        compiler_params=pltpu.CompilerParams(vmem_limit_bytes=8 * MIB),
        name="up_pass",
    )(me, *in_hbm(vectors, basis_t, up_one, up_two))

    def send(array, to):
        pairs = []
        for i in range(size):
            for c in range(cores):
                j, d = (to(i), c) if 0 <= to(i) < size else (i, cores - 1 - c)
                pairs.append((i * cores + c, j * cores + d))
        return lax.ppermute(array, ("space", "rhs"), pairs)

    def partner(i):
        return i + 1 - 2 * (i % 2)

    from_pair = send(pair, partner)
    turns = (lambda i: i + 2 - i // 2 % 2 * 4, lambda i: i - 2 + i // 2 % 2 * 4)
    first, second = [send(plain, turn) for turn in turns]

    near, points = pl.pallas_call(
        near_kernel,
        in_specs=[smem] + [hbm] * 3,
        out_specs=[vmem] * 2,
        out_shape=[pltpu.VMEM(vectors.shape, f32), pltpu.VMEM(vectors.shape, bf16)],
        scratch_shapes=[
            pltpu.SMEM(near_list.shape, jnp.int32),
            pltpu.VMEM((DEPTH, nears - 2, LEAF, LEAF), bf16),
            pltpu.SemaphoreType.DMA((DEPTH, 2)),
            pltpu.SemaphoreType.DMA((leaves // 4,)),
            pltpu.SemaphoreType.DMA,
        ],
        compiler_params=pltpu.CompilerParams(vmem_limit_bytes=16 * MIB),
        cost_estimate=pl.CostEstimate(
            flops=2 * leaves * (nears - 2) * LEAF * LEAF * columns,
            bytes_accessed=2 * leaves * nears * LEAF * LEAF + 6 * leaves * LEAF * columns,
            transcendentals=0,
        ),
        name="near_own",
    )(me, *in_hbm(near_list, vectors, near_blocks))

    def has_second(i):
        return 0 <= turns[1](i) < size

    split = leaves * rank
    from_pair, near = lax.optimization_barrier((from_pair, near))
    low = from_pair[:split]
    got_first = send(low, turns[0])
    first, second, near = lax.optimization_barrier((first, second, near))
    upper = jnp.where((me[0] // 2 + me[0]) % 2 == 0, first[split:], second[split:])
    at_end = (me[0] < 2) | (me[0] >= size - 2)
    got_second = send(
        jnp.where(at_end, upper, low), lambda i: turns[1](i) if has_second(i) else partner(i)
    )
    got_third = send(upper, lambda i: partner(i) if has_second(i) else -1)

    sums, edge, *rest = pl.pallas_call(
        prep_kernel,
        in_specs=[smem] + [vmem] * 5 + [hbm] * 4,
        out_specs=[vmem] * 8,
        out_shape=[
            pltpu.VMEM(vectors.shape, f32),
            pltpu.VMEM((leaves, 2, LEAF, LEAF), bf16),
            *[pltpu.VMEM((SPAN * n * rank, columns), bf16) for n in counts],
            *[pltpu.VMEM((n, rank, fars * rank), bf16) for n in counts],
        ],
        scratch_shapes=[
            *[pltpu.VMEM((n, fars, rank, rank), bf16) for n in counts],
            pltpu.SemaphoreType.DMA((sum(n // 4 for n in counts),)),
            pltpu.SemaphoreType.DMA((12,)),
            pltpu.SemaphoreType.DMA((leaves // 4,)),
        ],
        compiler_params=pltpu.CompilerParams(vmem_limit_bytes=16 * MIB),
        cost_estimate=pl.CostEstimate(
            flops=4 * 10**9,
            bytes_accessed=4 * nodes * fars * rank * rank + 4 * leaves * LEAF * LEAF,
            transcendentals=0,
        ),
        name="prep",
    )(
        me, plain, from_pair, first, second, near,
        *in_hbm(near_blocks, couple_zero, couple_one, couple_two),
    )
    windows, wides = rest[:3], rest[3:]

    out, *_ = pl.pallas_call(
        functools.partial(far_kernel, size=size),
        in_specs=[smem] * 4 + [vmem] * 15,
        out_specs=[hbm] + [vmem] * 3,
        out_shape=[
            jax.ShapeDtypeStruct(vectors.shape, bf16),
            *[pltpu.VMEM((SPAN * n * rank, columns), bf16) for n in counts],
        ],
        input_output_aliases={16: 1, 17: 2, 18: 3},
        scratch_shapes=[
            pltpu.VMEM(vectors.shape, f32),
            pltpu.VMEM(vectors.shape, bf16),
            pltpu.VMEM((LEAF, columns), bf16),
            pltpu.VMEM((nodes * rank, columns), f32),
            pltpu.VMEM((nodes * rank, columns), bf16),
            pltpu.SemaphoreType.DMA((3,)),
            pltpu.SemaphoreType.DMA((leaves // 4,)),
        ],
        compiler_params=pltpu.CompilerParams(vmem_limit_bytes=16 * MIB),
        name="far_down",
    )(
        me, far_zero, far_one, far_two, points, got_first, got_second, got_third, sums, edge,
        basis_t, up_one, up_two, *wides, *windows,
    )
    return out


def solution(mesh):
    placed = (
        P(("groups", "space"), "rhs"),
        P("space", None, None, None),
        P("space", None),
        P("space", None, None),
        P("space", None, None),
        P("space", None, None),
        P("space", None, None, None),
        P("space", None, None, None),
        P("space", None, None, None),
        P("space", None),
        P("space", None),
        P("space", None),
    )
    return jax.shard_map(
        body, mesh=mesh, in_specs=placed, out_specs=P(("groups", "space"), "rhs"), check_vma=False
    )
```

```python
import functools

import jax
import jax.numpy as jnp
from jax import lax
from jax.experimental import pallas as pl
from jax.experimental.pallas import tpu as pltpu
from jax.sharding import PartitionSpec as P

LEAF = 256
REACH = 2
SPAN = 2 * REACH + 1
DEPTH = 3
MIB = 1024 * 1024


def dot(a, b):
    return jnp.dot(a, b, preferred_element_type=jnp.float32)


def dot_t(a, b):
    return lax.dot_general(a, b, (((0,), (0,)), ((), ())), preferred_element_type=jnp.float32)


def up_kernel(
    me_ref, x_hbm, basis_hbm, up_one_hbm, up_two_hbm, plain_ref, pair_ref,
    x_ref, basis_ref, up_one_ref, up_two_ref, sems,
):
    leaves, rank = basis_ref.shape[:2]
    steps = leaves // 4
    copies = []
    for q in range(steps):
        rows = pl.ds(q * 4 * LEAF, 4 * LEAF)
        some = pl.ds(q * 4, 4)
        copies.append(
            (
                pltpu.make_async_copy(x_hbm.at[rows, :], x_ref.at[rows, :], sems.at[2 * q]),
                pltpu.make_async_copy(basis_hbm.at[some], basis_ref.at[some], sems.at[2 * q + 1]),
            )
        )
    ups = (
        pltpu.make_async_copy(up_one_hbm, up_one_ref, sems.at[2 * steps]),
        pltpu.make_async_copy(up_two_hbm, up_two_ref, sems.at[2 * steps + 1]),
    )
    for pair in (*copies, ups):
        for copy in pair:
            copy.start()

    def put(node, value):
        value = value.astype(jnp.bfloat16)
        plain_ref[pl.ds(node * rank, rank), :] = value
        pair_ref[pl.ds(node * rank, rank), :] = value
        return value

    def join(ups, pair):
        return dot_t(ups.reshape(2 * rank, rank), jnp.concatenate(pair, axis=0))

    zeros = []
    for q in range(steps):
        for copy in copies[q]:
            copy.wait()
        for leaf in range(4 * q, 4 * q + 4):
            coef = dot(basis_ref[leaf], x_ref[pl.ds(leaf * LEAF, LEAF), :])
            zeros.append(put(leaf, coef))
    for copy in ups:
        copy.wait()
    ones = []
    for p in range(leaves // 2):
        pair = slice(2 * p, 2 * p + 2)
        ones.append(put(leaves + p, join(up_one_ref[pair], zeros[pair])))
    for q in range(leaves // 4):
        pair = slice(2 * q, 2 * q + 2)
        put(leaves + leaves // 2 + q, join(up_two_ref[pair], ones[pair]))
    odd = lax.rem(me_ref[0], 2)
    last = (leaves - 1) * LEAF
    end = pl.ds(plain_ref.shape[0] - LEAF, LEAF)
    pair_ref[end, :] = x_ref[pl.ds(pl.multiple_of((1 - odd) * last, LEAF), LEAF), :]
    plain_ref[end, :] = x_ref[pl.ds(pl.multiple_of(odd * last, LEAF), LEAF), :]


def near_kernel(
    me_ref, list_hbm, x_hbm, blocks_hbm, out_ref, edge_ref, x_ref,
    list_ref, block_buf, sems, x_sems, list_sem,
):
    leaves, nears = list_ref.shape
    first = me_ref[0] * leaves
    depth = block_buf.shape[0]

    def copies(pair, slot):
        both = pl.ds(2 * pair, 2)
        pairs = (
            (blocks_hbm.at[both, pl.ds(0, 1)], block_buf.at[slot, :, pl.ds(0, 1)]),
            (blocks_hbm.at[both, pl.ds(3, nears - 3)], block_buf.at[slot, :, pl.ds(1, nears - 3)]),
            (blocks_hbm.at[both, pl.ds(1, 2)], edge_ref.at[both]),
        )
        return [
            pltpu.make_async_copy(src, dst, sems.at[slot, i]) for i, (src, dst) in enumerate(pairs)
        ]

    list_copy = pltpu.make_async_copy(list_hbm, list_ref, list_sem)
    list_copy.start()
    x_copies = []
    for q in range(leaves // 4):
        rows = pl.ds(q * 4 * LEAF, 4 * LEAF)
        x_copies.append(
            pltpu.make_async_copy(x_hbm.at[rows, :], x_ref.at[rows, :], x_sems.at[q])
        )
    for copy in x_copies:
        copy.start()
    for pair in range(depth - 1):
        for copy in copies(pair, pair):
            copy.start()
    list_copy.wait()
    for copy in x_copies:
        copy.wait()

    def step(pair, carry):
        slot = lax.rem(pair, depth)

        @pl.when(pair + depth - 1 < leaves // 2)
        def _():
            for copy in copies(pair + depth - 1, lax.rem(pair + depth - 1, depth)):
                copy.start()

        for copy in copies(pair, slot):
            copy.wait()
        totals = []
        for side in range(2):
            rows = []
            for k in (0, *range(3, nears)):
                start = (list_ref[2 * pair + side, k] - first) * LEAF
                rows.append(x_ref[pl.ds(pl.multiple_of(start, LEAF), LEAF), :])
            blocks = [block_buf[slot, side, k] for k in range(nears - 2)]
            totals.append(dot(jnp.concatenate(blocks, axis=1), jnp.concatenate(rows, axis=0)))
        here = pl.ds(pl.multiple_of(pair * 2 * LEAF, 2 * LEAF), 2 * LEAF)
        out_ref[here, :] = jnp.concatenate(totals, axis=0)
        return carry

    lax.fori_loop(0, leaves // 2, step, 0)


def add_edge(sum_ref, near_ref, edge_ref, side, rows):
    for leaf in range(edge_ref.shape[0]):
        here = pl.ds(leaf * LEAF, LEAF)
        sum_ref[here, :] = near_ref[here, :] + dot(edge_ref[leaf, side], rows)


def window_copies(plans, sems):
    copies = []
    for ref, start, win, at, size in plans:
        copies.append(
            pltpu.make_async_copy(
                ref.at[pl.ds(start, size), :], win.at[pl.ds(at, size), :], sems.at[len(copies)]
            )
        )
    return copies


def prep_kernel(
    me_ref, own_ref, pair_ref, first_ref, second_ref, near_ref, edge_ref,
    zero_hbm, one_hbm, two_hbm,
    sum_ref, zero_win, one_win, two_win, zero_wide, one_wide, two_wide,
    zero_buf, one_buf, two_buf, sems, win_sems,
):
    levels = (
        (two_hbm, two_buf, two_wide),
        (one_hbm, one_buf, one_wide),
        (zero_hbm, zero_buf, zero_wide),
    )
    chunks = []
    for hbm, buf, wide in levels:
        for first in range(0, buf.shape[0], 4):
            some = pl.ds(first, 4)
            copy = pltpu.make_async_copy(hbm.at[some], buf.at[some], sems.at[len(chunks)])
            copy.start()
            chunks.append((copy, buf, wide, first))
    me = me_ref[0]
    odd = lax.rem(me, 2)
    block = lax.rem(me // 2, 2)
    pieces = (
        (own_ref, 0, REACH),
        (first_ref, 0, (1 - block) * (SPAN - 1)),
        (second_ref, 0, block * (SPAN - 1)),
        (pair_ref, 0, REACH + 1 - 2 * odd),
    )
    plans = []
    for ref, start, place in pieces:
        for win in (zero_win, one_win, two_win):
            size = win.shape[0] // SPAN
            plans.append((ref, start, win, pl.multiple_of(place * size, size), size))
            start += size
    moves = window_copies(plans, win_sems)
    for move in moves:
        move.start()
    add_edge(sum_ref, near_ref, edge_ref, odd, pair_ref[pl.ds(pair_ref.shape[0] - LEAF, LEAF), :])
    for copy, buf, wide, first in chunks:
        copy.wait()
        for node in range(first, first + 4):
            fars = buf.shape[1]
            wide[node] = jnp.concatenate([buf[node, k] for k in range(fars)], axis=1)
    for move in moves:
        move.wait()


def far_kernel(
    me_ref, zero_list, one_list, two_list, x_ref, got_first, got_second, got_third, near_ref,
    edge_ref, basis_ref, up_one_ref, up_two_ref, zero_wide, one_wide, two_wide, zero_in, one_in, two_in,
    out_hbm, zero_win, one_win, two_win,
    sum_buf, out_buf, rows_buf, field_buf, down_buf, win_sems, out_sems, *, size,
):
    del zero_in, one_in, two_in
    leaves, rank, deep = zero_wide.shape
    ones, twos = leaves // 2, leaves // 4
    fars = deep // rank
    me = me_ref[0]
    odd = lax.rem(me, 2)
    place = REACH - 1 + 2 * odd
    sizes = [n * rank for n in (leaves, ones, twos)]
    at = [pl.multiple_of(place * n, n) for n in sizes]

    def arrivals(low_ref, high_ref):
        plans = (
            (low_ref, 0, zero_win, at[0], sizes[0]),
            (high_ref, 0, one_win, at[1], sizes[1]),
            (high_ref, sizes[1], two_win, at[2], sizes[2]),
        )
        return window_copies(plans, win_sems)

    end = pl.ds(got_first.shape[0] - LEAF, LEAF)
    low_first = lax.rem(me + me // 2, 2) == 1
    at_end = (me < 2) | (me >= size - 2)

    def take(low_ref, high_ref):
        def _():
            for move in arrivals(low_ref, high_ref):
                move.start()
            rows_buf[...] = high_ref[end, :]

        return _

    pl.when(low_first & at_end)(take(got_first, got_second))
    pl.when(low_first & jnp.logical_not(at_end))(take(got_first, got_third))
    pl.when(jnp.logical_not(low_first))(take(got_second, got_third))
    moves = arrivals(got_first, got_second)

    alone = (me == 0) | (me == size - 1)

    @pl.when(alone)
    def _():
        for leaf in range(leaves):
            here = pl.ds(leaf * LEAF, LEAF)
            sum_buf[here, :] = near_ref[here, :] + dot(edge_ref[leaf, 1 - odd], x_ref[here, :])

    @pl.when(jnp.logical_not(alone))
    def _():
        add_edge(sum_buf, near_ref, edge_ref, 1 - odd, rows_buf[...])

    for move in moves:
        move.wait()

    def node_rows(row):
        return pl.ds(row * rank, rank)

    base = leaves + ones
    levels = (
        (two_wide, two_list, two_win, base),
        (one_wide, one_list, one_win, leaves),
        (zero_wide, zero_list, zero_win, 0),
    )
    for wide, where, win, row in levels:
        first = (me - REACH) * wide.shape[0]
        for node in range(wide.shape[0]):
            picked = []
            for k in range(fars):
                start = pl.multiple_of((where[node, k] - first) * rank, rank)
                picked.append(win[pl.ds(start, rank), :])
            field_buf[node_rows(row + node), :] = dot(wide[node], jnp.concatenate(picked, axis=0))
    for q in range(twos):
        down_buf[node_rows(base + q), :] = field_buf[node_rows(base + q), :].astype(jnp.bfloat16)
    for p in range(ones):
        total = dot(up_two_ref[p], down_buf[node_rows(base + p // 2), :])
        total = total + field_buf[node_rows(leaves + p), :]
        down_buf[node_rows(leaves + p), :] = total.astype(jnp.bfloat16)
    for leaf in range(leaves):
        total = dot(up_one_ref[leaf], down_buf[node_rows(leaves + leaf // 2), :])
        total = total + field_buf[node_rows(leaf), :]
        down_buf[node_rows(leaf), :] = total.astype(jnp.bfloat16)
    outs = []
    for leaf in range(leaves):
        here = pl.ds(leaf * LEAF, LEAF)
        total = sum_buf[here, :] + dot_t(basis_ref[leaf], down_buf[node_rows(leaf), :])
        out_buf[here, :] = total.astype(jnp.bfloat16)
        if leaf % 4 == 3:
            some = pl.ds((leaf - 3) * LEAF, 4 * LEAF)
            outs.append(
                pltpu.make_async_copy(
                    out_buf.at[some, :], out_hbm.at[some, :], out_sems.at[leaf // 4]
                )
            )
            outs[-1].start()
    for copy in outs:
        copy.wait()


def body(
    vectors,
    near_blocks,
    near_list,
    basis,
    up_one,
    up_two,
    couple_zero,
    couple_one,
    couple_two,
    far_zero,
    far_one,
    far_two,
):
    leaves, nears = near_list.shape
    columns = vectors.shape[1]
    rank = basis.shape[2]
    fars = far_zero.shape[1]
    size = lax.axis_size("space")
    cores = lax.axis_size("rhs")
    me = lax.axis_index("space").astype(jnp.int32).reshape(1)
    counts = (leaves, leaves // 2, leaves // 4)
    nodes = sum(counts)
    basis_t = jnp.swapaxes(basis, 1, 2)
    bf16, f32 = jnp.bfloat16, jnp.float32

    hbm = pl.BlockSpec(memory_space=pltpu.HBM)
    vmem = pl.BlockSpec(memory_space=pltpu.VMEM)
    smem = pl.BlockSpec(memory_space=pltpu.SMEM)

    def in_hbm(*arrays):
        return [pltpu.with_memory_space_constraint(a, pltpu.HBM) for a in arrays]

    plain, pair = pl.pallas_call(
        up_kernel,
        in_specs=[smem] + [hbm] * 4,
        out_specs=[vmem] * 2,
        out_shape=[
            pltpu.VMEM((nodes * rank + LEAF, columns), bf16),
            pltpu.VMEM((nodes * rank + LEAF, columns), bf16),
        ],
        scratch_shapes=[
            pltpu.VMEM(vectors.shape, bf16),
            pltpu.VMEM(basis_t.shape, bf16),
            pltpu.VMEM(up_one.shape, bf16),
            pltpu.VMEM(up_two.shape, bf16),
            pltpu.SemaphoreType.DMA((leaves // 2 + 2,)),
        ],
        compiler_params=pltpu.CompilerParams(vmem_limit_bytes=8 * MIB),
        name="up_pass",
    )(me, *in_hbm(vectors, basis_t, up_one, up_two))

    def send(array, to):
        pairs = []
        for i in range(size):
            for c in range(cores):
                j, d = (to(i), c) if 0 <= to(i) < size else (i, cores - 1 - c)
                pairs.append((i * cores + c, j * cores + d))
        return lax.ppermute(array, ("space", "rhs"), pairs)

    def partner(i):
        return i + 1 - 2 * (i % 2)

    from_pair = send(pair, partner)
    turns = (lambda i: i + 2 - i // 2 % 2 * 4, lambda i: i - 2 + i // 2 % 2 * 4)
    first, second = [send(plain, turn) for turn in turns]

    near, edge, points = pl.pallas_call(
        near_kernel,
        in_specs=[smem] + [hbm] * 3,
        out_specs=[vmem] * 3,
        out_shape=[
            pltpu.VMEM(vectors.shape, f32),
            pltpu.VMEM((leaves, 2, LEAF, LEAF), bf16),
            pltpu.VMEM(vectors.shape, bf16),
        ],
        scratch_shapes=[
            pltpu.SMEM(near_list.shape, jnp.int32),
            pltpu.VMEM((DEPTH, 2, nears - 2, LEAF, LEAF), bf16),
            pltpu.SemaphoreType.DMA((DEPTH, 3)),
            pltpu.SemaphoreType.DMA((leaves // 4,)),
            pltpu.SemaphoreType.DMA,
        ],
        compiler_params=pltpu.CompilerParams(vmem_limit_bytes=16 * MIB),
        cost_estimate=pl.CostEstimate(
            flops=2 * leaves * (nears - 2) * LEAF * LEAF * columns,
            bytes_accessed=2 * leaves * nears * LEAF * LEAF + 6 * leaves * LEAF * columns,
            transcendentals=0,
        ),
        name="near_own",
    )(me, *in_hbm(near_list, vectors, near_blocks))

    def has_second(i):
        return 0 <= turns[1](i) < size

    split = leaves * rank
    from_pair, near = lax.optimization_barrier((from_pair, near))
    low = from_pair[:split]
    got_first = send(low, turns[0])
    first, second, near = lax.optimization_barrier((first, second, near))
    upper = jnp.where((me[0] // 2 + me[0]) % 2 == 0, first[split:], second[split:])
    at_end = (me[0] < 2) | (me[0] >= size - 2)
    got_second = send(
        jnp.where(at_end, upper, low), lambda i: turns[1](i) if has_second(i) else partner(i)
    )
    got_third = send(upper, lambda i: partner(i) if has_second(i) else -1)

    sums, *rest = pl.pallas_call(
        prep_kernel,
        in_specs=[smem] + [vmem] * 6 + [hbm] * 3,
        out_specs=[vmem] * 7,
        out_shape=[
            pltpu.VMEM(vectors.shape, f32),
            *[pltpu.VMEM((SPAN * n * rank, columns), bf16) for n in counts],
            *[pltpu.VMEM((n, rank, fars * rank), bf16) for n in counts],
        ],
        scratch_shapes=[
            *[pltpu.VMEM((n, fars, rank, rank), bf16) for n in counts],
            pltpu.SemaphoreType.DMA((sum(n // 4 for n in counts),)),
            pltpu.SemaphoreType.DMA((12,)),
        ],
        compiler_params=pltpu.CompilerParams(vmem_limit_bytes=16 * MIB),
        cost_estimate=pl.CostEstimate(
            flops=4 * 10**9,
            bytes_accessed=4 * nodes * fars * rank * rank,
            transcendentals=0,
        ),
        name="prep",
    )(
        me, plain, from_pair, first, second, near, edge,
        *in_hbm(couple_zero, couple_one, couple_two),
    )
    windows, wides = rest[:3], rest[3:]

    out, *_ = pl.pallas_call(
        functools.partial(far_kernel, size=size),
        in_specs=[smem] * 4 + [vmem] * 15,
        out_specs=[hbm] + [vmem] * 3,
        out_shape=[
            jax.ShapeDtypeStruct(vectors.shape, bf16),
            *[pltpu.VMEM((SPAN * n * rank, columns), bf16) for n in counts],
        ],
        input_output_aliases={16: 1, 17: 2, 18: 3},
        scratch_shapes=[
            pltpu.VMEM(vectors.shape, f32),
            pltpu.VMEM(vectors.shape, bf16),
            pltpu.VMEM((LEAF, columns), bf16),
            pltpu.VMEM((nodes * rank, columns), f32),
            pltpu.VMEM((nodes * rank, columns), bf16),
            pltpu.SemaphoreType.DMA((3,)),
            pltpu.SemaphoreType.DMA((leaves // 4,)),
        ],
        compiler_params=pltpu.CompilerParams(vmem_limit_bytes=16 * MIB),
        name="far_down",
    )(
        me, far_zero, far_one, far_two, points, got_first, got_second, got_third, sums, edge,
        basis_t, up_one, up_two, *wides, *windows,
    )
    return out


def solution(mesh):
    placed = (
        P(("groups", "space"), "rhs"),
        P("space", None, None, None),
        P("space", None),
        P("space", None, None),
        P("space", None, None),
        P("space", None, None),
        P("space", None, None, None),
        P("space", None, None, None),
        P("space", None, None, None),
        P("space", None),
        P("space", None),
        P("space", None),
    )
    return jax.shard_map(
        body, mesh=mesh, in_specs=placed, out_specs=P(("groups", "space"), "rhs"), check_vma=False
    )
```

```python
import functools

import jax
import jax.numpy as jnp
from jax import lax
from jax.experimental import pallas as pl
from jax.experimental.pallas import tpu as pltpu
from jax.sharding import PartitionSpec as P

LEAF = 256
REACH = 2
SPAN = 2 * REACH + 1
DEPTH = 3
MIB = 1024 * 1024


def dot(a, b):
    return jnp.dot(a, b, preferred_element_type=jnp.float32)


def dot_t(a, b):
    return lax.dot_general(a, b, (((0,), (0,)), ((), ())), preferred_element_type=jnp.float32)


def up_kernel(
    me_ref, x_hbm, basis_hbm, up_one_hbm, up_two_hbm, plain_ref, pair_ref,
    x_ref, basis_ref, up_one_ref, up_two_ref, sems,
):
    leaves, rank = basis_ref.shape[:2]
    steps = leaves // 4
    copies = []
    for q in range(steps):
        rows = pl.ds(q * 4 * LEAF, 4 * LEAF)
        some = pl.ds(q * 4, 4)
        copies.append(
            (
                pltpu.make_async_copy(x_hbm.at[rows, :], x_ref.at[rows, :], sems.at[2 * q]),
                pltpu.make_async_copy(basis_hbm.at[some], basis_ref.at[some], sems.at[2 * q + 1]),
            )
        )
    ups = (
        pltpu.make_async_copy(up_one_hbm, up_one_ref, sems.at[2 * steps]),
        pltpu.make_async_copy(up_two_hbm, up_two_ref, sems.at[2 * steps + 1]),
    )
    for pair in (*copies, ups):
        for copy in pair:
            copy.start()

    def put(node, value):
        value = value.astype(jnp.bfloat16)
        plain_ref[pl.ds(node * rank, rank), :] = value
        pair_ref[pl.ds(node * rank, rank), :] = value
        return value

    def join(ups, pair):
        return dot_t(ups.reshape(2 * rank, rank), jnp.concatenate(pair, axis=0))

    zeros = []
    for q in range(steps):
        for copy in copies[q]:
            copy.wait()
        for leaf in range(4 * q, 4 * q + 4):
            coef = dot(basis_ref[leaf], x_ref[pl.ds(leaf * LEAF, LEAF), :])
            zeros.append(put(leaf, coef))
    for copy in ups:
        copy.wait()
    ones = []
    for p in range(leaves // 2):
        pair = slice(2 * p, 2 * p + 2)
        ones.append(put(leaves + p, join(up_one_ref[pair], zeros[pair])))
    for q in range(leaves // 4):
        pair = slice(2 * q, 2 * q + 2)
        put(leaves + leaves // 2 + q, join(up_two_ref[pair], ones[pair]))
    odd = lax.rem(me_ref[0], 2)
    last = (leaves - 1) * LEAF
    end = pl.ds(plain_ref.shape[0] - LEAF, LEAF)
    pair_ref[end, :] = x_ref[pl.ds(pl.multiple_of((1 - odd) * last, LEAF), LEAF), :]
    plain_ref[end, :] = x_ref[pl.ds(pl.multiple_of(odd * last, LEAF), LEAF), :]


def near_kernel(
    me_ref, list_hbm, x_hbm, blocks_hbm, out_ref, edge_ref, x_ref,
    list_ref, block_buf, sems, x_sems, list_sem,
):
    leaves, nears = list_ref.shape
    first = me_ref[0] * leaves
    depth = block_buf.shape[0]

    def copies(pair, slot):
        both = pl.ds(2 * pair, 2)
        pairs = (
            (blocks_hbm.at[both, pl.ds(0, 1)], block_buf.at[slot, :, pl.ds(0, 1)]),
            (blocks_hbm.at[both, pl.ds(3, nears - 3)], block_buf.at[slot, :, pl.ds(1, nears - 3)]),
            (blocks_hbm.at[both, pl.ds(1, 2)], edge_ref.at[both]),
        )
        return [
            pltpu.make_async_copy(src, dst, sems.at[slot, i]) for i, (src, dst) in enumerate(pairs)
        ]

    list_copy = pltpu.make_async_copy(list_hbm, list_ref, list_sem)
    list_copy.start()
    x_copies = []
    for q in range(leaves // 4):
        rows = pl.ds(q * 4 * LEAF, 4 * LEAF)
        x_copies.append(
            pltpu.make_async_copy(x_hbm.at[rows, :], x_ref.at[rows, :], x_sems.at[q])
        )
    for copy in x_copies:
        copy.start()
    for pair in range(depth - 1):
        for copy in copies(pair, pair):
            copy.start()
    list_copy.wait()
    for copy in x_copies:
        copy.wait()

    def step(pair, carry):
        slot = lax.rem(pair, depth)

        @pl.when(pair + depth - 1 < leaves // 2)
        def _():
            for copy in copies(pair + depth - 1, lax.rem(pair + depth - 1, depth)):
                copy.start()

        for copy in copies(pair, slot):
            copy.wait()
        totals = []
        for side in range(2):
            rows = []
            for k in (0, *range(3, nears)):
                start = (list_ref[2 * pair + side, k] - first) * LEAF
                rows.append(x_ref[pl.ds(pl.multiple_of(start, LEAF), LEAF), :])
            blocks = [block_buf[slot, side, k] for k in range(nears - 2)]
            totals.append(dot(jnp.concatenate(blocks, axis=1), jnp.concatenate(rows, axis=0)))
        here = pl.ds(pl.multiple_of(pair * 2 * LEAF, 2 * LEAF), 2 * LEAF)
        out_ref[here, :] = jnp.concatenate(totals, axis=0)
        return carry

    lax.fori_loop(0, leaves // 2, step, 0)


def add_edge(sum_ref, near_ref, edge_ref, side, rows):
    for leaf in range(edge_ref.shape[0]):
        here = pl.ds(leaf * LEAF, LEAF)
        sum_ref[here, :] = near_ref[here, :] + dot(edge_ref[leaf, side], rows)


def window_copies(plans, sems):
    copies = []
    for ref, start, win, at, size in plans:
        copies.append(
            pltpu.make_async_copy(
                ref.at[pl.ds(start, size), :], win.at[pl.ds(at, size), :], sems.at[len(copies)]
            )
        )
    return copies


def prep_kernel(
    me_ref, own_ref, pair_ref, first_ref, second_ref, near_ref, edge_ref,
    zero_hbm, one_hbm, two_hbm,
    sum_ref, zero_win, one_win, two_win, zero_wide, one_wide, two_wide,
    zero_buf, one_buf, two_buf, sems, win_sems,
):
    levels = (
        (two_hbm, two_buf, two_wide),
        (one_hbm, one_buf, one_wide),
        (zero_hbm, zero_buf, zero_wide),
    )
    chunks = []
    for hbm, buf, wide in levels:
        for first in range(0, buf.shape[0], 4):
            some = pl.ds(first, 4)
            copy = pltpu.make_async_copy(hbm.at[some], buf.at[some], sems.at[len(chunks)])
            copy.start()
            chunks.append((copy, buf, wide, first))
    me = me_ref[0]
    odd = lax.rem(me, 2)
    block = lax.rem(me // 2, 2)
    pieces = (
        (own_ref, 0, REACH),
        (first_ref, 0, (1 - block) * (SPAN - 1)),
        (second_ref, 0, block * (SPAN - 1)),
        (pair_ref, 0, REACH + 1 - 2 * odd),
    )
    plans = []
    for ref, start, place in pieces:
        for win in (zero_win, one_win, two_win):
            size = win.shape[0] // SPAN
            plans.append((ref, start, win, pl.multiple_of(place * size, size), size))
            start += size
    moves = window_copies(plans, win_sems)
    for move in moves:
        move.start()
    add_edge(sum_ref, near_ref, edge_ref, odd, pair_ref[pl.ds(pair_ref.shape[0] - LEAF, LEAF), :])
    for copy, buf, wide, first in chunks:
        copy.wait()
        for node in range(first, first + 4):
            fars = buf.shape[1]
            wide[node] = jnp.concatenate([buf[node, k] for k in range(fars)], axis=1)
    for move in moves:
        move.wait()


def far_kernel(
    me_ref, zero_list, one_list, two_list, x_ref, got_first, got_second, got_third, near_ref,
    edge_ref, basis_ref, up_one_ref, up_two_ref, zero_wide, one_wide, two_wide, zero_in, one_in, two_in,
    out_hbm, zero_win, one_win, two_win,
    sum_buf, out_buf, rows_buf, field_buf, down_buf, win_sems, out_sems, *, size,
):
    del zero_in, one_in, two_in
    leaves, rank, deep = zero_wide.shape
    ones, twos = leaves // 2, leaves // 4
    fars = deep // rank
    me = me_ref[0]
    odd = lax.rem(me, 2)
    place = REACH - 1 + 2 * odd
    sizes = [n * rank for n in (leaves, ones, twos)]
    at = [pl.multiple_of(place * n, n) for n in sizes]

    def arrivals(low_ref, high_ref):
        plans = (
            (low_ref, 0, zero_win, at[0], sizes[0]),
            (high_ref, 0, one_win, at[1], sizes[1]),
            (high_ref, sizes[1], two_win, at[2], sizes[2]),
        )
        return window_copies(plans, win_sems)

    end = pl.ds(got_first.shape[0] - LEAF, LEAF)
    low_first = lax.rem(me + me // 2, 2) == 1
    at_end = (me < 2) | (me >= size - 2)

    def take(low_ref, high_ref):
        def _():
            for move in arrivals(low_ref, high_ref):
                move.start()
            rows_buf[...] = high_ref[end, :]

        return _

    pl.when(low_first & at_end)(take(got_first, got_second))
    pl.when(low_first & jnp.logical_not(at_end))(take(got_first, got_third))
    pl.when(jnp.logical_not(low_first))(take(got_second, got_third))
    moves = arrivals(got_first, got_second)

    alone = (me == 0) | (me == size - 1)

    @pl.when(alone)
    def _():
        for leaf in range(leaves):
            here = pl.ds(leaf * LEAF, LEAF)
            sum_buf[here, :] = near_ref[here, :] + dot(edge_ref[leaf, 1 - odd], x_ref[here, :])

    @pl.when(jnp.logical_not(alone))
    def _():
        add_edge(sum_buf, near_ref, edge_ref, 1 - odd, rows_buf[...])

    for move in moves:
        move.wait()

    def node_rows(row):
        return pl.ds(row * rank, rank)

    base = leaves + ones
    levels = (
        (two_wide, two_list, two_win, base),
        (one_wide, one_list, one_win, leaves),
        (zero_wide, zero_list, zero_win, 0),
    )
    for wide, where, win, row in levels:
        first = (me - REACH) * wide.shape[0]
        for node in range(wide.shape[0]):
            picked = []
            for k in range(fars):
                start = pl.multiple_of((where[node, k] - first) * rank, rank)
                picked.append(win[pl.ds(start, rank), :])
            field_buf[node_rows(row + node), :] = dot(wide[node], jnp.concatenate(picked, axis=0))
    for q in range(twos):
        down_buf[node_rows(base + q), :] = field_buf[node_rows(base + q), :].astype(jnp.bfloat16)
    for p in range(ones):
        total = dot(up_two_ref[p], down_buf[node_rows(base + p // 2), :])
        total = total + field_buf[node_rows(leaves + p), :]
        down_buf[node_rows(leaves + p), :] = total.astype(jnp.bfloat16)
    for leaf in range(leaves):
        total = dot(up_one_ref[leaf], down_buf[node_rows(leaves + leaf // 2), :])
        total = total + field_buf[node_rows(leaf), :]
        down_buf[node_rows(leaf), :] = total.astype(jnp.bfloat16)
    outs = []
    for leaf in range(leaves):
        here = pl.ds(leaf * LEAF, LEAF)
        total = sum_buf[here, :] + dot_t(basis_ref[leaf], down_buf[node_rows(leaf), :])
        out_buf[here, :] = total.astype(jnp.bfloat16)
        if leaf % 4 == 3:
            some = pl.ds((leaf - 3) * LEAF, 4 * LEAF)
            outs.append(
                pltpu.make_async_copy(
                    out_buf.at[some, :], out_hbm.at[some, :], out_sems.at[leaf // 4]
                )
            )
            outs[-1].start()
    for copy in outs:
        copy.wait()


def body(
    vectors,
    near_blocks,
    near_list,
    basis,
    up_one,
    up_two,
    couple_zero,
    couple_one,
    couple_two,
    far_zero,
    far_one,
    far_two,
):
    leaves, nears = near_list.shape
    columns = vectors.shape[1]
    rank = basis.shape[2]
    fars = far_zero.shape[1]
    size = lax.axis_size("space")
    cores = lax.axis_size("rhs")
    me = lax.axis_index("space").astype(jnp.int32).reshape(1)
    counts = (leaves, leaves // 2, leaves // 4)
    nodes = sum(counts)
    basis_t = jnp.swapaxes(basis, 1, 2)
    bf16, f32 = jnp.bfloat16, jnp.float32

    hbm = pl.BlockSpec(memory_space=pltpu.HBM)
    vmem = pl.BlockSpec(memory_space=pltpu.VMEM)
    smem = pl.BlockSpec(memory_space=pltpu.SMEM)

    def in_hbm(*arrays):
        return [pltpu.with_memory_space_constraint(a, pltpu.HBM) for a in arrays]

    plain, pair = pl.pallas_call(
        up_kernel,
        in_specs=[smem] + [hbm] * 4,
        out_specs=[vmem] * 2,
        out_shape=[
            pltpu.VMEM((nodes * rank + LEAF, columns), bf16),
            pltpu.VMEM((nodes * rank + LEAF, columns), bf16),
        ],
        scratch_shapes=[
            pltpu.VMEM(vectors.shape, bf16),
            pltpu.VMEM(basis_t.shape, bf16),
            pltpu.VMEM(up_one.shape, bf16),
            pltpu.VMEM(up_two.shape, bf16),
            pltpu.SemaphoreType.DMA((leaves // 2 + 2,)),
        ],
        compiler_params=pltpu.CompilerParams(vmem_limit_bytes=8 * MIB),
        name="up_pass",
    )(me, *in_hbm(vectors, basis_t, up_one, up_two))

    def send(array, to):
        pairs = []
        for i in range(size):
            for c in range(cores):
                j, d = (to(i), c) if 0 <= to(i) < size else (i, cores - 1 - c)
                pairs.append((i * cores + c, j * cores + d))
        return lax.ppermute(array, ("space", "rhs"), pairs)

    def partner(i):
        return i + 1 - 2 * (i % 2)

    from_pair = send(pair, partner)
    turns = (lambda i: i + 2 - i // 2 % 2 * 4, lambda i: i - 2 + i // 2 % 2 * 4)
    first, second = [send(plain, turn) for turn in turns]

    near, edge, points = pl.pallas_call(
        near_kernel,
        in_specs=[smem] + [hbm] * 3,
        out_specs=[vmem] * 3,
        out_shape=[
            pltpu.VMEM(vectors.shape, f32),
            pltpu.VMEM((leaves, 2, LEAF, LEAF), bf16),
            pltpu.VMEM(vectors.shape, bf16),
        ],
        scratch_shapes=[
            pltpu.SMEM(near_list.shape, jnp.int32),
            pltpu.VMEM((DEPTH, 2, nears - 2, LEAF, LEAF), bf16),
            pltpu.SemaphoreType.DMA((DEPTH, 3)),
            pltpu.SemaphoreType.DMA((leaves // 4,)),
            pltpu.SemaphoreType.DMA,
        ],
        compiler_params=pltpu.CompilerParams(vmem_limit_bytes=16 * MIB),
        cost_estimate=pl.CostEstimate(
            flops=2 * leaves * (nears - 2) * LEAF * LEAF * columns,
            bytes_accessed=2 * leaves * nears * LEAF * LEAF + 6 * leaves * LEAF * columns,
            transcendentals=0,
        ),
        name="near_own",
    )(me, *in_hbm(near_list, vectors, near_blocks))

    def has_second(i):
        return 0 <= turns[1](i) < size

    split = leaves * rank
    from_pair, near = lax.optimization_barrier((from_pair, near))
    low = lax.optimization_barrier(from_pair[:split])
    got_first = send(low, turns[0])
    second, first, low = lax.optimization_barrier((second, first, low))
    upper = jnp.where((me[0] // 2 + me[0]) % 2 == 1, second[split:], first[split:])
    at_end = (me[0] < 2) | (me[0] >= size - 2)
    got_second = send(
        jnp.where(at_end, upper, low), lambda i: turns[1](i) if has_second(i) else partner(i)
    )
    got_third = send(upper, lambda i: partner(i) if has_second(i) else -1)

    sums, *rest = pl.pallas_call(
        prep_kernel,
        in_specs=[smem] + [vmem] * 6 + [hbm] * 3,
        out_specs=[vmem] * 7,
        out_shape=[
            pltpu.VMEM(vectors.shape, f32),
            *[pltpu.VMEM((SPAN * n * rank, columns), bf16) for n in counts],
            *[pltpu.VMEM((n, rank, fars * rank), bf16) for n in counts],
        ],
        scratch_shapes=[
            *[pltpu.VMEM((n, fars, rank, rank), bf16) for n in counts],
            pltpu.SemaphoreType.DMA((sum(n // 4 for n in counts),)),
            pltpu.SemaphoreType.DMA((12,)),
        ],
        compiler_params=pltpu.CompilerParams(vmem_limit_bytes=16 * MIB),
        cost_estimate=pl.CostEstimate(
            flops=4 * 10**9,
            bytes_accessed=4 * nodes * fars * rank * rank,
            transcendentals=0,
        ),
        name="prep",
    )(
        me, plain, from_pair, first, second, near, edge,
        *in_hbm(couple_zero, couple_one, couple_two),
    )
    windows, wides = rest[:3], rest[3:]

    out, *_ = pl.pallas_call(
        functools.partial(far_kernel, size=size),
        in_specs=[smem] * 4 + [vmem] * 15,
        out_specs=[hbm] + [vmem] * 3,
        out_shape=[
            jax.ShapeDtypeStruct(vectors.shape, bf16),
            *[pltpu.VMEM((SPAN * n * rank, columns), bf16) for n in counts],
        ],
        input_output_aliases={16: 1, 17: 2, 18: 3},
        scratch_shapes=[
            pltpu.VMEM(vectors.shape, f32),
            pltpu.VMEM(vectors.shape, bf16),
            pltpu.VMEM((LEAF, columns), bf16),
            pltpu.VMEM((nodes * rank, columns), f32),
            pltpu.VMEM((nodes * rank, columns), bf16),
            pltpu.SemaphoreType.DMA((3,)),
            pltpu.SemaphoreType.DMA((leaves // 4,)),
        ],
        compiler_params=pltpu.CompilerParams(vmem_limit_bytes=16 * MIB),
        name="far_down",
    )(
        me, far_zero, far_one, far_two, points, got_first, got_second, got_third, sums, edge,
        basis_t, up_one, up_two, *wides, *windows,
    )
    return out


def solution(mesh):
    placed = (
        P(("groups", "space"), "rhs"),
        P("space", None, None, None),
        P("space", None),
        P("space", None, None),
        P("space", None, None),
        P("space", None, None),
        P("space", None, None, None),
        P("space", None, None, None),
        P("space", None, None, None),
        P("space", None),
        P("space", None),
        P("space", None),
    )
    return jax.shard_map(
        body, mesh=mesh, in_specs=placed, out_specs=P(("groups", "space"), "rhs"), check_vma=False
    )
```

```python
import functools

import jax
import jax.numpy as jnp
from jax import lax
from jax.experimental import pallas as pl
from jax.experimental.pallas import tpu as pltpu
from jax.sharding import PartitionSpec as P

LEAF = 256
REACH = 2
SPAN = 2 * REACH + 1
DEPTH = 3
MIB = 1024 * 1024


def dot(a, b):
    return jnp.dot(a, b, preferred_element_type=jnp.float32)


def dot_t(a, b):
    return lax.dot_general(a, b, (((0,), (0,)), ((), ())), preferred_element_type=jnp.float32)


def up_kernel(
    me_ref, x_hbm, basis_hbm, up_one_hbm, up_two_hbm, plain_ref, pair_ref,
    x_ref, basis_ref, up_one_ref, up_two_ref, sems,
):
    leaves, rank = basis_ref.shape[:2]
    steps = leaves // 4
    copies = []
    for q in range(steps):
        rows = pl.ds(q * 4 * LEAF, 4 * LEAF)
        some = pl.ds(q * 4, 4)
        copies.append(
            (
                pltpu.make_async_copy(x_hbm.at[rows, :], x_ref.at[rows, :], sems.at[2 * q]),
                pltpu.make_async_copy(basis_hbm.at[some], basis_ref.at[some], sems.at[2 * q + 1]),
            )
        )
    ups = (
        pltpu.make_async_copy(up_one_hbm, up_one_ref, sems.at[2 * steps]),
        pltpu.make_async_copy(up_two_hbm, up_two_ref, sems.at[2 * steps + 1]),
    )
    for pair in (*copies, ups):
        for copy in pair:
            copy.start()

    def put(node, value):
        value = value.astype(jnp.bfloat16)
        plain_ref[pl.ds(node * rank, rank), :] = value
        pair_ref[pl.ds(node * rank, rank), :] = value
        return value

    def join(ups, pair):
        return dot_t(ups.reshape(2 * rank, rank), jnp.concatenate(pair, axis=0))

    zeros = []
    for q in range(steps):
        for copy in copies[q]:
            copy.wait()
        for leaf in range(4 * q, 4 * q + 4):
            coef = dot(basis_ref[leaf], x_ref[pl.ds(leaf * LEAF, LEAF), :])
            zeros.append(put(leaf, coef))
    for copy in ups:
        copy.wait()
    ones = []
    for p in range(leaves // 2):
        pair = slice(2 * p, 2 * p + 2)
        ones.append(put(leaves + p, join(up_one_ref[pair], zeros[pair])))
    for q in range(leaves // 4):
        pair = slice(2 * q, 2 * q + 2)
        put(leaves + leaves // 2 + q, join(up_two_ref[pair], ones[pair]))
    odd = lax.rem(me_ref[0], 2)
    last = (leaves - 1) * LEAF
    end = pl.ds(plain_ref.shape[0] - LEAF, LEAF)
    pair_ref[end, :] = x_ref[pl.ds(pl.multiple_of((1 - odd) * last, LEAF), LEAF), :]
    plain_ref[end, :] = x_ref[pl.ds(pl.multiple_of(odd * last, LEAF), LEAF), :]


def last_place(me):
    return REACH - 1 + 2 * lax.rem(me, 2)


def near_kernel(
    me_ref, near_hbm, zero_hbm, one_hbm, two_hbm, x_hbm, blocks_hbm,
    out_ref, edge_ref, x_ref, starts_ref, turns_ref,
    list_ref, zero_list, one_list, two_list, block_buf, sems, x_sems, list_sems,
):
    leaves, nears = list_ref.shape
    ones, twos = one_list.shape[0], two_list.shape[0]
    me = me_ref[0]
    first = me * leaves
    depth = block_buf.shape[0]

    def copies(pair, slot):
        both = pl.ds(2 * pair, 2)
        pairs = (
            (blocks_hbm.at[both, pl.ds(0, 1)], block_buf.at[slot, :, pl.ds(0, 1)]),
            (blocks_hbm.at[both, pl.ds(3, nears - 3)], block_buf.at[slot, :, pl.ds(1, nears - 3)]),
            (blocks_hbm.at[both, pl.ds(1, 2)], edge_ref.at[both]),
        )
        return [
            pltpu.make_async_copy(src, dst, sems.at[slot, i]) for i, (src, dst) in enumerate(pairs)
        ]

    hbms = (near_hbm, zero_hbm, one_hbm, two_hbm)
    lists = (list_ref, zero_list, one_list, two_list)
    list_copies = [
        pltpu.make_async_copy(src, dst, list_sems.at[i])
        for i, (src, dst) in enumerate(zip(hbms, lists))
    ]
    for copy in list_copies:
        copy.start()
    x_copies = []
    for q in range(leaves // 4):
        rows = pl.ds(q * 4 * LEAF, 4 * LEAF)
        x_copies.append(
            pltpu.make_async_copy(x_hbm.at[rows, :], x_ref.at[rows, :], x_sems.at[q])
        )
    for copy in x_copies:
        copy.start()
    for pair in range(depth - 1):
        for copy in copies(pair, pair):
            copy.start()
    for copy in list_copies:
        copy.wait()

    def order(where, node, row):
        per, fars = where.shape
        base = (me - REACH) * per
        low = last_place(me) * per
        count = jnp.int32(0)
        for k in range(fars):
            index = where[node, k] - base
            late = (index >= low) & (index < low + per)
            at = jnp.where(late, count, fars - 1 - k + count)
            starts_ref[row, at] = index
            turns_ref[row, at] = k
            count = count + late.astype(jnp.int32)
        return count

    most = jnp.int32(0)
    for p in range(ones):
        most = jnp.maximum(most, order(one_list, p, leaves + p))
    for q in range(twos):
        most = jnp.maximum(most, order(two_list, q, leaves + ones + q))
    for copy in x_copies:
        copy.wait()

    def step(pair, most):
        slot = lax.rem(pair, depth)

        @pl.when(pair + depth - 1 < leaves // 2)
        def _():
            for copy in copies(pair + depth - 1, lax.rem(pair + depth - 1, depth)):
                copy.start()

        for copy in copies(pair, slot):
            copy.wait()
        totals = []
        for side in range(2):
            rows = []
            for k in (0, *range(3, nears)):
                start = (list_ref[2 * pair + side, k] - first) * LEAF
                rows.append(x_ref[pl.ds(pl.multiple_of(start, LEAF), LEAF), :])
            blocks = [block_buf[slot, side, k] for k in range(nears - 2)]
            totals.append(dot(jnp.concatenate(blocks, axis=1), jnp.concatenate(rows, axis=0)))
        here = pl.ds(pl.multiple_of(pair * 2 * LEAF, 2 * LEAF), 2 * LEAF)
        out_ref[here, :] = jnp.concatenate(totals, axis=0)
        for side in range(2):
            leaf = 2 * pair + side
            most = jnp.maximum(most, order(zero_list, leaf, leaf))
        return most

    starts_ref[leaves + ones + twos, 0] = lax.fori_loop(0, leaves // 2, step, most)


def add_edge(sum_ref, near_ref, edge_ref, side, rows):
    for leaf in range(edge_ref.shape[0]):
        here = pl.ds(leaf * LEAF, LEAF)
        sum_ref[here, :] = near_ref[here, :] + dot(edge_ref[leaf, side], rows)


def window_copies(plans, sems):
    copies = []
    for ref, start, win, at, size in plans:
        copies.append(
            pltpu.make_async_copy(
                ref.at[pl.ds(start, size), :], win.at[pl.ds(at, size), :], sems.at[len(copies)]
            )
        )
    return copies


def field(wide, starts_ref, row, win, slots):
    rank = wide.shape[0]
    rows = []
    for k in slots:
        rows.append(win[pl.ds(pl.multiple_of(starts_ref[row, k] * rank, rank), rank), :])
    some = wide[:, slots[0] * rank : (slots[-1] + 1) * rank]
    return dot(some, jnp.concatenate(rows, axis=0))


def prep_kernel(
    me_ref, starts_ref, turns_ref, own_ref, pair_ref, first_ref, second_ref, near_ref, edge_ref,
    zero_hbm, one_hbm, two_hbm,
    sum_ref, zero_win, one_win, two_win, zero_wide, one_wide, two_wide, part_ref,
    zero_buf, one_buf, two_buf, sems, win_sems,
):
    leaves, fars, rank = zero_buf.shape[:3]
    base = leaves + one_buf.shape[0]
    levels = (
        (two_hbm, two_buf, two_wide, two_win, base),
        (one_hbm, one_buf, one_wide, one_win, leaves),
        (zero_hbm, zero_buf, zero_wide, zero_win, 0),
    )
    chunks = []
    for hbm, buf, wide, _, row in levels:
        for first in range(0, buf.shape[0], 4):
            some = pl.ds(first, 4)
            copy = pltpu.make_async_copy(hbm.at[some], buf.at[some], sems.at[len(chunks)])
            copy.start()
            chunks.append((copy, buf, wide, first, row))
    me = me_ref[0]
    odd = lax.rem(me, 2)
    block = lax.rem(me // 2, 2)
    pieces = (
        (own_ref, 0, REACH),
        (first_ref, 0, (1 - block) * (SPAN - 1)),
        (second_ref, 0, block * (SPAN - 1)),
        (pair_ref, 0, REACH + 1 - 2 * odd),
    )
    plans = []
    for ref, start, place in pieces:
        for win in (zero_win, one_win, two_win):
            size = win.shape[0] // SPAN
            plans.append((ref, start, win, pl.multiple_of(place * size, size), size))
            start += size
    moves = window_copies(plans, win_sems)
    for move in moves:
        move.start()
    add_edge(sum_ref, near_ref, edge_ref, odd, pair_ref[pl.ds(pair_ref.shape[0] - LEAF, LEAF), :])
    for copy, buf, wide, first, row in chunks:
        copy.wait()
        for node in range(first, first + 4):
            picked = [buf[node, turns_ref[row + node, k]] for k in range(fars)]
            wide[node] = jnp.concatenate(picked, axis=1)
    for move in moves:
        move.wait()
    for _, _, wide, win, row in levels:
        for node in range(wide.shape[0]):
            part = field(wide.at[node], starts_ref, row + node, win, range(fars // 2, fars))
            part_ref[pl.ds((row + node) * rank, rank), :] = part


def far_kernel(
    me_ref, starts_ref, x_ref, got_first, got_second, got_third, near_ref,
    edge_ref, basis_ref, up_one_ref, up_two_ref, zero_wide, one_wide, two_wide, part_ref,
    zero_in, one_in, two_in, out_hbm, zero_win, one_win, two_win,
    sum_buf, out_buf, rows_buf, field_buf, down_buf, win_sems, out_sems, *, size,
):
    del zero_in, one_in, two_in
    leaves, rank, deep = zero_wide.shape
    ones, twos = leaves // 2, leaves // 4
    fars = deep // rank
    me = me_ref[0]
    odd = lax.rem(me, 2)
    place = last_place(me)
    sizes = [n * rank for n in (leaves, ones, twos)]
    at = [pl.multiple_of(place * n, n) for n in sizes]

    def arrivals(low_ref, high_ref):
        plans = (
            (low_ref, 0, zero_win, at[0], sizes[0]),
            (high_ref, 0, one_win, at[1], sizes[1]),
            (high_ref, sizes[1], two_win, at[2], sizes[2]),
        )
        return window_copies(plans, win_sems)

    end = pl.ds(got_first.shape[0] - LEAF, LEAF)
    low_first = lax.rem(me + me // 2, 2) == 1
    at_end = (me < 2) | (me >= size - 2)

    def take(low_ref, high_ref):
        def _():
            for move in arrivals(low_ref, high_ref):
                move.start()
            rows_buf[...] = high_ref[end, :]

        return _

    pl.when(low_first & at_end)(take(got_first, got_second))
    pl.when(low_first & jnp.logical_not(at_end))(take(got_first, got_third))
    pl.when(jnp.logical_not(low_first))(take(got_second, got_third))
    moves = arrivals(got_first, got_second)

    alone = (me == 0) | (me == size - 1)

    @pl.when(alone)
    def _():
        for leaf in range(leaves):
            here = pl.ds(leaf * LEAF, LEAF)
            sum_buf[here, :] = near_ref[here, :] + dot(edge_ref[leaf, 1 - odd], x_ref[here, :])

    @pl.when(jnp.logical_not(alone))
    def _():
        add_edge(sum_buf, near_ref, edge_ref, 1 - odd, rows_buf[...])

    for move in moves:
        move.wait()

    def node_rows(row):
        return pl.ds(row * rank, rank)

    base = leaves + ones
    half = fars // 2
    levels = ((two_wide, two_win, base), (one_wide, one_win, leaves), (zero_wide, zero_win, 0))
    for wide, win, row in levels:
        for node in range(wide.shape[0]):
            part = field(wide.at[node], starts_ref, row + node, win, range(half))
            rows = node_rows(row + node)
            field_buf[rows, :] = part_ref[rows, :] + part

    @pl.when(starts_ref[base + twos, 0] > half)
    def _():
        for wide, win, row in levels:

            def again(node, carry):
                part = field(wide.at[node], starts_ref, row + node, win, range(fars))
                field_buf[pl.ds(pl.multiple_of((row + node) * rank, rank), rank), :] = part
                return carry

            lax.fori_loop(0, wide.shape[0], again, 0)

    for q in range(twos):
        down_buf[node_rows(base + q), :] = field_buf[node_rows(base + q), :].astype(jnp.bfloat16)
    for p in range(ones):
        total = dot(up_two_ref[p], down_buf[node_rows(base + p // 2), :])
        total = total + field_buf[node_rows(leaves + p), :]
        down_buf[node_rows(leaves + p), :] = total.astype(jnp.bfloat16)
    for leaf in range(leaves):
        total = dot(up_one_ref[leaf], down_buf[node_rows(leaves + leaf // 2), :])
        total = total + field_buf[node_rows(leaf), :]
        down_buf[node_rows(leaf), :] = total.astype(jnp.bfloat16)
    outs = []
    for leaf in range(leaves):
        here = pl.ds(leaf * LEAF, LEAF)
        total = sum_buf[here, :] + dot_t(basis_ref[leaf], down_buf[node_rows(leaf), :])
        out_buf[here, :] = total.astype(jnp.bfloat16)
        if leaf % 4 == 3:
            some = pl.ds((leaf - 3) * LEAF, 4 * LEAF)
            outs.append(
                pltpu.make_async_copy(
                    out_buf.at[some, :], out_hbm.at[some, :], out_sems.at[leaf // 4]
                )
            )
            outs[-1].start()
    for copy in outs:
        copy.wait()


def body(
    vectors,
    near_blocks,
    near_list,
    basis,
    up_one,
    up_two,
    couple_zero,
    couple_one,
    couple_two,
    far_zero,
    far_one,
    far_two,
):
    leaves, nears = near_list.shape
    columns = vectors.shape[1]
    rank = basis.shape[2]
    fars = far_zero.shape[1]
    size = lax.axis_size("space")
    cores = lax.axis_size("rhs")
    me = lax.axis_index("space").astype(jnp.int32).reshape(1)
    counts = (leaves, leaves // 2, leaves // 4)
    nodes = sum(counts)
    basis_t = jnp.swapaxes(basis, 1, 2)
    bf16, f32 = jnp.bfloat16, jnp.float32

    hbm = pl.BlockSpec(memory_space=pltpu.HBM)
    vmem = pl.BlockSpec(memory_space=pltpu.VMEM)
    smem = pl.BlockSpec(memory_space=pltpu.SMEM)

    def in_hbm(*arrays):
        return [pltpu.with_memory_space_constraint(a, pltpu.HBM) for a in arrays]

    plain, pair = pl.pallas_call(
        up_kernel,
        in_specs=[smem] + [hbm] * 4,
        out_specs=[vmem] * 2,
        out_shape=[
            pltpu.VMEM((nodes * rank + LEAF, columns), bf16),
            pltpu.VMEM((nodes * rank + LEAF, columns), bf16),
        ],
        scratch_shapes=[
            pltpu.VMEM(vectors.shape, bf16),
            pltpu.VMEM(basis_t.shape, bf16),
            pltpu.VMEM(up_one.shape, bf16),
            pltpu.VMEM(up_two.shape, bf16),
            pltpu.SemaphoreType.DMA((leaves // 2 + 2,)),
        ],
        compiler_params=pltpu.CompilerParams(vmem_limit_bytes=8 * MIB),
        name="up_pass",
    )(me, *in_hbm(vectors, basis_t, up_one, up_two))

    def send(array, to):
        pairs = []
        for i in range(size):
            for c in range(cores):
                j, d = (to(i), c) if 0 <= to(i) < size else (i, cores - 1 - c)
                pairs.append((i * cores + c, j * cores + d))
        return lax.ppermute(array, ("space", "rhs"), pairs)

    def partner(i):
        return i + 1 - 2 * (i % 2)

    from_pair = send(pair, partner)
    turns = (lambda i: i + 2 - i // 2 % 2 * 4, lambda i: i - 2 + i // 2 % 2 * 4)
    first, second = [send(plain, turn) for turn in turns]

    near, edge, points, starts, turns_taken = pl.pallas_call(
        near_kernel,
        in_specs=[smem] + [hbm] * 6,
        out_specs=[vmem] * 3 + [smem] * 2,
        out_shape=[
            pltpu.VMEM(vectors.shape, f32),
            pltpu.VMEM((leaves, 2, LEAF, LEAF), bf16),
            pltpu.VMEM(vectors.shape, bf16),
            jax.ShapeDtypeStruct((nodes + 1, fars), jnp.int32),
            jax.ShapeDtypeStruct((nodes + 1, fars), jnp.int32),
        ],
        scratch_shapes=[
            *[pltpu.SMEM(a.shape, jnp.int32) for a in (near_list, far_zero, far_one, far_two)],
            pltpu.VMEM((DEPTH, 2, nears - 2, LEAF, LEAF), bf16),
            pltpu.SemaphoreType.DMA((DEPTH, 3)),
            pltpu.SemaphoreType.DMA((leaves // 4,)),
            pltpu.SemaphoreType.DMA((4,)),
        ],
        compiler_params=pltpu.CompilerParams(vmem_limit_bytes=16 * MIB),
        cost_estimate=pl.CostEstimate(
            flops=2 * leaves * (nears - 2) * LEAF * LEAF * columns,
            bytes_accessed=2 * leaves * nears * LEAF * LEAF + 6 * leaves * LEAF * columns,
            transcendentals=0,
        ),
        name="near_own",
    )(me, *in_hbm(near_list, far_zero, far_one, far_two, vectors, near_blocks))

    def has_second(i):
        return 0 <= turns[1](i) < size

    split = leaves * rank
    from_pair, near = lax.optimization_barrier((from_pair, near))
    low = lax.optimization_barrier(from_pair[:split])
    got_first = send(low, turns[0])
    second, first, low = lax.optimization_barrier((second, first, low))
    upper = jnp.where((me[0] // 2 + me[0]) % 2 == 1, second[split:], first[split:])
    at_end = (me[0] < 2) | (me[0] >= size - 2)
    got_second = send(
        jnp.where(at_end, upper, low), lambda i: turns[1](i) if has_second(i) else partner(i)
    )
    got_third = send(upper, lambda i: partner(i) if has_second(i) else -1)

    sums, *rest, part = pl.pallas_call(
        prep_kernel,
        in_specs=[smem] * 3 + [vmem] * 6 + [hbm] * 3,
        out_specs=[vmem] * 8,
        out_shape=[
            pltpu.VMEM(vectors.shape, f32),
            *[pltpu.VMEM((SPAN * n * rank, columns), bf16) for n in counts],
            *[pltpu.VMEM((n, rank, fars * rank), bf16) for n in counts],
            pltpu.VMEM((nodes * rank, columns), f32),
        ],
        scratch_shapes=[
            *[pltpu.VMEM((n, fars, rank, rank), bf16) for n in counts],
            pltpu.SemaphoreType.DMA((sum(n // 4 for n in counts),)),
            pltpu.SemaphoreType.DMA((12,)),
        ],
        compiler_params=pltpu.CompilerParams(vmem_limit_bytes=16 * MIB),
        cost_estimate=pl.CostEstimate(
            flops=4 * 10**9,
            bytes_accessed=4 * nodes * fars * rank * rank,
            transcendentals=0,
        ),
        name="prep",
    )(
        me, starts, turns_taken, plain, from_pair, first, second, near, edge,
        *in_hbm(couple_zero, couple_one, couple_two),
    )
    windows, wides = rest[:3], rest[3:]

    out, *_ = pl.pallas_call(
        functools.partial(far_kernel, size=size),
        in_specs=[smem] * 2 + [vmem] * 16,
        out_specs=[hbm] + [vmem] * 3,
        out_shape=[
            jax.ShapeDtypeStruct(vectors.shape, bf16),
            *[pltpu.VMEM((SPAN * n * rank, columns), bf16) for n in counts],
        ],
        input_output_aliases={15: 1, 16: 2, 17: 3},
        scratch_shapes=[
            pltpu.VMEM(vectors.shape, f32),
            pltpu.VMEM(vectors.shape, bf16),
            pltpu.VMEM((LEAF, columns), bf16),
            pltpu.VMEM((nodes * rank, columns), f32),
            pltpu.VMEM((nodes * rank, columns), bf16),
            pltpu.SemaphoreType.DMA((3,)),
            pltpu.SemaphoreType.DMA((leaves // 4,)),
        ],
        compiler_params=pltpu.CompilerParams(vmem_limit_bytes=16 * MIB),
        name="far_down",
    )(
        me, starts, points, got_first, got_second, got_third, sums, edge,
        basis_t, up_one, up_two, *wides, part, *windows,
    )
    return out


def solution(mesh):
    placed = (
        P(("groups", "space"), "rhs"),
        P("space", None, None, None),
        P("space", None),
        P("space", None, None),
        P("space", None, None),
        P("space", None, None),
        P("space", None, None, None),
        P("space", None, None, None),
        P("space", None, None, None),
        P("space", None),
        P("space", None),
        P("space", None),
    )
    return jax.shard_map(
        body, mesh=mesh, in_specs=placed, out_specs=P(("groups", "space"), "rhs"), check_vma=False
    )
```

```python
import functools

import jax
import jax.numpy as jnp
from jax import lax
from jax.experimental import pallas as pl
from jax.experimental.pallas import tpu as pltpu
from jax.sharding import PartitionSpec as P

LEAF = 256
REACH = 2
SPAN = 2 * REACH + 1
DEPTH = 3
MIB = 1024 * 1024


def dot(a, b):
    return jnp.dot(a, b, preferred_element_type=jnp.float32)


def dot_t(a, b):
    return lax.dot_general(a, b, (((0,), (0,)), ((), ())), preferred_element_type=jnp.float32)


def up_kernel(
    me_ref, x_hbm, basis_hbm, up_one_hbm, up_two_hbm, plain_ref, pair_ref,
    x_ref, basis_ref, up_one_ref, up_two_ref, sems,
):
    leaves, rank = basis_ref.shape[:2]
    steps = leaves // 4
    copies = []
    for q in range(steps):
        rows = pl.ds(q * 4 * LEAF, 4 * LEAF)
        some = pl.ds(q * 4, 4)
        copies.append(
            (
                pltpu.make_async_copy(x_hbm.at[rows, :], x_ref.at[rows, :], sems.at[2 * q]),
                pltpu.make_async_copy(basis_hbm.at[some], basis_ref.at[some], sems.at[2 * q + 1]),
            )
        )
    ups = (
        pltpu.make_async_copy(up_one_hbm, up_one_ref, sems.at[2 * steps]),
        pltpu.make_async_copy(up_two_hbm, up_two_ref, sems.at[2 * steps + 1]),
    )
    for pair in (*copies, ups):
        for copy in pair:
            copy.start()

    def put(node, value):
        value = value.astype(jnp.bfloat16)
        plain_ref[pl.ds(node * rank, rank), :] = value
        pair_ref[pl.ds(node * rank, rank), :] = value
        return value

    def join(ups, pair):
        return dot_t(ups.reshape(2 * rank, rank), jnp.concatenate(pair, axis=0))

    zeros = []
    for q in range(steps):
        for copy in copies[q]:
            copy.wait()
        for leaf in range(4 * q, 4 * q + 4):
            coef = dot(basis_ref[leaf], x_ref[pl.ds(leaf * LEAF, LEAF), :])
            zeros.append(put(leaf, coef))
    for copy in ups:
        copy.wait()
    ones = []
    for p in range(leaves // 2):
        pair = slice(2 * p, 2 * p + 2)
        ones.append(put(leaves + p, join(up_one_ref[pair], zeros[pair])))
    for q in range(leaves // 4):
        pair = slice(2 * q, 2 * q + 2)
        put(leaves + leaves // 2 + q, join(up_two_ref[pair], ones[pair]))
    odd = lax.rem(me_ref[0], 2)
    last = (leaves - 1) * LEAF
    end = pl.ds(plain_ref.shape[0] - LEAF, LEAF)
    pair_ref[end, :] = x_ref[pl.ds(pl.multiple_of((1 - odd) * last, LEAF), LEAF), :]
    plain_ref[end, :] = x_ref[pl.ds(pl.multiple_of(odd * last, LEAF), LEAF), :]


def last_place(me):
    return REACH - 1 + 2 * lax.rem(me, 2)


def near_kernel(
    me_ref, near_hbm, zero_hbm, one_hbm, two_hbm, x_hbm, blocks_hbm,
    out_ref, edge_ref, x_ref, starts_ref, turns_ref,
    list_ref, zero_list, one_list, two_list, block_buf, sems, x_sems, list_sems,
):
    leaves, nears = list_ref.shape
    ones, twos = one_list.shape[0], two_list.shape[0]
    me = me_ref[0]
    first = me * leaves
    depth = block_buf.shape[0]

    def copies(pair, slot):
        both = pl.ds(2 * pair, 2)
        pairs = (
            (blocks_hbm.at[both, pl.ds(0, 1)], block_buf.at[slot, :, pl.ds(0, 1)]),
            (blocks_hbm.at[both, pl.ds(3, nears - 3)], block_buf.at[slot, :, pl.ds(1, nears - 3)]),
            (blocks_hbm.at[both, pl.ds(1, 2)], edge_ref.at[both]),
        )
        return [
            pltpu.make_async_copy(src, dst, sems.at[slot, i]) for i, (src, dst) in enumerate(pairs)
        ]

    hbms = (near_hbm, zero_hbm, one_hbm, two_hbm)
    lists = (list_ref, zero_list, one_list, two_list)
    list_copies = [
        pltpu.make_async_copy(src, dst, list_sems.at[i])
        for i, (src, dst) in enumerate(zip(hbms, lists))
    ]
    for copy in list_copies:
        copy.start()
    x_copies = []
    for q in range(leaves // 4):
        rows = pl.ds(q * 4 * LEAF, 4 * LEAF)
        x_copies.append(
            pltpu.make_async_copy(x_hbm.at[rows, :], x_ref.at[rows, :], x_sems.at[q])
        )
    for copy in x_copies:
        copy.start()
    for pair in range(depth - 1):
        for copy in copies(pair, pair):
            copy.start()
    for copy in list_copies:
        copy.wait()

    def order(where, node, row):
        per, fars = where.shape
        base = (me - REACH) * per
        low = last_place(me) * per
        count = jnp.int32(0)
        for k in range(fars):
            index = where[node, k] - base
            late = (index >= low) & (index < low + per)
            at = jnp.where(late, count, fars - 1 - k + count)
            starts_ref[row, at] = index
            turns_ref[row, at] = k
            count = count + late.astype(jnp.int32)
        return count

    most = jnp.int32(0)
    for p in range(ones):
        most = jnp.maximum(most, order(one_list, p, leaves + p))
    for q in range(twos):
        most = jnp.maximum(most, order(two_list, q, leaves + ones + q))
    for copy in x_copies:
        copy.wait()

    def step(pair, most):
        slot = lax.rem(pair, depth)

        @pl.when(pair + depth - 1 < leaves // 2)
        def _():
            for copy in copies(pair + depth - 1, lax.rem(pair + depth - 1, depth)):
                copy.start()

        for copy in copies(pair, slot):
            copy.wait()
        totals = []
        for side in range(2):
            rows = []
            for k in (0, *range(3, nears)):
                start = (list_ref[2 * pair + side, k] - first) * LEAF
                rows.append(x_ref[pl.ds(pl.multiple_of(start, LEAF), LEAF), :])
            blocks = [block_buf[slot, side, k] for k in range(nears - 2)]
            totals.append(dot(jnp.concatenate(blocks, axis=1), jnp.concatenate(rows, axis=0)))
        here = pl.ds(pl.multiple_of(pair * 2 * LEAF, 2 * LEAF), 2 * LEAF)
        out_ref[here, :] = jnp.concatenate(totals, axis=0)
        for side in range(2):
            leaf = 2 * pair + side
            most = jnp.maximum(most, order(zero_list, leaf, leaf))
        return most

    starts_ref[leaves + ones + twos, 0] = lax.fori_loop(0, leaves // 2, step, most)


def add_edge(sum_ref, near_ref, edge_ref, side, rows):
    for leaf in range(edge_ref.shape[0]):
        here = pl.ds(leaf * LEAF, LEAF)
        sum_ref[here, :] = near_ref[here, :] + dot(edge_ref[leaf, side], rows)


def window_copies(plans, sems):
    copies = []
    for ref, start, win, at, size in plans:
        copies.append(
            pltpu.make_async_copy(
                ref.at[pl.ds(start, size), :], win.at[pl.ds(at, size), :], sems.at[len(copies)]
            )
        )
    return copies


def field(wide, starts_ref, row, win, slots):
    rank = wide.shape[0]
    rows = []
    for k in slots:
        rows.append(win[pl.ds(pl.multiple_of(starts_ref[row, k] * rank, rank), rank), :])
    some = wide[:, slots[0] * rank : (slots[-1] + 1) * rank]
    return dot(some, jnp.concatenate(rows, axis=0))


def prep_kernel(
    me_ref, starts_ref, turns_ref, own_ref, pair_ref, first_ref, second_ref, near_ref, edge_ref,
    zero_hbm, one_hbm, two_hbm,
    sum_ref, zero_win, one_win, two_win, zero_wide, one_wide, two_wide, part_ref,
    zero_buf, one_buf, two_buf, sems, win_sems,
):
    leaves, fars, rank = zero_buf.shape[:3]
    base = leaves + one_buf.shape[0]
    levels = (
        (two_hbm, two_buf, two_wide, two_win, base),
        (one_hbm, one_buf, one_wide, one_win, leaves),
        (zero_hbm, zero_buf, zero_wide, zero_win, 0),
    )
    chunks = []
    for hbm, buf, wide, _, row in levels:
        for first in range(0, buf.shape[0], 4):
            some = pl.ds(first, 4)
            copy = pltpu.make_async_copy(hbm.at[some], buf.at[some], sems.at[len(chunks)])
            copy.start()
            chunks.append((copy, buf, wide, first, row))
    me = me_ref[0]
    odd = lax.rem(me, 2)
    block = lax.rem(me // 2, 2)
    pieces = (
        (own_ref, 0, REACH),
        (first_ref, 0, (1 - block) * (SPAN - 1)),
        (second_ref, 0, block * (SPAN - 1)),
        (pair_ref, 0, REACH + 1 - 2 * odd),
    )
    plans = []
    for ref, start, place in pieces:
        for win in (zero_win, one_win, two_win):
            size = win.shape[0] // SPAN
            plans.append((ref, start, win, pl.multiple_of(place * size, size), size))
            start += size
    moves = window_copies(plans, win_sems)
    for move in moves:
        move.start()
    add_edge(sum_ref, near_ref, edge_ref, odd, pair_ref[pl.ds(pair_ref.shape[0] - LEAF, LEAF), :])
    for copy, buf, wide, first, row in chunks:
        copy.wait()
        for node in range(first, first + 4):
            picked = [buf[node, turns_ref[row + node, k]] for k in range(fars)]
            wide[node] = jnp.concatenate(picked, axis=1)
    for move in moves:
        move.wait()
    for _, _, wide, win, row in levels:
        for node in range(wide.shape[0]):
            part = field(wide.at[node], starts_ref, row + node, win, range(fars // 2, fars))
            part_ref[pl.ds((row + node) * rank, rank), :] = part


def far_kernel(
    me_ref, starts_ref, x_ref, got_first, got_second, got_third, near_ref,
    edge_ref, basis_ref, up_one_ref, up_two_ref, zero_wide, one_wide, two_wide, part_ref,
    zero_in, one_in, two_in, out_hbm, zero_win, one_win, two_win,
    sum_buf, out_buf, rows_buf, field_buf, down_buf, win_sems, out_sems, *, size,
):
    del zero_in, one_in, two_in
    leaves, rank, deep = zero_wide.shape
    ones, twos = leaves // 2, leaves // 4
    fars = deep // rank
    me = me_ref[0]
    odd = lax.rem(me, 2)
    place = last_place(me)
    sizes = [n * rank for n in (leaves, ones, twos)]
    at = [pl.multiple_of(place * n, n) for n in sizes]

    def arrivals(low_ref, high_ref):
        plans = (
            (low_ref, 0, zero_win, at[0], sizes[0]),
            (high_ref, 0, one_win, at[1], sizes[1]),
            (high_ref, sizes[1], two_win, at[2], sizes[2]),
        )
        return window_copies(plans, win_sems)

    end = pl.ds(got_first.shape[0] - LEAF, LEAF)
    low_first = lax.rem(me + me // 2, 2) == 1
    at_end = (me < 2) | (me >= size - 2)

    def take(low_ref, high_ref):
        def _():
            for move in arrivals(low_ref, high_ref):
                move.start()
            rows_buf[...] = high_ref[end, :]

        return _

    pl.when(low_first & at_end)(take(got_first, got_second))
    pl.when(low_first & jnp.logical_not(at_end))(take(got_first, got_third))
    pl.when(jnp.logical_not(low_first))(take(got_second, got_third))
    moves = arrivals(got_first, got_second)

    alone = (me == 0) | (me == size - 1)

    @pl.when(alone)
    def _():
        for leaf in range(leaves):
            here = pl.ds(leaf * LEAF, LEAF)
            sum_buf[here, :] = near_ref[here, :] + dot(edge_ref[leaf, 1 - odd], x_ref[here, :])

    @pl.when(jnp.logical_not(alone))
    def _():
        add_edge(sum_buf, near_ref, edge_ref, 1 - odd, rows_buf[...])

    for move in moves:
        move.wait()

    def node_rows(row):
        return pl.ds(row * rank, rank)

    base = leaves + ones
    half = fars // 2
    levels = ((two_wide, two_win, base), (one_wide, one_win, leaves), (zero_wide, zero_win, 0))
    for wide, win, row in levels:
        for node in range(wide.shape[0]):
            part = field(wide.at[node], starts_ref, row + node, win, range(half))
            rows = node_rows(row + node)
            field_buf[rows, :] = part_ref[rows, :] + part

    @pl.when(starts_ref[base + twos, 0] > half)
    def _():
        for wide, win, row in levels:

            def again(node, carry):
                part = field(wide.at[node], starts_ref, row + node, win, range(fars))
                field_buf[pl.ds(pl.multiple_of((row + node) * rank, rank), rank), :] = part
                return carry

            lax.fori_loop(0, wide.shape[0], again, 0)

    for q in range(twos):
        down_buf[node_rows(base + q), :] = field_buf[node_rows(base + q), :].astype(jnp.bfloat16)
    for p in range(ones):
        total = dot(up_two_ref[p], down_buf[node_rows(base + p // 2), :])
        total = total + field_buf[node_rows(leaves + p), :]
        down_buf[node_rows(leaves + p), :] = total.astype(jnp.bfloat16)
    for leaf in range(leaves):
        total = dot(up_one_ref[leaf], down_buf[node_rows(leaves + leaf // 2), :])
        total = total + field_buf[node_rows(leaf), :]
        down_buf[node_rows(leaf), :] = total.astype(jnp.bfloat16)
    outs = []
    for leaf in range(leaves):
        here = pl.ds(leaf * LEAF, LEAF)
        total = sum_buf[here, :] + dot_t(basis_ref[leaf], down_buf[node_rows(leaf), :])
        out_buf[here, :] = total.astype(jnp.bfloat16)
        if leaf % 4 == 3:
            some = pl.ds((leaf - 3) * LEAF, 4 * LEAF)
            outs.append(
                pltpu.make_async_copy(
                    out_buf.at[some, :], out_hbm.at[some, :], out_sems.at[leaf // 4]
                )
            )
            outs[-1].start()
    for copy in outs:
        copy.wait()


def body(
    vectors,
    near_blocks,
    near_list,
    basis,
    up_one,
    up_two,
    couple_zero,
    couple_one,
    couple_two,
    far_zero,
    far_one,
    far_two,
):
    leaves, nears = near_list.shape
    columns = vectors.shape[1]
    rank = basis.shape[2]
    fars = far_zero.shape[1]
    size = lax.axis_size("space")
    cores = lax.axis_size("rhs")
    me = lax.axis_index("space").astype(jnp.int32).reshape(1)
    counts = (leaves, leaves // 2, leaves // 4)
    nodes = sum(counts)
    basis_t = jnp.swapaxes(basis, 1, 2)
    bf16, f32 = jnp.bfloat16, jnp.float32

    hbm = pl.BlockSpec(memory_space=pltpu.HBM)
    vmem = pl.BlockSpec(memory_space=pltpu.VMEM)
    smem = pl.BlockSpec(memory_space=pltpu.SMEM)

    def in_hbm(*arrays):
        return [pltpu.with_memory_space_constraint(a, pltpu.HBM) for a in arrays]

    plain, pair = pl.pallas_call(
        up_kernel,
        in_specs=[smem] + [hbm] * 4,
        out_specs=[vmem] * 2,
        out_shape=[
            pltpu.VMEM((nodes * rank + LEAF, columns), bf16),
            pltpu.VMEM((nodes * rank + LEAF, columns), bf16),
        ],
        scratch_shapes=[
            pltpu.VMEM(vectors.shape, bf16),
            pltpu.VMEM(basis_t.shape, bf16),
            pltpu.VMEM(up_one.shape, bf16),
            pltpu.VMEM(up_two.shape, bf16),
            pltpu.SemaphoreType.DMA((leaves // 2 + 2,)),
        ],
        compiler_params=pltpu.CompilerParams(vmem_limit_bytes=8 * MIB),
        name="up_pass",
    )(me, *in_hbm(vectors, basis_t, up_one, up_two))

    def send(array, to):
        pairs = []
        for i in range(size):
            for c in range(cores):
                j, d = (to(i), c) if 0 <= to(i) < size else (i, cores - 1 - c)
                pairs.append((i * cores + c, j * cores + d))
        return lax.ppermute(array, ("space", "rhs"), pairs)

    def partner(i):
        return i + 1 - 2 * (i % 2)

    from_pair = send(pair, partner)
    turns = (lambda i: i + 2 - i // 2 % 2 * 4, lambda i: i - 2 + i // 2 % 2 * 4)
    first, second = [send(plain, turn) for turn in turns]

    near, edge, points, starts, turns_taken = pl.pallas_call(
        near_kernel,
        in_specs=[smem] + [hbm] * 6,
        out_specs=[vmem] * 3 + [smem] * 2,
        out_shape=[
            pltpu.VMEM(vectors.shape, f32),
            pltpu.VMEM((leaves, 2, LEAF, LEAF), bf16),
            pltpu.VMEM(vectors.shape, bf16),
            jax.ShapeDtypeStruct((nodes + 1, fars), jnp.int32),
            jax.ShapeDtypeStruct((nodes + 1, fars), jnp.int32),
        ],
        scratch_shapes=[
            *[pltpu.SMEM(a.shape, jnp.int32) for a in (near_list, far_zero, far_one, far_two)],
            pltpu.VMEM((DEPTH, 2, nears - 2, LEAF, LEAF), bf16),
            pltpu.SemaphoreType.DMA((DEPTH, 3)),
            pltpu.SemaphoreType.DMA((leaves // 4,)),
            pltpu.SemaphoreType.DMA((4,)),
        ],
        compiler_params=pltpu.CompilerParams(vmem_limit_bytes=16 * MIB),
        cost_estimate=pl.CostEstimate(
            flops=2 * leaves * (nears - 2) * LEAF * LEAF * columns,
            bytes_accessed=2 * leaves * nears * LEAF * LEAF + 6 * leaves * LEAF * columns,
            transcendentals=0,
        ),
        name="near_own",
    )(me, *in_hbm(near_list, far_zero, far_one, far_two, vectors, near_blocks))

    def has_second(i):
        return 0 <= turns[1](i) < size

    split = leaves * rank
    second, first, from_pair, near = lax.optimization_barrier((second, first, from_pair, near))
    low = from_pair[:split]
    got_first = send(low, turns[0])
    upper = jnp.where((me[0] // 2 + me[0]) % 2 == 1, second[split:], first[split:])
    at_end = (me[0] < 2) | (me[0] >= size - 2)
    got_second = send(
        jnp.where(at_end, upper, low), lambda i: turns[1](i) if has_second(i) else partner(i)
    )
    got_third = send(upper, lambda i: partner(i) if has_second(i) else -1)

    sums, *rest, part = pl.pallas_call(
        prep_kernel,
        in_specs=[smem] * 3 + [vmem] * 6 + [hbm] * 3,
        out_specs=[vmem] * 8,
        out_shape=[
            pltpu.VMEM(vectors.shape, f32),
            *[pltpu.VMEM((SPAN * n * rank, columns), bf16) for n in counts],
            *[pltpu.VMEM((n, rank, fars * rank), bf16) for n in counts],
            pltpu.VMEM((nodes * rank, columns), f32),
        ],
        scratch_shapes=[
            *[pltpu.VMEM((n, fars, rank, rank), bf16) for n in counts],
            pltpu.SemaphoreType.DMA((sum(n // 4 for n in counts),)),
            pltpu.SemaphoreType.DMA((12,)),
        ],
        compiler_params=pltpu.CompilerParams(vmem_limit_bytes=16 * MIB),
        cost_estimate=pl.CostEstimate(
            flops=4 * 10**9,
            bytes_accessed=4 * nodes * fars * rank * rank,
            transcendentals=0,
        ),
        name="prep",
    )(
        me, starts, turns_taken, plain, from_pair, first, second, near, edge,
        *in_hbm(couple_zero, couple_one, couple_two),
    )
    windows, wides = rest[:3], rest[3:]

    out, *_ = pl.pallas_call(
        functools.partial(far_kernel, size=size),
        in_specs=[smem] * 2 + [vmem] * 16,
        out_specs=[hbm] + [vmem] * 3,
        out_shape=[
            jax.ShapeDtypeStruct(vectors.shape, bf16),
            *[pltpu.VMEM((SPAN * n * rank, columns), bf16) for n in counts],
        ],
        input_output_aliases={15: 1, 16: 2, 17: 3},
        scratch_shapes=[
            pltpu.VMEM(vectors.shape, f32),
            pltpu.VMEM(vectors.shape, bf16),
            pltpu.VMEM((LEAF, columns), bf16),
            pltpu.VMEM((nodes * rank, columns), f32),
            pltpu.VMEM((nodes * rank, columns), bf16),
            pltpu.SemaphoreType.DMA((3,)),
            pltpu.SemaphoreType.DMA((leaves // 4,)),
        ],
        compiler_params=pltpu.CompilerParams(vmem_limit_bytes=16 * MIB),
        name="far_down",
    )(
        me, starts, points, got_first, got_second, got_third, sums, edge,
        basis_t, up_one, up_two, *wides, part, *windows,
    )
    return out


def solution(mesh):
    placed = (
        P(("groups", "space"), "rhs"),
        P("space", None, None, None),
        P("space", None),
        P("space", None, None),
        P("space", None, None),
        P("space", None, None),
        P("space", None, None, None),
        P("space", None, None, None),
        P("space", None, None, None),
        P("space", None),
        P("space", None),
        P("space", None),
    )
    return jax.shard_map(
        body, mesh=mesh, in_specs=placed, out_specs=P(("groups", "space"), "rhs"), check_vma=False
    )
```

```python
import functools

import jax
import jax.numpy as jnp
from jax import lax
from jax.experimental import pallas as pl
from jax.experimental.pallas import tpu as pltpu
from jax.sharding import PartitionSpec as P

LEAF = 256
REACH = 2
SPAN = 2 * REACH + 1
DEPTH = 3
MIB = 1024 * 1024


def dot(a, b):
    return jnp.dot(a, b, preferred_element_type=jnp.float32)


def dot_t(a, b):
    return lax.dot_general(a, b, (((0,), (0,)), ((), ())), preferred_element_type=jnp.float32)


def up_kernel(
    me_ref, x_hbm, basis_hbm, up_one_hbm, up_two_hbm, plain_ref, pair_ref,
    x_ref, basis_ref, up_one_ref, up_two_ref, sems,
):
    leaves, rank = basis_ref.shape[:2]
    steps = leaves // 4
    copies = []
    for q in range(steps):
        rows = pl.ds(q * 4 * LEAF, 4 * LEAF)
        some = pl.ds(q * 4, 4)
        copies.append(
            (
                pltpu.make_async_copy(x_hbm.at[rows, :], x_ref.at[rows, :], sems.at[2 * q]),
                pltpu.make_async_copy(basis_hbm.at[some], basis_ref.at[some], sems.at[2 * q + 1]),
            )
        )
    ups = (
        pltpu.make_async_copy(up_one_hbm, up_one_ref, sems.at[2 * steps]),
        pltpu.make_async_copy(up_two_hbm, up_two_ref, sems.at[2 * steps + 1]),
    )
    for pair in (*copies, ups):
        for copy in pair:
            copy.start()

    def put(node, value):
        value = value.astype(jnp.bfloat16)
        plain_ref[pl.ds(node * rank, rank), :] = value
        pair_ref[pl.ds(node * rank, rank), :] = value
        return value

    def join(ups, pair):
        return dot_t(ups.reshape(2 * rank, rank), jnp.concatenate(pair, axis=0))

    zeros = []
    for q in range(steps):
        for copy in copies[q]:
            copy.wait()
        for leaf in range(4 * q, 4 * q + 4):
            coef = dot(basis_ref[leaf], x_ref[pl.ds(leaf * LEAF, LEAF), :])
            zeros.append(put(leaf, coef))
    for copy in ups:
        copy.wait()
    ones = []
    for p in range(leaves // 2):
        pair = slice(2 * p, 2 * p + 2)
        ones.append(put(leaves + p, join(up_one_ref[pair], zeros[pair])))
    for q in range(leaves // 4):
        pair = slice(2 * q, 2 * q + 2)
        put(leaves + leaves // 2 + q, join(up_two_ref[pair], ones[pair]))
    odd = lax.rem(me_ref[0], 2)
    last = (leaves - 1) * LEAF
    end = pl.ds(plain_ref.shape[0] - LEAF, LEAF)
    pair_ref[end, :] = x_ref[pl.ds(pl.multiple_of((1 - odd) * last, LEAF), LEAF), :]
    plain_ref[end, :] = x_ref[pl.ds(pl.multiple_of(odd * last, LEAF), LEAF), :]


def last_place(me):
    return REACH - 1 + 2 * lax.rem(me, 2)


def near_kernel(
    me_ref, near_hbm, zero_hbm, one_hbm, two_hbm, x_hbm, blocks_hbm,
    out_ref, edge_ref, x_ref, starts_ref, turns_ref,
    list_ref, zero_list, one_list, two_list, block_buf, sems, x_sems, list_sems,
):
    leaves, nears = list_ref.shape
    ones, twos = one_list.shape[0], two_list.shape[0]
    me = me_ref[0]
    first = me * leaves
    depth = block_buf.shape[0]

    def copies(pair, slot):
        both = pl.ds(2 * pair, 2)
        pairs = (
            (blocks_hbm.at[both, pl.ds(0, 1)], block_buf.at[slot, :, pl.ds(0, 1)]),
            (blocks_hbm.at[both, pl.ds(3, nears - 3)], block_buf.at[slot, :, pl.ds(1, nears - 3)]),
            (blocks_hbm.at[both, pl.ds(1, 2)], edge_ref.at[both]),
        )
        return [
            pltpu.make_async_copy(src, dst, sems.at[slot, i]) for i, (src, dst) in enumerate(pairs)
        ]

    hbms = (near_hbm, zero_hbm, one_hbm, two_hbm)
    lists = (list_ref, zero_list, one_list, two_list)
    list_copies = [
        pltpu.make_async_copy(src, dst, list_sems.at[i])
        for i, (src, dst) in enumerate(zip(hbms, lists))
    ]
    for copy in list_copies:
        copy.start()
    x_copies = []
    for q in range(leaves // 4):
        rows = pl.ds(q * 4 * LEAF, 4 * LEAF)
        x_copies.append(
            pltpu.make_async_copy(x_hbm.at[rows, :], x_ref.at[rows, :], x_sems.at[q])
        )
    for copy in x_copies:
        copy.start()
    for pair in range(depth - 1):
        for copy in copies(pair, pair):
            copy.start()
    for copy in list_copies:
        copy.wait()

    def order(where, node, row):
        per, fars = where.shape
        base = (me - REACH) * per
        low = last_place(me) * per
        count = jnp.int32(0)
        for k in range(fars):
            index = where[node, k] - base
            late = (index >= low) & (index < low + per)
            at = jnp.where(late, count, fars - 1 - k + count)
            starts_ref[row, at] = index
            turns_ref[row, at] = k
            count = count + late.astype(jnp.int32)
        return count

    most = jnp.int32(0)
    for p in range(ones):
        most = jnp.maximum(most, order(one_list, p, leaves + p))
    for q in range(twos):
        most = jnp.maximum(most, order(two_list, q, leaves + ones + q))
    for copy in x_copies:
        copy.wait()

    def step(pair, most):
        slot = lax.rem(pair, depth)

        @pl.when(pair + depth - 1 < leaves // 2)
        def _():
            for copy in copies(pair + depth - 1, lax.rem(pair + depth - 1, depth)):
                copy.start()

        for copy in copies(pair, slot):
            copy.wait()
        totals = []
        for side in range(2):
            rows = []
            for k in (0, *range(3, nears)):
                start = (list_ref[2 * pair + side, k] - first) * LEAF
                rows.append(x_ref[pl.ds(pl.multiple_of(start, LEAF), LEAF), :])
            blocks = [block_buf[slot, side, k] for k in range(nears - 2)]
            totals.append(dot(jnp.concatenate(blocks, axis=1), jnp.concatenate(rows, axis=0)))
        here = pl.ds(pl.multiple_of(pair * 2 * LEAF, 2 * LEAF), 2 * LEAF)
        out_ref[here, :] = jnp.concatenate(totals, axis=0)
        for side in range(2):
            leaf = 2 * pair + side
            most = jnp.maximum(most, order(zero_list, leaf, leaf))
        return most

    starts_ref[leaves + ones + twos, 0] = lax.fori_loop(0, leaves // 2, step, most)


def add_edge(sum_ref, near_ref, edge_ref, side, rows, leaves):
    for leaf in leaves:
        here = pl.ds(leaf * LEAF, LEAF)
        sum_ref[here, :] = near_ref[here, :] + dot(edge_ref[leaf, side], rows)


def place_piece(ref, start, win, at, size):
    win[pl.ds(at, size), :] = ref[pl.ds(start, size), :]


def field(wide, starts_ref, row, win, slots):
    rank = wide.shape[0]
    rows = []
    for k in slots:
        rows.append(win[pl.ds(pl.multiple_of(starts_ref[row, k] * rank, rank), rank), :])
    some = wide[:, slots[0] * rank : (slots[-1] + 1) * rank]
    return dot(some, jnp.concatenate(rows, axis=0))


def prep_kernel(
    me_ref, starts_ref, turns_ref, own_ref, pair_ref, first_ref, second_ref, near_ref, edge_ref,
    zero_hbm, one_hbm, two_hbm,
    sum_ref, zero_win, one_win, two_win, zero_wide, one_wide, two_wide, part_ref,
    zero_buf, one_buf, two_buf, sems,
):
    leaves, fars, rank = zero_buf.shape[:3]
    base = leaves + one_buf.shape[0]
    levels = (
        (two_hbm, two_buf, two_wide, two_win, base),
        (one_hbm, one_buf, one_wide, one_win, leaves),
        (zero_hbm, zero_buf, zero_wide, zero_win, 0),
    )
    chunks = []
    for hbm, buf, wide, _, row in levels:
        for first in range(0, buf.shape[0], 4):
            some = pl.ds(first, 4)
            copy = pltpu.make_async_copy(hbm.at[some], buf.at[some], sems.at[len(chunks)])
            copy.start()
            chunks.append((copy, buf, wide, first, row))
    me = me_ref[0]
    odd = lax.rem(me, 2)
    block = lax.rem(me // 2, 2)
    pieces = (
        (own_ref, 0, REACH),
        (first_ref, 0, (1 - block) * (SPAN - 1)),
        (second_ref, 0, block * (SPAN - 1)),
        (pair_ref, 0, REACH + 1 - 2 * odd),
    )
    for ref, start, place in pieces:
        for win in (zero_win, one_win, two_win):
            size = win.shape[0] // SPAN
            place_piece(ref, start, win, pl.multiple_of(place * size, size), size)
            start += size
    rows = pair_ref[pl.ds(pair_ref.shape[0] - LEAF, LEAF), :]
    add_edge(sum_ref, near_ref, edge_ref, odd, rows, range(leaves))
    for copy, buf, wide, first, row in chunks:
        copy.wait()
        for node in range(first, first + 4):
            picked = [buf[node, turns_ref[row + node, k]] for k in range(fars)]
            wide[node] = jnp.concatenate(picked, axis=1)
    for _, _, wide, win, row in levels:
        for node in range(wide.shape[0]):
            part = field(wide.at[node], starts_ref, row + node, win, range(fars // 2, fars))
            part_ref[pl.ds((row + node) * rank, rank), :] = part


def far_kernel(
    me_ref, starts_ref, x_ref, got_first, got_second, got_third, sum_in,
    edge_ref, basis_ref, up_one_ref, up_two_ref, zero_wide, one_wide, two_wide, part_ref,
    zero_in, one_in, two_in, out_hbm, sum_ref, zero_win, one_win, two_win,
    out_buf, rows_buf, field_buf, down_buf, out_sems, *, size,
):
    del sum_in, zero_in, one_in, two_in
    leaves, rank, deep = zero_wide.shape
    ones, twos = leaves // 2, leaves // 4
    fars = deep // rank
    me = me_ref[0]
    odd = lax.rem(me, 2)
    place = last_place(me)
    sizes = [n * rank for n in (leaves, ones, twos)]
    at = [pl.multiple_of(place * n, n) for n in sizes]

    end = pl.ds(got_first.shape[0] - LEAF, LEAF)
    low_first = lax.rem(me + me // 2, 2) == 1
    at_end = (me < 2) | (me >= size - 2)

    def take(low_ref, high_ref):
        def _():
            place_piece(low_ref, 0, zero_win, at[0], sizes[0])
            place_piece(high_ref, 0, one_win, at[1], sizes[1])
            place_piece(high_ref, sizes[1], two_win, at[2], sizes[2])
            rows_buf[...] = high_ref[end, :]

        return _

    pl.when(low_first & at_end)(take(got_first, got_second))
    pl.when(low_first & jnp.logical_not(at_end))(take(got_first, got_third))
    pl.when(jnp.logical_not(low_first))(take(got_second, got_third))

    alone = (me == 0) | (me == size - 1)

    @pl.when(alone)
    def _():
        rows_buf[...] = jnp.zeros_like(rows_buf)
        for leaf in range(leaves):
            here = pl.ds(leaf * LEAF, LEAF)
            sum_ref[here, :] += dot(edge_ref[leaf, 1 - odd], x_ref[here, :])

    def node_rows(row):
        return pl.ds(row * rank, rank)

    base = leaves + ones
    half = fars // 2
    levels = ((two_wide, two_win, base), (one_wide, one_win, leaves), (zero_wide, zero_win, 0))
    for wide, win, row in levels:
        for node in range(wide.shape[0]):
            part = field(wide.at[node], starts_ref, row + node, win, range(half))
            rows = node_rows(row + node)
            field_buf[rows, :] = part_ref[rows, :] + part

    @pl.when(starts_ref[base + twos, 0] > half)
    def _():
        for wide, win, row in levels:

            def again(node, carry):
                part = field(wide.at[node], starts_ref, row + node, win, range(fars))
                field_buf[pl.ds(pl.multiple_of((row + node) * rank, rank), rank), :] = part
                return carry

            lax.fori_loop(0, wide.shape[0], again, 0)

    rows = rows_buf[...]
    add_edge(sum_ref, sum_ref, edge_ref, 1 - odd, rows, range(leaves // 2))
    for q in range(twos):
        down_buf[node_rows(base + q), :] = field_buf[node_rows(base + q), :].astype(jnp.bfloat16)
    for p in range(ones):
        total = dot(up_two_ref[p], down_buf[node_rows(base + p // 2), :])
        total = total + field_buf[node_rows(leaves + p), :]
        down_buf[node_rows(leaves + p), :] = total.astype(jnp.bfloat16)
    add_edge(sum_ref, sum_ref, edge_ref, 1 - odd, rows, range(leaves // 2, leaves))
    for leaf in range(leaves):
        total = dot(up_one_ref[leaf], down_buf[node_rows(leaves + leaf // 2), :])
        total = total + field_buf[node_rows(leaf), :]
        down_buf[node_rows(leaf), :] = total.astype(jnp.bfloat16)
    outs = []
    for leaf in range(leaves):
        here = pl.ds(leaf * LEAF, LEAF)
        total = sum_ref[here, :] + dot_t(basis_ref[leaf], down_buf[node_rows(leaf), :])
        out_buf[here, :] = total.astype(jnp.bfloat16)
        if leaf % 2 == 1:
            some = pl.ds((leaf - 1) * LEAF, 2 * LEAF)
            outs.append(
                pltpu.make_async_copy(
                    out_buf.at[some, :], out_hbm.at[some, :], out_sems.at[leaf // 2]
                )
            )
            outs[-1].start()
    for copy in outs:
        copy.wait()


def body(
    vectors,
    near_blocks,
    near_list,
    basis,
    up_one,
    up_two,
    couple_zero,
    couple_one,
    couple_two,
    far_zero,
    far_one,
    far_two,
):
    leaves, nears = near_list.shape
    columns = vectors.shape[1]
    rank = basis.shape[2]
    fars = far_zero.shape[1]
    size = lax.axis_size("space")
    cores = lax.axis_size("rhs")
    me = lax.axis_index("space").astype(jnp.int32).reshape(1)
    counts = (leaves, leaves // 2, leaves // 4)
    nodes = sum(counts)
    basis_t = jnp.swapaxes(basis, 1, 2)
    bf16, f32 = jnp.bfloat16, jnp.float32

    hbm = pl.BlockSpec(memory_space=pltpu.HBM)
    vmem = pl.BlockSpec(memory_space=pltpu.VMEM)
    smem = pl.BlockSpec(memory_space=pltpu.SMEM)

    def in_hbm(*arrays):
        return [pltpu.with_memory_space_constraint(a, pltpu.HBM) for a in arrays]

    plain, pair = pl.pallas_call(
        up_kernel,
        in_specs=[smem] + [hbm] * 4,
        out_specs=[vmem] * 2,
        out_shape=[
            pltpu.VMEM((nodes * rank + LEAF, columns), bf16),
            pltpu.VMEM((nodes * rank + LEAF, columns), bf16),
        ],
        scratch_shapes=[
            pltpu.VMEM(vectors.shape, bf16),
            pltpu.VMEM(basis_t.shape, bf16),
            pltpu.VMEM(up_one.shape, bf16),
            pltpu.VMEM(up_two.shape, bf16),
            pltpu.SemaphoreType.DMA((leaves // 2 + 2,)),
        ],
        compiler_params=pltpu.CompilerParams(vmem_limit_bytes=8 * MIB),
        name="up_pass",
    )(me, *in_hbm(vectors, basis_t, up_one, up_two))

    def send(array, to):
        pairs = []
        for i in range(size):
            for c in range(cores):
                j, d = (to(i), c) if 0 <= to(i) < size else (i, cores - 1 - c)
                pairs.append((i * cores + c, j * cores + d))
        return lax.ppermute(array, ("space", "rhs"), pairs)

    def partner(i):
        return i + 1 - 2 * (i % 2)

    from_pair = send(pair, partner)
    turns = (lambda i: i + 2 - i // 2 % 2 * 4, lambda i: i - 2 + i // 2 % 2 * 4)
    first, second = [send(plain, turn) for turn in turns]

    near, edge, points, starts, turns_taken = pl.pallas_call(
        near_kernel,
        in_specs=[smem] + [hbm] * 6,
        out_specs=[vmem] * 3 + [smem] * 2,
        out_shape=[
            pltpu.VMEM(vectors.shape, f32),
            pltpu.VMEM((leaves, 2, LEAF, LEAF), bf16),
            pltpu.VMEM(vectors.shape, bf16),
            jax.ShapeDtypeStruct((nodes + 1, fars), jnp.int32),
            jax.ShapeDtypeStruct((nodes + 1, fars), jnp.int32),
        ],
        scratch_shapes=[
            *[pltpu.SMEM(a.shape, jnp.int32) for a in (near_list, far_zero, far_one, far_two)],
            pltpu.VMEM((DEPTH, 2, nears - 2, LEAF, LEAF), bf16),
            pltpu.SemaphoreType.DMA((DEPTH, 3)),
            pltpu.SemaphoreType.DMA((leaves // 4,)),
            pltpu.SemaphoreType.DMA((4,)),
        ],
        compiler_params=pltpu.CompilerParams(vmem_limit_bytes=16 * MIB),
        cost_estimate=pl.CostEstimate(
            flops=2 * leaves * (nears - 2) * LEAF * LEAF * columns,
            bytes_accessed=2 * leaves * nears * LEAF * LEAF + 6 * leaves * LEAF * columns,
            transcendentals=0,
        ),
        name="near_own",
    )(me, *in_hbm(near_list, far_zero, far_one, far_two, vectors, near_blocks))

    def has_second(i):
        return 0 <= turns[1](i) < size

    split = leaves * rank
    from_pair, near = lax.optimization_barrier((from_pair, near))
    low = lax.optimization_barrier(from_pair[:split])
    got_first = send(low, turns[0])
    first, second, low = lax.optimization_barrier((first, second, low))
    upper = jnp.where((me[0] // 2 + me[0]) % 2 == 1, second[split:], first[split:])
    at_end = (me[0] < 2) | (me[0] >= size - 2)
    got_second = send(
        jnp.where(at_end, upper, low), lambda i: turns[1](i) if has_second(i) else partner(i)
    )
    got_third = send(upper, lambda i: partner(i) if has_second(i) else -1)

    sums, *rest, part = pl.pallas_call(
        prep_kernel,
        in_specs=[smem] * 3 + [vmem] * 6 + [hbm] * 3,
        out_specs=[vmem] * 8,
        out_shape=[
            pltpu.VMEM(vectors.shape, f32),
            *[pltpu.VMEM((SPAN * n * rank, columns), bf16) for n in counts],
            *[pltpu.VMEM((n, rank, fars * rank), bf16) for n in counts],
            pltpu.VMEM((nodes * rank, columns), f32),
        ],
        scratch_shapes=[
            *[pltpu.VMEM((n, fars, rank, rank), bf16) for n in counts],
            pltpu.SemaphoreType.DMA((sum(n // 4 for n in counts),)),
        ],
        compiler_params=pltpu.CompilerParams(vmem_limit_bytes=16 * MIB),
        cost_estimate=pl.CostEstimate(
            flops=4 * 10**9,
            bytes_accessed=4 * nodes * fars * rank * rank,
            transcendentals=0,
        ),
        name="prep",
    )(
        me, starts, turns_taken, plain, from_pair, first, second, near, edge,
        *in_hbm(couple_zero, couple_one, couple_two),
    )
    windows, wides = rest[:3], rest[3:]

    out, *_ = pl.pallas_call(
        functools.partial(far_kernel, size=size),
        in_specs=[smem] * 2 + [vmem] * 16,
        out_specs=[hbm] + [vmem] * 4,
        out_shape=[
            jax.ShapeDtypeStruct(vectors.shape, bf16),
            pltpu.VMEM(vectors.shape, f32),
            *[pltpu.VMEM((SPAN * n * rank, columns), bf16) for n in counts],
        ],
        input_output_aliases={6: 1, 15: 2, 16: 3, 17: 4},
        scratch_shapes=[
            pltpu.VMEM(vectors.shape, bf16),
            pltpu.VMEM((LEAF, columns), bf16),
            pltpu.VMEM((nodes * rank, columns), f32),
            pltpu.VMEM((nodes * rank, columns), bf16),
            pltpu.SemaphoreType.DMA((leaves // 2,)),
        ],
        compiler_params=pltpu.CompilerParams(vmem_limit_bytes=16 * MIB),
        name="far_down",
    )(
        me, starts, points, got_first, got_second, got_third, sums, edge,
        basis_t, up_one, up_two, *wides, part, *windows,
    )
    return out


def solution(mesh):
    placed = (
        P(("groups", "space"), "rhs"),
        P("space", None, None, None),
        P("space", None),
        P("space", None, None),
        P("space", None, None),
        P("space", None, None),
        P("space", None, None, None),
        P("space", None, None, None),
        P("space", None, None, None),
        P("space", None),
        P("space", None),
        P("space", None),
    )
    return jax.shard_map(
        body, mesh=mesh, in_specs=placed, out_specs=P(("groups", "space"), "rhs"), check_vma=False
    )
```

```python
import functools

import jax
import jax.numpy as jnp
from jax import lax
from jax.experimental import pallas as pl
from jax.experimental.pallas import tpu as pltpu
from jax.sharding import PartitionSpec as P

LEAF = 256
REACH = 2
SPAN = 2 * REACH + 1
DEPTH = 3
MIB = 1024 * 1024


def dot(a, b):
    return jnp.dot(a, b, preferred_element_type=jnp.float32)


def dot_t(a, b):
    return lax.dot_general(a, b, (((0,), (0,)), ((), ())), preferred_element_type=jnp.float32)


def up_kernel(
    me_ref, x_hbm, basis_hbm, up_one_hbm, up_two_hbm, plain_ref, pair_ref,
    x_ref, basis_ref, up_one_ref, up_two_ref, sems,
):
    leaves, rank = basis_ref.shape[:2]
    steps = leaves // 4
    copies = []
    for q in range(steps):
        rows = pl.ds(q * 4 * LEAF, 4 * LEAF)
        some = pl.ds(q * 4, 4)
        copies.append(
            (
                pltpu.make_async_copy(x_hbm.at[rows, :], x_ref.at[rows, :], sems.at[2 * q]),
                pltpu.make_async_copy(basis_hbm.at[some], basis_ref.at[some], sems.at[2 * q + 1]),
            )
        )
    ups = (
        pltpu.make_async_copy(up_one_hbm, up_one_ref, sems.at[2 * steps]),
        pltpu.make_async_copy(up_two_hbm, up_two_ref, sems.at[2 * steps + 1]),
    )
    for pair in (*copies, ups):
        for copy in pair:
            copy.start()

    def put(node, value):
        value = value.astype(jnp.bfloat16)
        plain_ref[pl.ds(node * rank, rank), :] = value
        pair_ref[pl.ds(node * rank, rank), :] = value
        return value

    def join(ups, pair):
        return dot_t(ups.reshape(2 * rank, rank), jnp.concatenate(pair, axis=0))

    zeros = []
    for q in range(steps):
        for copy in copies[q]:
            copy.wait()
        for leaf in range(4 * q, 4 * q + 4):
            coef = dot(basis_ref[leaf], x_ref[pl.ds(leaf * LEAF, LEAF), :])
            zeros.append(put(leaf, coef))
    for copy in ups:
        copy.wait()
    ones = []
    for p in range(leaves // 2):
        pair = slice(2 * p, 2 * p + 2)
        ones.append(put(leaves + p, join(up_one_ref[pair], zeros[pair])))
    for q in range(leaves // 4):
        pair = slice(2 * q, 2 * q + 2)
        put(leaves + leaves // 2 + q, join(up_two_ref[pair], ones[pair]))
    odd = lax.rem(me_ref[0], 2)
    last = (leaves - 1) * LEAF
    end = pl.ds(plain_ref.shape[0] - LEAF, LEAF)
    pair_ref[end, :] = x_ref[pl.ds(pl.multiple_of((1 - odd) * last, LEAF), LEAF), :]
    plain_ref[end, :] = x_ref[pl.ds(pl.multiple_of(odd * last, LEAF), LEAF), :]


def last_place(me):
    return REACH - 1 + 2 * lax.rem(me, 2)


def near_kernel(
    me_ref, near_hbm, zero_hbm, one_hbm, two_hbm, x_hbm, blocks_hbm,
    out_ref, edge_ref, x_ref, starts_ref, turns_ref,
    list_ref, zero_list, one_list, two_list, block_buf, sems, x_sems, list_sems,
):
    leaves, nears = list_ref.shape
    ones, twos = one_list.shape[0], two_list.shape[0]
    me = me_ref[0]
    first = me * leaves
    depth = block_buf.shape[0]

    def copies(pair, slot):
        both = pl.ds(2 * pair, 2)
        pairs = (
            (blocks_hbm.at[both, pl.ds(0, 1)], block_buf.at[slot, :, pl.ds(0, 1)]),
            (blocks_hbm.at[both, pl.ds(3, nears - 3)], block_buf.at[slot, :, pl.ds(1, nears - 3)]),
            (blocks_hbm.at[both, pl.ds(1, 2)], edge_ref.at[both]),
        )
        return [
            pltpu.make_async_copy(src, dst, sems.at[slot, i]) for i, (src, dst) in enumerate(pairs)
        ]

    hbms = (near_hbm, zero_hbm, one_hbm, two_hbm)
    lists = (list_ref, zero_list, one_list, two_list)
    list_copies = [
        pltpu.make_async_copy(src, dst, list_sems.at[i])
        for i, (src, dst) in enumerate(zip(hbms, lists))
    ]
    for copy in list_copies:
        copy.start()
    x_copies = []
    for q in range(leaves // 4):
        rows = pl.ds(q * 4 * LEAF, 4 * LEAF)
        x_copies.append(
            pltpu.make_async_copy(x_hbm.at[rows, :], x_ref.at[rows, :], x_sems.at[q])
        )
    for copy in x_copies:
        copy.start()
    for pair in range(depth - 1):
        for copy in copies(pair, pair):
            copy.start()
    for copy in list_copies:
        copy.wait()

    def order(where, node, row):
        per, fars = where.shape
        base = (me - REACH) * per
        low = last_place(me) * per
        count = jnp.int32(0)
        for k in range(fars):
            index = where[node, k] - base
            late = (index >= low) & (index < low + per)
            at = jnp.where(late, count, fars - 1 - k + count)
            starts_ref[row, at] = index
            turns_ref[row, at] = k
            count = count + late.astype(jnp.int32)
        return count

    most = jnp.int32(0)
    for p in range(ones):
        most = jnp.maximum(most, order(one_list, p, leaves + p))
    for q in range(twos):
        most = jnp.maximum(most, order(two_list, q, leaves + ones + q))
    for copy in x_copies:
        copy.wait()

    def step(pair, most):
        slot = lax.rem(pair, depth)

        @pl.when(pair + depth - 1 < leaves // 2)
        def _():
            for copy in copies(pair + depth - 1, lax.rem(pair + depth - 1, depth)):
                copy.start()

        for copy in copies(pair, slot):
            copy.wait()
        totals = []
        for side in range(2):
            rows = []
            for k in (0, *range(3, nears)):
                start = (list_ref[2 * pair + side, k] - first) * LEAF
                rows.append(x_ref[pl.ds(pl.multiple_of(start, LEAF), LEAF), :])
            blocks = [block_buf[slot, side, k] for k in range(nears - 2)]
            totals.append(dot(jnp.concatenate(blocks, axis=1), jnp.concatenate(rows, axis=0)))
        here = pl.ds(pl.multiple_of(pair * 2 * LEAF, 2 * LEAF), 2 * LEAF)
        out_ref[here, :] = jnp.concatenate(totals, axis=0)
        for side in range(2):
            leaf = 2 * pair + side
            most = jnp.maximum(most, order(zero_list, leaf, leaf))
        return most

    starts_ref[leaves + ones + twos, 0] = lax.fori_loop(0, leaves // 2, step, most)


def add_edge(sum_ref, near_ref, edge_ref, side, rows, leaves):
    for leaf in leaves:
        here = pl.ds(leaf * LEAF, LEAF)
        sum_ref[here, :] = near_ref[here, :] + dot(edge_ref[leaf, side], rows)


def place_piece(ref, start, win, at, size):
    win[pl.ds(at, size), :] = ref[pl.ds(start, size), :]


def field(wide, starts_ref, row, win, slots):
    rank = wide.shape[0]
    rows = []
    for k in slots:
        rows.append(win[pl.ds(pl.multiple_of(starts_ref[row, k] * rank, rank), rank), :])
    some = wide[:, slots[0] * rank : (slots[-1] + 1) * rank]
    return dot(some, jnp.concatenate(rows, axis=0))


def prep_kernel(
    me_ref, starts_ref, turns_ref, own_ref, pair_ref, first_ref, second_ref, near_ref, edge_ref,
    zero_hbm, one_hbm, two_hbm,
    sum_ref, zero_win, one_win, two_win, zero_wide, one_wide, two_wide, part_ref,
    zero_buf, one_buf, two_buf, sems,
):
    leaves, fars, rank = zero_buf.shape[:3]
    base = leaves + one_buf.shape[0]
    levels = (
        (two_hbm, two_buf, two_wide, two_win, base),
        (one_hbm, one_buf, one_wide, one_win, leaves),
        (zero_hbm, zero_buf, zero_wide, zero_win, 0),
    )
    chunks = []
    for hbm, buf, wide, _, row in levels:
        for first in range(0, buf.shape[0], 4):
            some = pl.ds(first, 4)
            copy = pltpu.make_async_copy(hbm.at[some], buf.at[some], sems.at[len(chunks)])
            copy.start()
            chunks.append((copy, buf, wide, first, row))
    me = me_ref[0]
    odd = lax.rem(me, 2)
    block = lax.rem(me // 2, 2)
    pieces = (
        (own_ref, 0, REACH),
        (first_ref, 0, (1 - block) * (SPAN - 1)),
        (second_ref, 0, block * (SPAN - 1)),
        (pair_ref, 0, REACH + 1 - 2 * odd),
    )
    for ref, start, place in pieces:
        for win in (zero_win, one_win, two_win):
            size = win.shape[0] // SPAN
            place_piece(ref, start, win, pl.multiple_of(place * size, size), size)
            start += size
    rows = pair_ref[pl.ds(pair_ref.shape[0] - LEAF, LEAF), :]
    add_edge(sum_ref, near_ref, edge_ref, odd, rows, range(leaves))
    for copy, buf, wide, first, row in chunks:
        copy.wait()
        for node in range(first, first + 4):
            picked = [buf[node, turns_ref[row + node, k]] for k in range(fars)]
            wide[node] = jnp.concatenate(picked, axis=1)
    for _, _, wide, win, row in levels:
        for node in range(wide.shape[0]):
            part = field(wide.at[node], starts_ref, row + node, win, range(fars // 2, fars))
            part_ref[pl.ds((row + node) * rank, rank), :] = part


def far_kernel(
    me_ref, starts_ref, x_ref, got_first, got_second, got_third, sum_in,
    edge_ref, basis_ref, up_one_ref, up_two_ref, zero_wide, one_wide, two_wide, part_ref,
    zero_in, one_in, two_in, out_hbm, sum_ref, zero_win, one_win, two_win,
    out_buf, rows_buf, field_buf, down_buf, out_sems, *, size,
):
    del sum_in, zero_in, one_in, two_in
    leaves, rank, deep = zero_wide.shape
    ones, twos = leaves // 2, leaves // 4
    fars = deep // rank
    me = me_ref[0]
    odd = lax.rem(me, 2)
    place = last_place(me)
    sizes = [n * rank for n in (leaves, ones, twos)]
    at = [pl.multiple_of(place * n, n) for n in sizes]

    end = pl.ds(got_first.shape[0] - LEAF, LEAF)
    low_first = lax.rem(me + me // 2, 2) == 1
    at_end = (me < 2) | (me >= size - 2)

    def take(low_ref, high_ref):
        def _():
            place_piece(low_ref, 0, zero_win, at[0], sizes[0])
            place_piece(high_ref, 0, one_win, at[1], sizes[1])
            place_piece(high_ref, sizes[1], two_win, at[2], sizes[2])
            rows_buf[...] = high_ref[end, :]

        return _

    pl.when(low_first & at_end)(take(got_first, got_second))
    pl.when(low_first & jnp.logical_not(at_end))(take(got_first, got_third))
    pl.when(jnp.logical_not(low_first))(take(got_second, got_third))

    alone = (me == 0) | (me == size - 1)

    def add_last(some):
        for leaf in some:
            here = pl.ds(leaf * LEAF, LEAF)
            rows = jnp.where(alone, x_ref[here, :], rows_buf[...])
            sum_ref[here, :] += dot(edge_ref[leaf, 1 - odd], rows)

    def node_rows(row):
        return pl.ds(row * rank, rank)

    base = leaves + ones
    half = fars // 2
    levels = ((two_wide, two_win, base), (one_wide, one_win, leaves), (zero_wide, zero_win, 0))
    for wide, win, row in levels:
        for node in range(wide.shape[0]):
            part = field(wide.at[node], starts_ref, row + node, win, range(half))
            rows = node_rows(row + node)
            field_buf[rows, :] = part_ref[rows, :] + part

    @pl.when(starts_ref[base + twos, 0] > half)
    def _():
        for wide, win, row in levels:

            def again(node, carry):
                part = field(wide.at[node], starts_ref, row + node, win, range(fars))
                field_buf[pl.ds(pl.multiple_of((row + node) * rank, rank), rank), :] = part
                return carry

            lax.fori_loop(0, wide.shape[0], again, 0)

    add_last(range(leaves // 2))
    for q in range(twos):
        down_buf[node_rows(base + q), :] = field_buf[node_rows(base + q), :].astype(jnp.bfloat16)
    for p in range(ones):
        total = dot(up_two_ref[p], down_buf[node_rows(base + p // 2), :])
        total = total + field_buf[node_rows(leaves + p), :]
        down_buf[node_rows(leaves + p), :] = total.astype(jnp.bfloat16)
    add_last(range(leaves // 2, leaves))
    for leaf in range(leaves):
        total = dot(up_one_ref[leaf], down_buf[node_rows(leaves + leaf // 2), :])
        total = total + field_buf[node_rows(leaf), :]
        down_buf[node_rows(leaf), :] = total.astype(jnp.bfloat16)
    outs = []
    for leaf in range(leaves):
        here = pl.ds(leaf * LEAF, LEAF)
        total = sum_ref[here, :] + dot_t(basis_ref[leaf], down_buf[node_rows(leaf), :])
        out_buf[here, :] = total.astype(jnp.bfloat16)
        if leaf % 2 == 1:
            some = pl.ds((leaf - 1) * LEAF, 2 * LEAF)
            outs.append(
                pltpu.make_async_copy(
                    out_buf.at[some, :], out_hbm.at[some, :], out_sems.at[leaf // 2]
                )
            )
            outs[-1].start()
    for copy in outs:
        copy.wait()


def body(
    vectors,
    near_blocks,
    near_list,
    basis,
    up_one,
    up_two,
    couple_zero,
    couple_one,
    couple_two,
    far_zero,
    far_one,
    far_two,
):
    leaves, nears = near_list.shape
    columns = vectors.shape[1]
    rank = basis.shape[2]
    fars = far_zero.shape[1]
    size = lax.axis_size("space")
    cores = lax.axis_size("rhs")
    me = lax.axis_index("space").astype(jnp.int32).reshape(1)
    counts = (leaves, leaves // 2, leaves // 4)
    nodes = sum(counts)
    basis_t = jnp.swapaxes(basis, 1, 2)
    bf16, f32 = jnp.bfloat16, jnp.float32

    hbm = pl.BlockSpec(memory_space=pltpu.HBM)
    vmem = pl.BlockSpec(memory_space=pltpu.VMEM)
    smem = pl.BlockSpec(memory_space=pltpu.SMEM)

    def in_hbm(*arrays):
        return [pltpu.with_memory_space_constraint(a, pltpu.HBM) for a in arrays]

    plain, pair = pl.pallas_call(
        up_kernel,
        in_specs=[smem] + [hbm] * 4,
        out_specs=[vmem] * 2,
        out_shape=[
            pltpu.VMEM((nodes * rank + LEAF, columns), bf16),
            pltpu.VMEM((nodes * rank + LEAF, columns), bf16),
        ],
        scratch_shapes=[
            pltpu.VMEM(vectors.shape, bf16),
            pltpu.VMEM(basis_t.shape, bf16),
            pltpu.VMEM(up_one.shape, bf16),
            pltpu.VMEM(up_two.shape, bf16),
            pltpu.SemaphoreType.DMA((leaves // 2 + 2,)),
        ],
        compiler_params=pltpu.CompilerParams(vmem_limit_bytes=8 * MIB),
        name="up_pass",
    )(me, *in_hbm(vectors, basis_t, up_one, up_two))

    def send(array, to):
        pairs = []
        for i in range(size):
            for c in range(cores):
                j, d = (to(i), c) if 0 <= to(i) < size else (i, cores - 1 - c)
                pairs.append((i * cores + c, j * cores + d))
        return lax.ppermute(array, ("space", "rhs"), pairs)

    def partner(i):
        return i + 1 - 2 * (i % 2)

    from_pair = send(pair, partner)
    turns = (lambda i: i + 2 - i // 2 % 2 * 4, lambda i: i - 2 + i // 2 % 2 * 4)
    first, second = [send(plain, turn) for turn in turns]

    near, edge, points, starts, turns_taken = pl.pallas_call(
        near_kernel,
        in_specs=[smem] + [hbm] * 6,
        out_specs=[vmem] * 3 + [smem] * 2,
        out_shape=[
            pltpu.VMEM(vectors.shape, f32),
            pltpu.VMEM((leaves, 2, LEAF, LEAF), bf16),
            pltpu.VMEM(vectors.shape, bf16),
            jax.ShapeDtypeStruct((nodes + 1, fars), jnp.int32),
            jax.ShapeDtypeStruct((nodes + 1, fars), jnp.int32),
        ],
        scratch_shapes=[
            *[pltpu.SMEM(a.shape, jnp.int32) for a in (near_list, far_zero, far_one, far_two)],
            pltpu.VMEM((DEPTH, 2, nears - 2, LEAF, LEAF), bf16),
            pltpu.SemaphoreType.DMA((DEPTH, 3)),
            pltpu.SemaphoreType.DMA((leaves // 4,)),
            pltpu.SemaphoreType.DMA((4,)),
        ],
        compiler_params=pltpu.CompilerParams(vmem_limit_bytes=16 * MIB),
        cost_estimate=pl.CostEstimate(
            flops=2 * leaves * (nears - 2) * LEAF * LEAF * columns,
            bytes_accessed=2 * leaves * nears * LEAF * LEAF + 6 * leaves * LEAF * columns,
            transcendentals=0,
        ),
        name="near_own",
    )(me, *in_hbm(near_list, far_zero, far_one, far_two, vectors, near_blocks))

    def has_second(i):
        return 0 <= turns[1](i) < size

    split = leaves * rank
    from_pair, near = lax.optimization_barrier((from_pair, near))
    low = lax.optimization_barrier(from_pair[:split])
    got_first = send(low, turns[0])
    first, second, low = lax.optimization_barrier((first, second, low))
    upper = jnp.where((me[0] // 2 + me[0]) % 2 == 1, second[split:], first[split:])
    at_end = (me[0] < 2) | (me[0] >= size - 2)
    got_second = send(
        jnp.where(at_end, upper, low), lambda i: turns[1](i) if has_second(i) else partner(i)
    )
    got_third = send(upper, lambda i: partner(i) if has_second(i) else -1)

    sums, *rest, part = pl.pallas_call(
        prep_kernel,
        in_specs=[smem] * 3 + [vmem] * 6 + [hbm] * 3,
        out_specs=[vmem] * 8,
        out_shape=[
            pltpu.VMEM(vectors.shape, f32),
            *[pltpu.VMEM((SPAN * n * rank, columns), bf16) for n in counts],
            *[pltpu.VMEM((n, rank, fars * rank), bf16) for n in counts],
            pltpu.VMEM((nodes * rank, columns), f32),
        ],
        scratch_shapes=[
            *[pltpu.VMEM((n, fars, rank, rank), bf16) for n in counts],
            pltpu.SemaphoreType.DMA((sum(n // 4 for n in counts),)),
        ],
        compiler_params=pltpu.CompilerParams(vmem_limit_bytes=16 * MIB),
        cost_estimate=pl.CostEstimate(
            flops=4 * 10**9,
            bytes_accessed=4 * nodes * fars * rank * rank,
            transcendentals=0,
        ),
        name="prep",
    )(
        me, starts, turns_taken, plain, from_pair, first, second, near, edge,
        *in_hbm(couple_zero, couple_one, couple_two),
    )
    windows, wides = rest[:3], rest[3:]

    out, *_ = pl.pallas_call(
        functools.partial(far_kernel, size=size),
        in_specs=[smem] * 2 + [vmem] * 16,
        out_specs=[hbm] + [vmem] * 4,
        out_shape=[
            jax.ShapeDtypeStruct(vectors.shape, bf16),
            pltpu.VMEM(vectors.shape, f32),
            *[pltpu.VMEM((SPAN * n * rank, columns), bf16) for n in counts],
        ],
        input_output_aliases={6: 1, 15: 2, 16: 3, 17: 4},
        scratch_shapes=[
            pltpu.VMEM(vectors.shape, bf16),
            pltpu.VMEM((LEAF, columns), bf16),
            pltpu.VMEM((nodes * rank, columns), f32),
            pltpu.VMEM((nodes * rank, columns), bf16),
            pltpu.SemaphoreType.DMA((leaves // 2,)),
        ],
        compiler_params=pltpu.CompilerParams(vmem_limit_bytes=16 * MIB),
        name="far_down",
    )(
        me, starts, points, got_first, got_second, got_third, sums, edge,
        basis_t, up_one, up_two, *wides, part, *windows,
    )
    return out


def solution(mesh):
    placed = (
        P(("groups", "space"), "rhs"),
        P("space", None, None, None),
        P("space", None),
        P("space", None, None),
        P("space", None, None),
        P("space", None, None),
        P("space", None, None, None),
        P("space", None, None, None),
        P("space", None, None, None),
        P("space", None),
        P("space", None),
        P("space", None),
    )
    return jax.shard_map(
        body, mesh=mesh, in_specs=placed, out_specs=P(("groups", "space"), "rhs"), check_vma=False
    )
```
